32 devices in a mesh: gx: 8 (over y, x, core), gy: 4 (over z).
Axes of the slice: x: 2, y: 2, z: 4, core: 2. Of those that a mesh axis runs over, the one named last changes fastest.
Arguments:
- source: float32 [64, 64, 512], P('gx', 'gy'), may hold values from -6 to 6
- face_coef: bfloat16 [3, 64, 64, 512], P(None, 'gx', 'gy'), may hold values from 0.25 to 4
Outputs:
- potential: float32 [64, 64, 512], P('gx', 'gy')
The draws below stay inside these ranges and needn't reach their ends.
All inputs are finite; a program needn't handle non-finite values.
Results may differ from the reference program's by a relative error of at most 0.0003.
Values sent between devices are 32-bit elements; how exact they have to be, the bound alone decides.
No kernel may reach another device: no remote copies, remote signals or barrier semaphores. Data moves between devices by JAX's collectives and lax.ppermute only.
A program may use at most 64 MiB of HBM per device.

```python
import math
import jax
import jax.numpy as jnp

NZ = 512
LEVELS = 3
SWEEPS = 2
NX = 64
NY = 64


def draw_source(key, part):
    return jax.random.truncated_normal(key, -6.0, 6.0, (NX, NY, NZ), jnp.float32)


def shard_levels(key, shape, pieces, smallest, largest):
    loudness = 1.0
    for dim, blocks in pieces:
        heights = jax.random.uniform(jax.random.fold_in(jax.random.fold_in(key, 6), dim), (blocks,), jnp.float32, smallest / len(pieces), largest / len(pieces))
        loudness = loudness * jnp.repeat(jnp.exp(heights), shape[dim] // blocks).reshape((-1,) + (1,) * (len(shape) - 1 - dim))
    return loudness


def setup_inputs(seed: int = 0) -> dict:
    key_list = jax.random.split(jax.random.key(seed), 3)
    source = draw_source(jax.random.fold_in(key_list[2], 71), 0)
    face_coef = jnp.clip(jnp.exp(math.log(4.0) - 2.7725887 * jax.random.uniform(key_list[1], (3, NX, NY, NZ), jnp.float32) ** shard_levels(key_list[1], (3, NX, NY, NZ), ((1, 8), (2, 4)), -0.2, 0.2)), 0.25, 4.0).astype(jnp.bfloat16)
    return {"source": source, "face_coef": face_coef}


MASS = 0.002


def coarsen(couplings):
    east_face = couplings[0][1::2]
    east_face = east_face[:, 0::2, 0::2] + east_face[:, 1::2, 0::2] + east_face[:, 0::2, 1::2] + east_face[:, 1::2, 1::2]
    north_face = couplings[1][:, 1::2]
    north_face = north_face[0::2, :, 0::2] + north_face[1::2, :, 0::2] + north_face[0::2, :, 1::2] + north_face[1::2, :, 1::2]
    upper_face = couplings[2][:, :, 1::2]
    upper_face = upper_face[0::2, 0::2] + upper_face[1::2, 0::2] + upper_face[0::2, 1::2] + upper_face[1::2, 1::2]
    return jnp.stack((east_face, north_face, upper_face)) * 0.0625


def restrict(residual):
    dims = residual.shape
    return residual.reshape(dims[0] // 2, 2, dims[1] // 2, 2, dims[2] // 2, 2).mean(axis=(1, 3, 5))


def prolong(correction):
    return jnp.repeat(jnp.repeat(jnp.repeat(correction, 2, 0), 2, 1), 2, 2)


def neighbour_sum(potential, couplings, lagged):
    summed = couplings[0] * jnp.roll(potential, -1, 0) + lagged[0] * jnp.roll(potential, 1, 0)
    summed = summed + couplings[1] * jnp.roll(potential, -1, 1) + lagged[1] * jnp.roll(potential, 1, 1)
    summed = summed + couplings[2] * jnp.roll(potential, -1, 2) + lagged[2] * jnp.roll(potential, 1, 2)
    return summed


def parity_of(dims):
    row_ids = jnp.arange(dims[0], dtype=jnp.int32)
    col_ids = jnp.arange(dims[1], dtype=jnp.int32)
    depth_ids = jnp.arange(dims[2], dtype=jnp.int32)
    return (row_ids[:, None, None] + col_ids[None, :, None] + depth_ids[None, None, :]) % 2


def smoothing(potential, right_side, couplings, lagged, diagonal, parity):
    for sweep_index in range(SWEEPS):
        for colour in (0, 1):
            updated = (right_side + neighbour_sum(potential, couplings, lagged)) / diagonal
            potential = jnp.where(parity == colour, updated, potential)
    return potential


def coarse_solve(right_side, couplings):
    averages = jnp.mean(couplings, axis=(1, 2, 3))
    dims = right_side.shape
    eigen_parts = []
    for axis_index in range(3):
        wave = jnp.arange(dims[axis_index], dtype=jnp.int32).astype(jnp.float32) * (2.0 * math.pi / dims[axis_index])
        eigen_parts.append(2.0 * averages[axis_index] * (1.0 - jnp.cos(wave)))
    eigenvalue = MASS + eigen_parts[0][:, None, None] + eigen_parts[1][None, :, None] + eigen_parts[2][None, None, :]
    spectrum = jnp.fft.fftn(right_side) / eigenvalue
    return jnp.real(jnp.fft.ifftn(spectrum)).astype(right_side.dtype)


def multigrid_cycle(right_side, couplings, level_index):
    if level_index == LEVELS - 1:
        return coarse_solve(right_side, couplings)
    lagged = [jnp.roll(couplings[axis_index], 1, axis_index) for axis_index in range(3)]
    diagonal = MASS + couplings[0] + lagged[0] + couplings[1] + lagged[1] + couplings[2] + lagged[2]
    parity = parity_of(right_side.shape)
    potential = smoothing(jnp.zeros_like(right_side), right_side, couplings, lagged, diagonal, parity)
    residual = right_side - (diagonal * potential - neighbour_sum(potential, couplings, lagged))
    correction = multigrid_cycle(restrict(residual), coarsen(couplings), level_index + 1)
    potential = potential + prolong(correction)
    return smoothing(potential, right_side, couplings, lagged, diagonal, parity)


def reference(source, face_coef):
    return multigrid_cycle(source, face_coef.astype(jnp.float32), 0)
```

```python
import functools
import math

import jax
import jax.numpy as jnp
import ml_dtypes
import numpy as np
from jax import lax
from jax.experimental import pallas as pl
from jax.experimental.pallas import tpu as pltpu
from jax.sharding import PartitionSpec as P

LEVELS = 3
SWEEPS = 2
MASS = 0.002
BOTH = ("gx", "gy")
H = 2 * SWEEPS
F32 = jnp.float32
BF16 = jnp.bfloat16
VMEM = pl.BlockSpec(memory_space=pltpu.VMEM)

CORNER0 = (
    (0, 1, 1), (0, 1, 2), (0, 1, 3), (1, 2, 3), (3, 1, 1), (3, 1, 2), (3, 1, 3), (2, 2, 3),
    (1, 1, 1), (1, 1, 2), (1, 1, 3), (1, 1, 4), (2, 1, 1), (2, 1, 2), (2, 1, 3), (2, 1, 4),
    (0, 2, 1), (0, 2, 2), (0, 3, 1), (1, 4, 1), (3, 2, 1), (3, 2, 2), (3, 3, 1), (2, 4, 1),
    (1, 2, 1), (1, 2, 2), (1, 3, 1), (1, 3, 2), (2, 2, 1), (2, 2, 2), (2, 3, 1), (2, 3, 2),
)
CORNER1 = (
    (0, 1, 1), (0, 1, 2), (0, 1, 3), (0, 2, 1), (0, 2, 2), (0, 3, 1), (2, 1, 1), (2, 1, 2),
    (1, 1, 1), (1, 1, 2), (1, 1, 3), (1, 2, 1), (1, 2, 2), (1, 3, 1), (2, 2, 1), None,
)


def call(kernel, out, *args, scratch=()):
    return pl.pallas_call(
        kernel,
        out_shape=[jax.ShapeDtypeStruct(s, F32) for s in out],
        in_specs=[VMEM] * len(args),
        out_specs=[VMEM] * len(out),
        scratch_shapes=[pltpu.VMEM(s, F32) for s in scratch],
        compiler_params=pltpu.CompilerParams(vmem_limit_bytes=48 * 1024 * 1024),
    )(*args)


def moved(block, dx, dy):
    nx, ny = lax.axis_size("gx"), lax.axis_size("gy")
    if dy == 0:
        return lax.ppermute(block, "gx", [(i, (i + dx) % nx) for i in range(nx)])
    if dx == 0:
        return lax.ppermute(block, "gy", [(j, (j + dy) % ny) for j in range(ny)])
    route = []
    for i in range(nx):
        for j in range(ny):
            route.append((i * ny + j, ((i + dx) % nx) * ny + (j + dy) % ny))
    return lax.ppermute(block, BOTH, route)


def split3(x):
    high = x.astype(BF16)
    rest = x - high.astype(F32)
    middle = rest.astype(BF16)
    return high, middle, (rest - middle.astype(F32)).astype(BF16)


def dot(a, b):
    return jnp.dot(a, b, preferred_element_type=F32)


def dot_exact(x, table):
    high, middle, low = split3(x)
    return dot(high, table) + (dot(middle, table) + dot(low, table))


def dot_pair(a, b):
    a_high = a.astype(BF16)
    a_low = (a - a_high.astype(F32)).astype(BF16)
    b_high = b.astype(BF16)
    b_low = (b - b_high.astype(F32)).astype(BF16)
    return dot(a_high, b_high) + (dot(a_high, b_low) + dot(a_low, b_high))


def pair_table(depth):
    table = np.zeros((depth, depth // 2), ml_dtypes.bfloat16)
    table[np.arange(depth), np.arange(depth) // 2] = 1
    return table


def odd_table(depth):
    table = np.zeros((depth, depth // 2), ml_dtypes.bfloat16)
    table[np.arange(1, depth, 2), np.arange(depth // 2)] = 1
    return table


def put_tiles(tiles, x):
    for k in range(tiles.shape[0]):
        tiles[k] = x[:, 128 * k : 128 * k + 128]


def every_other(tiles, start, size):
    return jnp.concatenate(
        [tiles[k, pl.ds(start, size, stride=2), :] for k in range(tiles.shape[0])], axis=1
    )


def back(x, axis):
    return pltpu.roll(x, 1, axis)


def ahead(x, axis):
    return pltpu.roll(x, x.shape[axis] - 1, axis)


def parity2(shape):
    return (lax.broadcasted_iota(jnp.int32, shape, 0) + lax.broadcasted_iota(jnp.int32, shape, 1)) & 1


def row_sum(r, v, wx, wy, wz):
    centre = v[r]
    y, z = wy[r], wz[r]
    total = wx[r] * v[r + 1] + wx[r - 1] * v[r - 1]
    total = total + y * ahead(centre, 0) + back(y * centre, 0)
    return centre, total + z * ahead(centre, 1) + back(z * centre, 1)


def half_sweep(first, last, colour, parity, v, b, wx, wy, wz, rdiag):
    def body(r, carry):
        centre, total = row_sum(r, v, wx, wy, wz)
        mine = parity == ((r + colour) & 1)
        v[r] = jnp.where(mine, (b[r] + total) * rdiag[r], centre)
        return carry

    lax.fori_loop(first, last, body, 0)


def pack_kernel(src, face, pairs, odds, to_up, to_down, to_right, to_left, *rest):
    corners, w1 = rest[:4], rest[4]
    (tx,) = rest[5:]
    rows, cols, depth = src.shape
    half = depth // 2

    for i in range(rows // 2):
        put_tiles(tx, dot(face[0, 2 * i + 1], pairs[...]))
        w1[0, i] = 0.0625 * (every_other(tx, 0, cols // 2) + every_other(tx, 1, cols // 2))
        put_tiles(tx, dot(face[1, 2 * i], pairs[...]) + dot(face[1, 2 * i + 1], pairs[...]))
        w1[1, i] = 0.0625 * every_other(tx, 1, cols // 2)
        put_tiles(tx, dot(face[2, 2 * i], odds[...]) + dot(face[2, 2 * i + 1], odds[...]))
        w1[2, i] = 0.0625 * (every_other(tx, 0, cols // 2) + every_other(tx, 1, cols // 2))

    def plane(a, r):
        return src[r] if a == 0 else face[a - 1, r].astype(F32)

    for out, base in ((to_up, rows - H), (to_down, 0)):
        for a in range(4):
            for k in range(H):
                value = plane(a, base + k)
                if out is to_up and a == 3 and k == 0:
                    value = value + back(value, 1) + plane(1, base - 1)
                for t in range(cols // 8):
                    out[(a * H + k) * (cols // 8) + t] = value[8 * t : 8 * t + 8]
        base1 = 4 * H * (cols // 8)
        for d in range(3):
            for i in range(H // 2):
                out[base1 + d * (H // 2) + i] = jnp.concatenate((w1[d, 2 * i], w1[d, 2 * i + 1]), axis=1)

    for out, base, base1 in ((to_right, cols - H, cols // 2 - H), (to_left, 0, 0)):
        for r in range(rows):
            for t, pair in enumerate(((0, 3), (1, 2))):
                for s, a in enumerate(pair):
                    value = plane(a, r)
                    if out is to_right and a == 3:
                        value_all = value + back(value, 1) + back(plane(2, r), 0)
                        first = lax.broadcasted_iota(jnp.int32, value.shape, 0) == base
                        value = jnp.where(first, value_all, value)
                    out[2 * r + t, H * s : H * s + H] = value[base : base + H]
        for i in range(rows // 2):
            k, lane = 2 * rows + i // 2, half * (i % 2)
            out[k, 0:H, lane : lane + half] = w1[0, i, base1 : base1 + H]
            out[k, H : 2 * H, lane : lane + half] = w1[1, i, base1 : base1 + H]
            k = 2 * rows + rows // 4 + i // 4
            s = H * (i % 2)
            lane = half * ((i // 2) % 2)
            out[k, s : s + H, lane : lane + half] = w1[2, i, base1 : base1 + H]

    for out, (sx, sy) in zip(corners, ((1, 1), (1, -1), (-1, 1), (-1, -1))):
        def at(distance, size, sign):
            return size - distance if sign > 0 else distance - 1

        for n, (a, dx, dy) in enumerate(CORNER0):
            r, c = at(dx, rows, sx), at(dy, cols, sy)
            line = src[r, c : c + 1] if a == 0 else plane(a, r)[c : c + 1]
            out[n // 8, n % 8 : n % 8 + 1] = line
        for n, entry in enumerate(CORNER1):
            if entry is None:
                continue
            d, dx, dy = entry
            r, c = at(dx, rows // 2, sx), at(dy, cols // 2, sy)
            lane = half * (n // 8)
            out[len(CORNER0) // 8, n % 8 : n % 8 + 1, lane : lane + half] = w1[d, r, c : c + 1]


def pre_kernel(src, face, w1, up, down, right, left, c0, c1, c2, c3, pairs, *rest):
    (b, wx, wy, wz, rdiag, v_own, right1, to_up, to_down, w1e, rdiag1, diag1, merged_up, merged_down) = rest[:14]
    v, diag, t512, t256 = rest[14:]
    rows, cols, depth = src.shape
    half = depth // 2
    ext = (b, wx, wy, wz)
    er, ec = rows + 2 * H, cols + 2 * H
    rows1, cols1 = rows // 2, cols // 2

    for r in range(rows):
        b[H + r, H : H + cols] = src[r]
        for d in range(3):
            ext[1 + d][H + r, H : H + cols] = face[d, r].astype(F32)
    for d in range(3):
        for i in range(rows1):
            w1e[d, H + i, H : H + cols1] = w1[d, i]
    tiles = cols // 8
    for msg, base, base1 in ((up, 0, 0), (down, H + rows, H + rows1)):
        for a in range(4):
            for k in range(H):
                for t in range(tiles):
                    ext[a][base + k, H + 8 * t : H + 8 * t + 8] = msg[(a * H + k) * tiles + t]
        n = 4 * H * tiles
        for d in range(3):
            for i in range(H):
                lane = half * (i % 2)
                w1e[d, base1 + i, H : H + cols1] = msg[n + d * (H // 2) + i // 2, :, lane : lane + half]
    for msg, base, base1 in ((right, 0, 0), (left, H + cols, H + cols1)):
        for r in range(rows):
            for t, pair in enumerate(((0, 3), (1, 2))):
                for s, a in enumerate(pair):
                    ext[a][H + r, base : base + H] = msg[2 * r + t, H * s : H * s + H]
        for i in range(rows1):
            k, lane = 2 * rows + i // 2, half * (i % 2)
            w1e[0, H + i, base1 : base1 + H] = msg[k, 0:H, lane : lane + half]
            w1e[1, H + i, base1 : base1 + H] = msg[k, H : 2 * H, lane : lane + half]
            k = 2 * rows + rows // 4 + i // 4
            s = H * (i % 2)
            lane = half * ((i // 2) % 2)
            w1e[2, H + i, base1 : base1 + H] = msg[k, s : s + H, lane : lane + half]
    for msg, (sx, sy) in zip((c0, c1, c2, c3), ((1, 1), (1, -1), (-1, 1), (-1, -1))):
        def at(distance, size, sign):
            return H - distance if sign > 0 else H + size + distance - 1

        for n, (a, dx, dy) in enumerate(CORNER0):
            r, c = at(dx, rows, sx), at(dy, cols, sy)
            ext[a][r, c : c + 1] = msg[n // 8, n % 8 : n % 8 + 1]
        for n, entry in enumerate(CORNER1):
            if entry is None:
                continue
            d, dx, dy = entry
            r, c = at(dx, rows1, sx), at(dy, cols1, sy)
            lane = half * (n // 8)
            w1e[d, r, c : c + 1] = msg[len(CORNER0) // 8, n % 8 : n % 8 + 1, lane : lane + half]

    parity = parity2((ec, depth))
    low_col = lax.broadcasted_iota(jnp.int32, (ec, depth), 0) == 0

    def finish(r, total):
        diag[r] = total
        inverse = 1.0 / total
        rdiag[r] = inverse
        v[r] = jnp.where(parity == (r & 1), b[r] * inverse, 0.0)

    y = wy[0]
    finish(0, MASS + wx[0] + wz[0] + y + back(y, 0))

    def diag_body(r, carry):
        y, z = wy[r], wz[r]
        total = MASS + wx[r] + wx[r - 1] + y
        finish(r, total + jnp.where(low_col, z, z + back(z, 1) + back(y, 0)))
        return carry

    lax.fori_loop(1, er, diag_body, 0)
    half_sweep(1, er - 1, 1, parity, v, b, wx, wy, wz, rdiag)
    half_sweep(2, er - 2, 0, parity, v, b, wx, wy, wz, rdiag)
    half_sweep(3, er - 3, 1, parity, v, b, wx, wy, wz, rdiag)

    def residual_body(i, carry):
        total = 0.0
        for k in range(2):
            r = H + 2 * i + k
            centre, around = row_sum(r, v, wx, wy, wz)
            total = total + (b[r] - (diag[r] * centre - around))
        t512[i] = total
        return carry

    lax.fori_loop(0, rows1, residual_body, 0)
    put_tiles(t256, dot_exact(t512[...].reshape(rows1 * ec, depth), pairs[...]))
    for i in range(rows1):
        start = i * ec + H
        right1[i] = 0.125 * (every_other(t256, start, cols1) + every_other(t256, start + 1, cols1))

    for r in range(rows1 + 2 * H):
        y, z = w1e[1, r], w1e[2, r]
        total = MASS + w1e[0, r] + w1e[0, max(r - 1, 0)] + y + back(y, 0) + z + back(z, 1)
        diag1[r] = total
        rdiag1[r] = 1.0 / total
    for k in range(H):
        value = right1[rows1 - H + k]
        to_up[k] = value * rdiag1[rows1 + k, H : H + cols1] if k == 0 else value
        value = right1[k]
        to_down[k] = value * rdiag1[H + k, H : H + cols1] if k == H - 1 else value

    own_parity = parity2((cols, depth))
    for r in range(rows):
        v_own[r] = v[H + r, H : H + cols]
    for k in range(H // 2):
        for out, base in ((merged_up, rows - H), (merged_down, 0)):
            r = base + 2 * k
            out[k] = jnp.where(own_parity == ((r + 1) & 1), v_own[r], v_own[r + 1])


def pack1_kernel(own, up, down, rdiag1, to_right, to_left):
    rows, cols, depth = own.shape
    for out, base in ((to_right, cols - H), (to_left, 0)):
        for n in range(rows + 2 * H - 2):
            r = n + 1
            if r < H:
                value, distance = up[r], H - r
            elif r < H + rows:
                value, distance = own[r - H], 0
            else:
                value, distance = down[r - H - rows], r - H - rows + 1
            if out is to_right:
                c = cols - (H - distance)
            else:
                c = H - distance - 1
            edge = lax.broadcasted_iota(jnp.int32, value.shape, 0) == c
            value = jnp.where(edge, value * rdiag1[r, H : H + cols], value)
            s = H * (n % 2)
            out[n // 2, s : s + H] = value[base : base + H]


def fill1(ext, own, up, down, right, left):
    rows, cols, depth = own.shape
    for r in range(rows):
        ext[H + r, H : H + cols] = own[r]
    for k in range(H):
        ext[k, H : H + cols] = up[k]
        ext[H + rows + k, H : H + cols] = down[k]
    for n in range(rows + 2 * H - 2):
        s = H * (n % 2)
        ext[n + 1, 0:H] = right[n // 2, s : s + H]
        ext[n + 1, H + cols : 2 * H + cols] = left[n // 2, s : s + H]


def pre1_kernel(own, up, down, right, left, w1e, rdiag1, diag1, pairs, merged_up, merged_down, *rest):
    b1, v_own, chunk, to_up, to_down = rest[:5]
    v, t256, t128 = rest[5:]
    rows, cols, depth = own.shape
    er, ec = rows + 2 * H, cols + 2 * H
    half = depth // 2
    wx, wy, wz = w1e.at[0], w1e.at[1], w1e.at[2]
    fill1(b1, own, up, down, right, left)
    parity = parity2((ec, depth))
    col = lax.broadcasted_iota(jnp.int32, (ec, depth), 0)
    col_distance = jnp.maximum(jnp.maximum(H - col, col - (H + cols - 1)), 0)
    for r in range(er):
        distance = max(H - r, r - (H + rows - 1), 0)
        first = jnp.where(col_distance + distance >= H, b1[r], b1[r] * rdiag1[r])
        v[r] = jnp.where(parity == (r & 1), first, 0.0)
    half_sweep(1, er - 1, 1, parity, v, b1, wx, wy, wz, rdiag1)
    half_sweep(2, er - 2, 0, parity, v, b1, wx, wy, wz, rdiag1)
    half_sweep(3, er - 3, 1, parity, v, b1, wx, wy, wz, rdiag1)
    for i in range(rows // 2):
        total = 0.0
        for k in range(2):
            r = H + 2 * i + k
            centre, around = row_sum(r, v, wx, wy, wz)
            total = total + (b1[r] - (diag1[r] * centre - around))
        t256[i] = total
    n = rows // 2
    put_tiles(t128, dot_exact(t256[...].reshape(n * ec, depth), pairs[...]))
    for i in range(n):
        start = i * ec + H
        chunk[i * (cols // 2) : (i + 1) * (cols // 2)] = 0.125 * (
            every_other(t128, start, cols // 2) + every_other(t128, start + 1, cols // 2)
        )
    lane = lax.broadcasted_iota(jnp.int32, (1, half), 1)
    row_odd = lax.broadcasted_iota(jnp.int32, (cols, depth), 0) & 1
    depth_odd = lax.broadcasted_iota(jnp.int32, (cols, depth), 1) & 1
    parts = [0.0, 0.0, 0.0]
    for i in range(rows):
        if i % 2 == 1:
            parts[0] = parts[0] + w1e[0, H + i, H : H + cols]
        parts[1] = parts[1] + jnp.where(row_odd == 1, w1e[1, H + i, H : H + cols], 0.0)
        parts[2] = parts[2] + jnp.where(depth_odd == 1, w1e[2, H + i, H : H + cols], 0.0)
    line = jnp.zeros((1, half), F32)
    for d in range(3):
        line = jnp.where(lane == d, 0.0625 * jnp.sum(parts[d]), line)
    n = (rows // 2) * (cols // 2)
    chunk[n : n + 1] = line

    for r in range(rows):
        v_own[r] = v[H + r, H : H + cols]
    for out, base, merged in ((to_up, rows - H, merged_up), (to_down, 0, merged_down)):
        for k in range(H // 2):
            out[k] = jnp.concatenate((v_own[base + 2 * k], v_own[base + 2 * k + 1]), axis=1)
            for t in range(merged.shape[1] // 8):
                out[H // 2 + k * (merged.shape[1] // 8) + t] = merged[k, 8 * t : 8 * t + 8]


def pack_v_kernel(v1, up, down, v0, to_right, to_left):
    rows1, cols1, half = v1.shape
    rows, cols, depth = v0.shape
    tiles = cols // 8
    parity = parity2((cols, depth))
    for out, base1, base in ((to_right, cols1 - H, cols - H), (to_left, 0, 0)):
        for n in range(rows1 + 2 * H - 2):
            r = n + 1
            if r < H:
                line = up[r // 2, base1 : base1 + H, half * (r % 2) : half * (r % 2) + half]
            elif r < H + rows1:
                line = v1[r - H, base1 : base1 + H]
            else:
                k = r - H - rows1
                line = down[k // 2, base1 : base1 + H, half * (k % 2) : half * (k % 2) + half]
            s, lane = H * (n % 2), half * ((n // 2) % 2)
            out[n // 4, s : s + H, lane : lane + half] = line
        start = (rows1 + 2 * H - 2 + 3) // 4
        for r in range(rows):
            value = v0[r]
            value = jnp.where(parity == ((r + 1) & 1), value, ahead(value, 0))
            for p in range(H // 2):
                n = p * rows + r
                out[start + n // 8, n % 8 : n % 8 + 1] = value[base + 2 * p : base + 2 * p + 1]
        start += (rows * (H // 2)) // 8
        for m, msg in enumerate((up, down)):
            for k in range(H // 2):
                c = base // 8
                tile = msg[H // 2 + k * tiles + c]
                n = m * (H // 2) + k
                out[start + n // 2, H * (n % 2) : H * (n % 2) + H] = tile[base % 8 : base % 8 + H]


def solve_kernel(got, forward, back_x, back_y, depth_in, depth_out, eig_x, eig_y, eig_z, out, *, count):
    devices, lines, depth = got.shape
    own = lines - 1
    values = jnp.concatenate([got[d, 0:own] for d in range(devices)], axis=0)
    sums = got[0, own : own + 1]
    for d in range(1, devices):
        sums = sums + got[d, own : own + 1]
    sums = sums * (1.0 / count)
    lam = MASS + sums[0:1, 0:1] * eig_x[...] + sums[0:1, 1:2] * eig_y[...] + sums[0:1, 2:3] * eig_z[...]
    spec = dot_pair(forward[...], dot_pair(values, depth_in[...]))
    spec = spec / (lam * float(count))
    spec = dot_pair(spec, depth_out[...])
    rx, ry = back_x.shape[0], back_y.shape[0]
    table = jnp.concatenate([back_x[i : i + 1] * back_y[...] for i in range(rx)], axis=0)
    out[...] = dot_pair(table, spec).reshape(out.shape)


def post1_kernel(v1, up, down, right, left, correction, b1, w1e, rdiag1, out, v):
    rows, cols, depth = v1.shape
    er, ec = rows + 2 * H, cols + 2 * H
    for r in range(rows):
        v[H + r, H : H + cols] = v1[r]
    for k in range(H):
        lane = depth * (k % 2)
        v[k, H : H + cols] = up[k // 2, :, lane : lane + depth]
        v[H + rows + k, H : H + cols] = down[k // 2, :, lane : lane + depth]
    for n in range(rows + 2 * H - 2):
        s, lane = H * (n % 2), depth * ((n // 2) % 2)
        v[n + 1, 0:H] = right[n // 4, s : s + H, lane : lane + depth]
        v[n + 1, H + cols : 2 * H + cols] = left[n // 4, s : s + H, lane : lane + depth]
    for r in range(er):
        v[r] = v[r] + correction[r]
    parity = parity2((ec, depth))
    wx, wy, wz = w1e.at[0], w1e.at[1], w1e.at[2]
    half_sweep(1, er - 1, 0, parity, v, b1, wx, wy, wz, rdiag1)
    half_sweep(2, er - 2, 1, parity, v, b1, wx, wy, wz, rdiag1)
    half_sweep(3, er - 3, 0, parity, v, b1, wx, wy, wz, rdiag1)
    half_sweep(4, er - 4, 1, parity, v, b1, wx, wy, wz, rdiag1)
    for r in range(rows):
        out[r] = v[H + r, H : H + cols]


def pack2_kernel(own, up, down, to_right, to_left):
    rows, cols, depth = own.shape
    h = H // 2
    for out, base in ((to_right, cols - h), (to_left, 0)):
        for n in range(rows + 2 * h):
            if n < h:
                line = up[n, base : base + h]
            elif n < h + rows:
                line = own[n - h, base : base + h]
            else:
                line = down[n - h - rows, base : base + h]
            s = h * (n % 4)
            out[n // 4, s : s + h] = line


def post_kernel(v0, up, down, right, left, own1, up1, down1, right1, left1, b, wx, wy, wz, rdiag, spread, out, v, t256):
    rows, cols, depth = v0.shape
    rows1, cols1, half = own1.shape
    er, ec = rows + 2 * H, cols + 2 * H
    h = H // 2
    tiles = cols // 8
    for r in range(rows):
        v[H + r, H : H + cols] = v0[r]
    for msg, base in ((up, 0), (down, H + rows)):
        for k in range(H // 2):
            for t in range(tiles):
                tile = msg[H // 2 + k * tiles + t]
                v[base + 2 * k, H + 8 * t : H + 8 * t + 8] = tile
                v[base + 2 * k + 1, H + 8 * t : H + 8 * t + 8] = tile
    for msg, base in ((right, 0), (left, H + cols)):
        start = (rows1 + 2 * H - 2 + 3) // 4
        for r in range(rows):
            for p in range(H // 2):
                n = p * rows + r
                line = msg[start + n // 8, n % 8 : n % 8 + 1]
                v[H + r, base + 2 * p : base + 2 * p + 2] = jnp.broadcast_to(line, (2, depth))
        start += (rows * (H // 2)) // 8
        for m, row in enumerate((0, H + rows)):
            for k in range(H // 2):
                n = m * (H // 2) + k
                block = msg[start + n // 2, H * (n % 2) : H * (n % 2) + H]
                v[row + 2 * k, base : base + H] = block
                v[row + 2 * k + 1, base : base + H] = block
    ec1 = cols1 + 2 * h
    for n in range(rows1 + 2 * h):
        if n < h:
            line = up1[n]
        elif n < h + rows1:
            line = own1[n - h]
        else:
            line = down1[n - h - rows1]
        s = h * (n % 4)
        t256[n, h : h + cols1] = line
        t256[n, 0:h] = right1[n // 4, s : s + h]
        t256[n, h + cols1 : ec1] = left1[n // 4, s : s + h]
        t256[n, ec1:] = jnp.zeros((t256.shape[1] - ec1, half), F32)
    n1 = rows1 + 2 * h
    wide = dot_exact(t256[...].reshape(n1 * t256.shape[1], half), spread[...])
    wide = wide.reshape(n1, t256.shape[1], depth)
    for n in range(n1):
        line = wide[n, 0:ec1]
        line = jnp.broadcast_to(line[:, None, :], (ec1, 2, depth)).reshape(2 * ec1, depth)
        v[2 * n] = v[2 * n] + line
        v[2 * n + 1] = v[2 * n + 1] + line
    parity = parity2((ec, depth))
    half_sweep(1, er - 1, 0, parity, v, b, wx, wy, wz, rdiag)
    half_sweep(2, er - 2, 1, parity, v, b, wx, wy, wz, rdiag)
    half_sweep(3, er - 3, 0, parity, v, b, wx, wy, wz, rdiag)
    half_sweep(4, er - 4, 1, parity, v, b, wx, wy, wz, rdiag)
    for r in range(rows):
        out[r] = v[H + r, H : H + cols]


def hartley(rows, columns, length):
    angle = (np.outer(rows, columns) % length) * (2.0 * math.pi / length)
    return np.cos(angle) + np.sin(angle)


def waves(length):
    return 2.0 * (1.0 - np.cos(np.arange(length) * (2.0 * math.pi / length)))


def coarse_correction(chunk, rows, cols, depth):
    nx, ny = lax.axis_size("gx"), lax.axis_size("gy")
    total_rows, total_cols = rows * nx, cols * ny
    count = total_rows * total_cols * depth
    got = lax.all_to_all(jnp.broadcast_to(chunk[None], (nx * ny,) + chunk.shape), BOTH, 0, 0)
    out_rows, out_cols = 2 * rows + 2 * H, 2 * cols + 2 * H
    rows_ids = (np.arange(-H, 2 * total_rows + H) // 2) % total_rows
    cols_ids = (np.arange(-H, 2 * total_cols + H) // 2) % total_cols
    table_x = hartley(rows_ids, np.arange(total_rows), total_rows)
    table_y = hartley(cols_ids, np.arange(total_cols), total_cols)
    depth_in = hartley(np.arange(depth), np.arange(depth), depth)
    depth_out = np.repeat(depth_in, 2, axis=1)

    def own(table, axis, step, size):
        table = jnp.asarray(table, F32)
        return lax.dynamic_slice_in_dim(table, lax.axis_index(axis) * step, size, 0)

    if total_rows * total_cols <= 512:
        cells = total_rows * total_cols
        order = np.arange(cells).reshape(nx, rows, ny, cols).transpose(0, 2, 1, 3).reshape(-1)
        forward = np.einsum(
            "ax,by->abxy",
            hartley(np.arange(total_rows), np.arange(total_rows), total_rows),
            hartley(np.arange(total_cols), np.arange(total_cols), total_cols),
        ).reshape(cells, cells)[:, order]
        back_x = own(np.repeat(table_x, total_cols, axis=1), "gx", 2 * rows, out_rows)
        back_y = own(np.tile(table_y, (1, total_rows)), "gy", 2 * cols, out_cols)
        ones = np.ones((cells, depth))
        eig = (
            np.repeat(waves(total_rows), total_cols)[:, None] * ones,
            np.tile(waves(total_cols), total_rows)[:, None] * ones,
            waves(depth)[None, :] * ones,
        )
        constants = [jnp.asarray(x, F32) for x in (forward, depth_in, depth_out) + eig]
        return call(
            functools.partial(solve_kernel, count=count),
            [(out_rows, out_cols, 2 * depth)],
            got, constants[0], back_x, back_y, *constants[1:],
        )[0]

    hi = lax.Precision.HIGHEST
    averages = jnp.sum(got[:, rows * cols, :3], axis=0) / count
    full = got[:, : rows * cols].reshape(nx, ny, rows, cols, depth)
    full = full.transpose(0, 2, 1, 3, 4).reshape(total_rows, total_cols, depth)
    f32 = lambda x: jnp.asarray(x, F32)
    spec = jnp.einsum("abz,zk->abk", full, f32(depth_in), precision=hi)
    spec = jnp.einsum("ij,jbz->ibz", f32(hartley(np.arange(total_rows), np.arange(total_rows), total_rows)), spec, precision=hi)
    spec = jnp.einsum("ij,ajz->aiz", f32(hartley(np.arange(total_cols), np.arange(total_cols), total_cols)), spec, precision=hi)
    lam = (
        MASS
        + averages[0] * f32(waves(total_rows))[:, None, None]
        + averages[1] * f32(waves(total_cols))[None, :, None]
        + averages[2] * f32(waves(depth))[None, None, :]
    )
    spec = spec / (lam * float(count))
    out = jnp.einsum("ij,jbz->ibz", own(table_x, "gx", 2 * rows, out_rows), spec, precision=hi)
    out = jnp.einsum("ij,ajz->aiz", own(table_y, "gy", 2 * cols, out_cols), out, precision=hi)
    return jnp.einsum("abz,zk->abk", out, f32(depth_out), precision=hi)


def shards(source, face_coef):
    rows, cols, depth = source.shape
    rows1, cols1, depth1 = rows // 2, cols // 2, depth // 2
    er, ec, er1, ec1 = rows + 2 * H, cols + 2 * H, rows1 + 2 * H, cols1 + 2 * H
    pairs = jnp.asarray(pair_table(depth))
    odds = jnp.asarray(odd_table(depth))

    nx_tiles = 4 * H * (cols // 8) + 3 * (H // 2)
    ny_tiles = 2 * rows + rows // 4 + (rows // 2 + 3) // 4
    corner_tiles = len(CORNER0) // 8 + 1
    *sends, w1 = call(
        pack_kernel,
        [(nx_tiles, 8, depth)] * 2 + [(ny_tiles, 8, depth)] * 2 + [(corner_tiles, 8, depth)] * 4 + [(3, rows1, cols1, depth1)],
        source, face_coef, pairs, odds,
        scratch=[(depth1 // 128, cols, 128)],
    )
    right, left = moved(sends[2], 0, 1), moved(sends[3], 0, -1)
    corners = [moved(m, dx, dy) for m, (dx, dy) in zip(sends[4:], ((1, 1), (1, -1), (-1, 1), (-1, -1)))]
    up, down = moved(sends[0], 1, 0), moved(sends[1], -1, 0)

    b, wx, wy, wz, rdiag, v0, right1, to_up, to_down, w1e, rdiag1, diag1, merged_up, merged_down = call(
        pre_kernel,
        [(er, ec, depth)] * 5
        + [(rows, cols, depth), (rows1, cols1, depth1)]
        + [(H, cols1, depth1)] * 2
        + [(3, er1, ec1, depth1), (er1, ec1, depth1), (er1, ec1, depth1)]
        + [(H // 2, cols, depth)] * 2,
        source, face_coef, w1, up, down, right, left, *corners, pairs,
        scratch=[(er, ec, depth), (er, ec, depth), (rows1, ec, depth), (depth1 // 128, rows1 * ec, 128)],
    )

    up, down = moved(to_up, 1, 0), moved(to_down, -1, 0)
    beside = (er1 - 2 + 1) // 2
    to_right, to_left = call(pack1_kernel, [(beside, 8, depth1)] * 2, right1, up, down, rdiag1)
    right, left = moved(to_right, 0, 1), moved(to_left, 0, -1)
    x_tiles = H // 2 + (H // 2) * (cols // 8)
    b1, v1, chunk, to_up, to_down = call(
        pre1_kernel,
        [(er1, ec1, depth1), (rows1, cols1, depth1), (rows1 * cols1 // 4 + 1, depth1 // 2)]
        + [(x_tiles, 8, depth)] * 2,
        right1, up, down, right, left, w1e, rdiag1, diag1, jnp.asarray(pair_table(depth1)), merged_up, merged_down,
        scratch=[(er1, ec1, depth1), (rows1 // 2, ec1, depth1), (depth1 // 256, rows1 // 2 * ec1, 128)],
    )

    up, down = moved(to_up, 1, 0), moved(to_down, -1, 0)
    correction2 = coarse_correction(chunk, rows1 // 2, cols1 // 2, depth1 // 2)
    y_tiles = (er1 - 2 + 3) // 4 + (rows * (H // 2)) // 8 + H // 2
    to_right, to_left = call(pack_v_kernel, [(y_tiles, 8, depth)] * 2, v1, up, down, v0)
    right, left = moved(to_right, 0, 1), moved(to_left, 0, -1)
    (v1,) = call(
        post1_kernel,
        [(rows1, cols1, depth1)],
        v1, up, down, right, left, correction2, b1, w1e, rdiag1,
        scratch=[(er1, ec1, depth1)],
    )

    h = H // 2
    up1, down1 = moved(v1[rows1 - h :], 1, 0), moved(v1[:h], -1, 0)
    to_right, to_left = call(pack2_kernel, [((rows1 + 2 * h) // 4, 8, depth1)] * 2, v1, up1, down1)
    right1, left1 = moved(to_right, 0, 1), moved(to_left, 0, -1)
    (out,) = call(
        post_kernel,
        [(rows, cols, depth)],
        v0, up, down, right, left, v1, up1, down1, right1, left1, b, wx, wy, wz, rdiag,
        jnp.asarray(np.ascontiguousarray(pair_table(depth).T)),
        scratch=[(er, ec, depth), (rows1 + 2 * h, 16, depth1)],
    )
    return out


def solution(mesh):
    return jax.shard_map(
        shards,
        mesh=mesh,
        in_specs=(P("gx", "gy", None), P(None, "gx", "gy", None)),
        out_specs=P("gx", "gy", None),
        check_vma=False,
    )
```

```python
import functools
import math

import jax
import jax.numpy as jnp
import ml_dtypes
import numpy as np
from jax import lax
from jax.experimental import pallas as pl
from jax.experimental.pallas import tpu as pltpu
from jax.sharding import PartitionSpec as P

LEVELS = 3
SWEEPS = 2
MASS = 0.002
BOTH = ("gx", "gy")
H = 2 * SWEEPS
F32 = jnp.float32
UNROLL = 4
VMEM_LIMIT = 12 * 1024 * 1024
K1LIMIT = 12 * 1024 * 1024
BF16 = jnp.bfloat16
VMEM = pl.BlockSpec(memory_space=pltpu.VMEM)
HBM = pl.BlockSpec(memory_space=pltpu.HBM)

CORNER0 = (
    (0, 1, 1), (0, 1, 2), (0, 1, 3), (1, 2, 3), (3, 1, 1), (3, 1, 2), (3, 1, 3), (2, 2, 3),
    (1, 1, 1), (1, 1, 2), (1, 1, 3), (1, 1, 4), (2, 1, 1), (2, 1, 2), (2, 1, 3), (2, 1, 4),
    (0, 2, 1), (0, 2, 2), (0, 3, 1), (1, 4, 1), (3, 2, 1), (3, 2, 2), (3, 3, 1), (2, 4, 1),
    (1, 2, 1), (1, 2, 2), (1, 3, 1), (1, 3, 2), (2, 2, 1), (2, 2, 2), (2, 3, 1), (2, 3, 2),
)
CORNER1 = (
    (0, 1, 1), (0, 1, 2), (0, 1, 3), (0, 2, 1), (0, 2, 2), (0, 3, 1), (2, 1, 1), (2, 1, 2),
    (1, 1, 1), (1, 1, 2), (1, 1, 3), (1, 2, 1), (1, 2, 2), (1, 3, 1), (2, 2, 1), None,
)


def call(kernel, out, *args, scratch=(), remote=(), limit=VMEM_LIMIT, near=()):
    count = len(args)
    args = (*args, *near)

    def body(*refs):
        kernel(*refs[:count], *refs[len(args) :])

    return pl.pallas_call(
        body,
        out_shape=[s if hasattr(s, "dtype") else jax.ShapeDtypeStruct(s, F32) for s in out],
        in_specs=[HBM if i in remote else VMEM for i in range(len(args))],
        out_specs=[VMEM] * len(out),
        scratch_shapes=[pltpu.VMEM(s, F32) if isinstance(s, tuple) else s for s in scratch],
        compiler_params=pltpu.CompilerParams(vmem_limit_bytes=limit),
    )(*args)


def moved(block, dx, dy):
    nx, ny = lax.axis_size("gx"), lax.axis_size("gy")
    if dy == 0:
        return lax.ppermute(block, "gx", [(i, (i + dx) % nx) for i in range(nx)])
    if dx == 0:
        return lax.ppermute(block, "gy", [(j, (j + dy) % ny) for j in range(ny)])
    route = []
    for i in range(nx):
        for j in range(ny):
            route.append((i * ny + j, ((i + dx) % nx) * ny + (j + dy) % ny))
    return lax.ppermute(block, BOTH, route)


def split3(x):
    high = x.astype(BF16)
    rest = x - high.astype(F32)
    middle = rest.astype(BF16)
    return high, middle, (rest - middle.astype(F32)).astype(BF16)


def dot(a, b):
    return jnp.dot(a, b, preferred_element_type=F32)


def dot_exact(x, table):
    high, middle, low = split3(x)
    return dot(high, table) + (dot(middle, table) + dot(low, table))


def pair_table(depth):
    table = np.zeros((depth, depth // 2), ml_dtypes.bfloat16)
    table[np.arange(depth), np.arange(depth) // 2] = 1
    return table


def put_tiles(tiles, x):
    for k in range(tiles.shape[0]):
        tiles[k] = x[:, 128 * k : 128 * k + 128]


def every_other(tiles, start, size):
    return jnp.concatenate(
        [tiles[k, pl.ds(start, size, stride=2), :] for k in range(tiles.shape[0])], axis=1
    )


def back(x, axis):
    return pltpu.roll(x, 1, axis)


def ahead(x, axis):
    return pltpu.roll(x, x.shape[axis] - 1, axis)


def parity2(shape):
    return (lax.broadcasted_iota(jnp.int32, shape, 0) + lax.broadcasted_iota(jnp.int32, shape, 1)) & 1


def row_sum(r, v, wx, wy, wz):
    centre = v[r]
    y, z = wy[r], wz[r]
    total = wx[r] * v[r + 1] + wx[r - 1] * v[r - 1]
    total = total + y * ahead(centre, 0) + back(y * centre, 0)
    return centre, total + z * ahead(centre, 1) + back(z * centre, 1)


def half_sweep(first, last, colour, parity, v, b, wx, wy, wz, rdiag):
    unroll = UNROLL if v.shape[-1] > 256 else last - first

    def body(r, carry):
        centre, total = row_sum(r, v, wx, wy, wz)
        mine = parity == ((r + colour) & 1)
        v[r] = jnp.where(mine, (b[r] + total) * rdiag[r], centre)
        return carry

    lax.fori_loop(first, last, body, 0, unroll=unroll)


def pack_kernel(src_in, face_in, to_right, to_left, to_up, to_down, w1, src, face, pairs, *scratch):
    odds, tx, sem = scratch
    rows, cols, depth = src.shape
    half = depth // 2
    copies = [pltpu.make_async_copy(src_in, src, sem.at[0]), pltpu.make_async_copy(face_in, face, sem.at[1])]
    for copy in copies:
        copy.start()
    fine = lax.broadcasted_iota(jnp.int32, pairs.shape, 0)
    coarse = 2 * lax.broadcasted_iota(jnp.int32, pairs.shape, 1)
    pairs[...] = jnp.where((fine & -2) == coarse, 1.0, 0.0).astype(BF16)
    odds[...] = jnp.where(fine == coarse + 1, 1.0, 0.0).astype(BF16)
    for copy in copies:
        copy.wait()

    for i in range(rows // 2):
        put_tiles(tx, dot(face[0, 2 * i + 1], pairs[...]))
        w1[0, i] = 0.0625 * (every_other(tx, 0, cols // 2) + every_other(tx, 1, cols // 2))
        put_tiles(tx, dot(face[1, 2 * i], pairs[...]) + dot(face[1, 2 * i + 1], pairs[...]))
        w1[1, i] = 0.0625 * every_other(tx, 1, cols // 2)
        put_tiles(tx, dot(face[2, 2 * i], odds[...]) + dot(face[2, 2 * i + 1], odds[...]))
        w1[2, i] = 0.0625 * (every_other(tx, 0, cols // 2) + every_other(tx, 1, cols // 2))

    def plane(a, r):
        return src[r] if a == 0 else face[a - 1, r].astype(F32)

    for out, base, base1 in ((to_right, cols - H, cols // 2 - H), (to_left, 0, 0)):
        for r in range(rows):
            for t, pair in enumerate(((0, 3), (1, 2))):
                for s, a in enumerate(pair):
                    value = plane(a, r)
                    if out is to_right and a == 3:
                        value_all = value + back(value, 1) + back(plane(2, r), 0)
                        first = lax.broadcasted_iota(jnp.int32, value.shape, 0) == base
                        value = jnp.where(first, value_all, value)
                    out[2 * r + t, H * s : H * s + H] = value[base : base + H]
        for i in range(rows // 2):
            k, lane = 2 * rows + i // 2, half * (i % 2)
            out[k, 0:H, lane : lane + half] = w1[0, i, base1 : base1 + H]
            out[k, H : 2 * H, lane : lane + half] = w1[1, i, base1 : base1 + H]
            k = 2 * rows + rows // 4 + i // 4
            s = H * (i % 2)
            lane = half * ((i // 2) % 2)
            out[k, s : s + H, lane : lane + half] = w1[2, i, base1 : base1 + H]

    for out, base in ((to_up, rows - H), (to_down, 0)):
        for a in range(4):
            for k in range(H):
                value = plane(a, base + k)
                if out is to_up and a == 3 and k == 0:
                    value = value + back(value, 1) + plane(1, base - 1)
                for t in range(cols // 8):
                    out[(a * H + k) * (cols // 8) + t] = value[8 * t : 8 * t + 8]
        base1 = 4 * H * (cols // 8)
        for d in range(3):
            for i in range(H // 2):
                out[base1 + d * (H // 2) + i] = jnp.concatenate((w1[d, 2 * i], w1[d, 2 * i + 1]), axis=1)


def forward_kernel(right, left, to_up, to_down, *, rows):
    half = right.shape[2] // 2
    tiles = to_up.shape[0] // 2
    place = {0: (0, 0), 3: (0, 1), 1: (1, 0), 2: (1, 1)}
    for msg, sy in ((right, 1), (left, -1)):
        start = 0 if sy > 0 else tiles
        for out, sx in ((to_up, 1), (to_down, -1)):
            for n, (a, dx, dy) in enumerate(CORNER0):
                r = rows - dx if sx > 0 else dx - 1
                t, s = place[a]
                s = H * s + (H - dy if sy > 0 else dy - 1)
                out[start + n // 8, n % 8 : n % 8 + 1] = msg[2 * r + t, s : s + 1]
            for n, entry in enumerate(CORNER1):
                if entry is None:
                    continue
                d, dx, dy = entry
                i = rows // 2 - dx if sx > 0 else dx - 1
                c = H - dy if sy > 0 else dy - 1
                if d == 2:
                    k, s, lane = 2 * rows + rows // 4 + i // 4, H * (i % 2) + c, half * ((i // 2) % 2)
                else:
                    k, s, lane = 2 * rows + i // 2, H * d + c, half * (i % 2)
                to = half * (n // 8)
                out[start + tiles - 1, n % 8 : n % 8 + 1, to : to + half] = msg[k, s : s + 1, lane : lane + half]


def diagonal_row(r, parity, low_col, b, wx, wy, wz, diag, rdiag, v):
    y, z = wy[r], wz[r]
    if isinstance(r, int) and r == 0:
        total = MASS + wx[r] + z + y + back(y, 0)
    else:
        total = MASS + wx[r] + wx[r - 1] + y
        total = total + jnp.where(low_col, z, z + back(z, 1) + back(y, 0))
    diag[r] = total
    inverse = 1.0 / total
    rdiag[r] = inverse
    v[r] = jnp.where(parity == (r & 1), b[r] * inverse, 0.0)


def assemble_kernel(src, face, w1, up, down, right, left, state, w1e):
    b, wx, wy, wz, rdiag, diag, v = (state.at[i] for i in range(7))
    rows, cols, depth = src.shape
    half = depth // 2
    ext = (b, wx, wy, wz)
    er, ec = rows + 2 * H, cols + 2 * H
    rows1, cols1 = rows // 2, cols // 2

    for r in range(rows):
        b[H + r, H : H + cols] = src[r]
        for d in range(3):
            ext[1 + d][H + r, H : H + cols] = face[d, r].astype(F32)
    for d in range(3):
        for i in range(rows1):
            w1e[d, H + i, H : H + cols1] = w1[d, i]
    tiles = cols // 8
    for msg, base, base1 in ((up, 0, 0), (down, H + rows, H + rows1)):
        for a in range(4):
            for k in range(H):
                for t in range(tiles):
                    ext[a][base + k, H + 8 * t : H + 8 * t + 8] = msg[(a * H + k) * tiles + t]
        n = 4 * H * tiles
        for d in range(3):
            for i in range(H):
                lane = half * (i % 2)
                w1e[d, base1 + i, H : H + cols1] = msg[n + d * (H // 2) + i // 2, :, lane : lane + half]
    for msg, base, base1 in ((right, 0, 0), (left, H + cols, H + cols1)):
        for r in range(rows):
            for t, pair in enumerate(((0, 3), (1, 2))):
                for s, a in enumerate(pair):
                    ext[a][H + r, base : base + H] = msg[2 * r + t, H * s : H * s + H]
        for i in range(rows1):
            k, lane = 2 * rows + i // 2, half * (i % 2)
            w1e[0, H + i, base1 : base1 + H] = msg[k, 0:H, lane : lane + half]
            w1e[1, H + i, base1 : base1 + H] = msg[k, H : 2 * H, lane : lane + half]
            k = 2 * rows + rows // 4 + i // 4
            s = H * (i % 2)
            lane = half * ((i // 2) % 2)
            w1e[2, H + i, base1 : base1 + H] = msg[k, s : s + H, lane : lane + half]
    parity = parity2((ec, depth))
    low_col = lax.broadcasted_iota(jnp.int32, (ec, depth), 0) == 0

    def body(r, carry):
        diagonal_row(r, parity, low_col, b, wx, wy, wz, diag, rdiag, v)
        return carry

    lax.fori_loop(H + 1, H + rows, body, 0)


def pre_kernel(up, down, pairs, *rest):
    state, w1_in, kept, w1e = rest[:4]
    (v_own, right1, to_right, to_left, rdiag1, diag1, merged_right, merged_left) = rest[4:12]
    t512, t256, diag, v = rest[12:]
    b, wx, wy, wz, rdiag = (kept.at[i] for i in range(5))
    kept[...] = state[0:5]
    diag[...] = state[5]
    v[...] = state[6]
    w1e[...] = w1_in[...]
    ext = (b, wx, wy, wz)
    rows, cols, depth = v_own.shape
    half = depth // 2
    er, ec = rows + 2 * H, cols + 2 * H
    rows1, cols1 = rows // 2, cols // 2
    tiles = len(CORNER0) // 8 + 1
    for msg, sx, sy in ((up, 1, 1), (up, 1, -1), (down, -1, 1), (down, -1, -1)):
        start = 0 if sy > 0 else tiles

        def at(distance, size, sign):
            return H - distance if sign > 0 else H + size + distance - 1

        for n, (a, dx, dy) in enumerate(CORNER0):
            r, c = at(dx, rows, sx), at(dy, cols, sy)
            ext[a][r, c : c + 1] = msg[start + n // 8, n % 8 : n % 8 + 1]
        for n, entry in enumerate(CORNER1):
            if entry is None:
                continue
            d, dx, dy = entry
            r, c = at(dx, rows1, sx), at(dy, cols1, sy)
            lane = half * (n // 8)
            w1e[d, r, c : c + 1] = msg[start + tiles - 1, n % 8 : n % 8 + 1, lane : lane + half]

    parity = parity2((ec, depth))
    low_col = lax.broadcasted_iota(jnp.int32, (ec, depth), 0) == 0
    for r in (*range(H + 1), *range(H + rows, er)):
        diagonal_row(r, parity, low_col, b, wx, wy, wz, diag, rdiag, v)
    half_sweep(1, er - 1, 1, parity, v, b, wx, wy, wz, rdiag)
    half_sweep(2, er - 2, 0, parity, v, b, wx, wy, wz, rdiag)
    half_sweep(3, er - 3, 1, parity, v, b, wx, wy, wz, rdiag)

    def residual_body(i, carry):
        total = 0.0
        for k in range(2):
            r = H + 2 * i + k
            centre, around = row_sum(r, v, wx, wy, wz)
            total = total + (b[r] - (diag[r] * centre - around))
        t512[i] = total
        return carry

    lax.fori_loop(0, rows1, residual_body, 0, unroll=UNROLL)
    put_tiles(t256, dot_exact(t512[...].reshape(rows1 * ec, depth), pairs[...]))
    for i in range(rows1):
        start = i * ec + H
        right1[i] = 0.125 * (every_other(t256, start, cols1) + every_other(t256, start + 1, cols1))

    for r in range(rows1 + 2 * H):
        y, z = w1e[1, r], w1e[2, r]
        total = MASS + w1e[0, r] + w1e[0, max(r - 1, 0)] + y + back(y, 0) + z + back(z, 1)
        diag1[r] = total
        rdiag1[r] = 1.0 / total
    for i in range(rows1):
        value, inverse = right1[i], rdiag1[H + i, H : H + cols1]
        col = lax.broadcasted_iota(jnp.int32, value.shape, 0)
        place = (i // 2, slice(H * (i % 2), H * (i % 2) + H))
        to_right[place] = jnp.where(col == cols1 - H, value * inverse, value)[cols1 - H :]
        to_left[place] = jnp.where(col == H - 1, value * inverse, value)[:H]

    own_parity = parity2((cols, depth))
    for r in range(rows):
        value = v[H + r, H : H + cols]
        v_own[r] = value
        value = jnp.where(own_parity == ((r + 1) & 1), value, ahead(value, 0))
        for p in range(H // 2):
            n = p * rows + r
            for out, base in ((merged_right, cols - H), (merged_left, 0)):
                out[n // 8, n % 8 : n % 8 + 1] = value[base + 2 * p : base + 2 * p + 1]


def pack1_kernel(own, right, left, rdiag1, rows_own, to_up, to_down):
    rows, cols, depth = own.shape
    for i in range(rows):
        rows_own[i, H : H + cols] = own[i]
        rows_own[i, 0:H] = right[i // 2, H * (i % 2) : H * (i % 2) + H]
        rows_own[i, H + cols : 2 * H + cols] = left[i // 2, H * (i % 2) : H * (i % 2) + H]
    shape = rows_own.shape[1:]
    col = lax.broadcasted_iota(jnp.int32, shape, 0)
    col_distance = jnp.maximum(jnp.maximum(H - col, col - (H + cols - 1)), 0)
    for k in range(H):
        for out, i, distance in ((to_up, rows - H + k, H - k), (to_down, k, k + 1)):
            edge = col_distance + distance == H
            value = rows_own[i]
            out[k] = jnp.where(edge, value * rdiag1[H + i], value)


def pre1_kernel(rows_own, up, down, w1e, rdiag1, diag1, pairs, merged_right, merged_left, *rest):
    kept, chunks, to_right, to_left = rest[:4]
    chunk = chunks.at[0]
    t256, t128 = rest[4:]
    b1, v = kept.at[4], kept.at[5]
    kept[0:3] = w1e[...]
    kept[3] = rdiag1[...]
    rows, _, depth = rows_own.shape
    cols = rows_own.shape[1] - 2 * H
    er, ec = rows + 2 * H, cols + 2 * H
    half = depth // 2
    wx, wy, wz = w1e.at[0], w1e.at[1], w1e.at[2]
    b1[0:H] = up[...]
    b1[H : H + rows] = rows_own[...]
    b1[H + rows :] = down[...]
    parity = parity2((ec, depth))
    col = lax.broadcasted_iota(jnp.int32, (ec, depth), 0)
    col_distance = jnp.maximum(jnp.maximum(H - col, col - (H + cols - 1)), 0)
    for r in range(er):
        distance = max(H - r, r - (H + rows - 1), 0)
        first = jnp.where(col_distance + distance >= H, b1[r], b1[r] * rdiag1[r])
        v[r] = jnp.where(parity == (r & 1), first, 0.0)
    half_sweep(1, er - 1, 1, parity, v, b1, wx, wy, wz, rdiag1)
    half_sweep(2, er - 2, 0, parity, v, b1, wx, wy, wz, rdiag1)
    half_sweep(3, er - 3, 1, parity, v, b1, wx, wy, wz, rdiag1)
    for i in range(rows // 2):
        total = 0.0
        for k in range(2):
            r = H + 2 * i + k
            centre, around = row_sum(r, v, wx, wy, wz)
            total = total + (b1[r] - (diag1[r] * centre - around))
        t256[i] = total
    n = rows // 2
    put_tiles(t128, dot_exact(t256[...].reshape(n * ec, depth), pairs[...]))
    for i in range(n):
        start = i * ec + H
        chunk[i * (cols // 2) : (i + 1) * (cols // 2)] = 0.125 * (
            every_other(t128, start, cols // 2) + every_other(t128, start + 1, cols // 2)
        )
    lane = lax.broadcasted_iota(jnp.int32, (1, half), 1)
    row_odd = lax.broadcasted_iota(jnp.int32, (cols, depth), 0) & 1
    depth_odd = lax.broadcasted_iota(jnp.int32, (cols, depth), 1) & 1
    parts = [0.0, 0.0, 0.0]
    for i in range(rows):
        if i % 2 == 1:
            parts[0] = parts[0] + w1e[0, H + i, H : H + cols]
        parts[1] = parts[1] + jnp.where(row_odd == 1, w1e[1, H + i, H : H + cols], 0.0)
        parts[2] = parts[2] + jnp.where(depth_odd == 1, w1e[2, H + i, H : H + cols], 0.0)
    line = jnp.zeros((1, half), F32)
    for d in range(3):
        line = jnp.where(lane == d, 0.0625 * jnp.sum(parts[d]), line)
    n = (rows // 2) * (cols // 2)
    chunk[n : n + 1] = line
    value = chunk[...]
    for i in range(1, chunks.shape[0]):
        chunks[i] = value

    for out, base, merged in ((to_right, cols - H, merged_right), (to_left, 0, merged_left)):
        n = merged.shape[0]
        out[0:n] = merged[...]
        for i in range(rows):
            s, lane = H * (i % 2), depth * ((i // 2) % 2)
            out[n + i // 4, s : s + H, lane : lane + depth] = v[H + i, H + base : 2 * H + base]


def pack_v_kernel(kept1, right, left, v0, rows_out, to_up, to_down, v1_rows):
    rows1, ec1, half = v1_rows.shape
    cols1 = ec1 - 2 * H
    rows, cols, depth = v0.shape
    v0_rows = rows_out.at[0:rows]
    n0 = rows * (H // 2) // 8
    for i in range(rows1):
        s, lane = H * (i % 2), half * ((i // 2) % 2)
        v1_rows[i] = kept1[5, H + i]
        v1_rows[i, 0:H] = right[n0 + i // 4, s : s + H, lane : lane + half]
        v1_rows[i, H + cols1 : 2 * H + cols1] = left[n0 + i // 4, s : s + H, lane : lane + half]
    for r in range(rows):
        v0_rows[r, H : H + cols] = v0[r]
        for msg, base in ((right, 0), (left, H + cols)):
            for p in range(H // 2):
                n = p * rows + r
                line = msg[n // 8, n % 8 : n % 8 + 1]
                v0_rows[r, base + 2 * p : base + 2 * p + 2] = jnp.broadcast_to(line, (2, depth))
    ec = v0_rows.shape[1]
    for i in range(rows1 // 2):
        rows_out[rows + i, 0:ec1] = jnp.concatenate((v1_rows[2 * i], v1_rows[2 * i + 1]), axis=1)
    parity = parity2((ec, depth))
    tiles, tiles1 = ec // 8, ec1 // 8
    for out, base, base1 in ((to_up, rows - H, rows1 - H), (to_down, 0, 0)):
        for k in range(H // 2):
            r = base + 2 * k
            value = jnp.where(parity == ((r + 1) & 1), v0_rows[r], v0_rows[r + 1])
            for t in range(tiles):
                out[k * tiles + t] = value[8 * t : 8 * t + 8]
            start = (H // 2) * tiles + k * tiles1
            value = jnp.concatenate((v1_rows[base1 + 2 * k], v1_rows[base1 + 2 * k + 1]), axis=1)
            for t in range(tiles1):
                out[start + t] = value[8 * t : 8 * t + 8]


def split2(x):
    high = x.astype(BF16)
    return high, (x - high.astype(F32)).astype(BF16)


def dot_split(a, b):
    return dot(a[0], b[0]) + (dot(a[0], b[1]) + dot(a[1], b[0]))


def solve_kernel(got, table, out, *, count, start):
    devices, lines, depth = got.shape
    own = lines - 1
    cells = devices * own
    rx, ry, _ = out.shape

    def part(name, size, lane=0, width=None):
        return table[start[name] : start[name] + size, lane : lane + (width or table.shape[1])]

    values = jnp.concatenate([got[d, 0:own] for d in range(devices)], axis=0)
    sums = got[0, own : own + 1]
    for d in range(1, devices):
        sums = sums + got[d, own : own + 1]
    sums = sums * (1.0 / count)
    lam = MASS + sums[0:1, 0:1] * part("eig", cells, 0, depth)
    lam = lam + sums[0:1, 1:2] * part("eig", cells, depth, depth)
    lam = lam + sums[0:1, 2:3] * part("depth", 1, depth, depth)
    spec = dot_split(split2(values), split2(part("depth_in", depth, 0, depth)))
    spec = dot_split(split2(part("forward", cells)), split2(spec))
    spec = spec / (lam * float(count))
    spec = dot_split(split2(spec), split2(part("depth_out", depth)))
    ix, iy = lax.axis_index("gx"), lax.axis_index("gy")
    x_step, y_step = -(-rx // 8) * 8, -(-ry // 8) * 8
    along_x = table[pl.ds(pl.multiple_of(start["x"] + ix * x_step, 8), x_step), :]
    along_y = table[pl.ds(pl.multiple_of(start["y"] + iy * y_step, 8), y_step), :][0:ry]
    back_table = jnp.concatenate([along_x[i : i + 1] * along_y for i in range(rx)], axis=0)
    out[...] = dot_split(split2(back_table), split2(spec)).reshape(out.shape)


def post1_kernel(v_rows, up, down, correction, kept1, out, to_right, to_left, v):
    rdiag1, b1 = kept1.at[3], kept1.at[4]
    rows, cols, depth = out.shape
    er, ec = rows + 2 * H, cols + 2 * H
    start = v_rows.shape[0] - rows // 2
    for i in range(rows // 2):
        value = v_rows[start + i, 0:ec]
        v[H + 2 * i] = value[:, :depth]
        v[H + 2 * i + 1] = value[:, depth:]
    tiles = ec // 8
    for msg, base in ((up, 0), (down, H + rows)):
        start = msg.shape[0] - (H // 2) * tiles
        for k in range(H // 2):
            for t in range(tiles):
                tile = msg[start + k * tiles + t]
                v[base + 2 * k, 8 * t : 8 * t + 8] = tile[:, :depth]
                v[base + 2 * k + 1, 8 * t : 8 * t + 8] = tile[:, depth:]
    for r in range(er):
        v[r] = v[r] + correction[r]
    parity = parity2((ec, depth))
    wx, wy, wz = kept1.at[0], kept1.at[1], kept1.at[2]
    half_sweep(1, er - 1, 0, parity, v, b1, wx, wy, wz, rdiag1)
    half_sweep(2, er - 2, 1, parity, v, b1, wx, wy, wz, rdiag1)
    half_sweep(3, er - 3, 0, parity, v, b1, wx, wy, wz, rdiag1)
    half_sweep(4, er - 4, 1, parity, v, b1, wx, wy, wz, rdiag1)
    for r in range(rows):
        out[r] = v[H + r, H : H + cols]
    h = H // 2
    for r in range(rows):
        s = h * (r % 4)
        to_right[r // 4, s : s + h] = out[r, cols - h : cols]
        to_left[r // 4, s : s + h] = out[r, 0:h]


def pack2_kernel(own, right, left, rows_own, to_up, to_down):
    rows, cols, depth = own.shape
    h = H // 2
    used = cols + 2 * h
    for r in range(rows):
        s = h * (r % 4)
        rows_own[r, h : h + cols] = own[r]
        rows_own[r, 0:h] = right[r // 4, s : s + h]
        rows_own[r, h + cols : used] = left[r // 4, s : s + h]
        if used < rows_own.shape[1]:
            rows_own[r, used:] = jnp.zeros((rows_own.shape[1] - used, depth), F32)
    to_up[...] = rows_own[rows - h :]
    to_down[...] = rows_own[0:h]


def spread_kernel(v0_rows, up, down, v):
    er, ec, _ = v.shape
    rows = er - 2 * H
    v[H : H + rows] = v0_rows[0:rows]
    tiles = ec // 8
    for msg, base in ((up, 0), (down, H + rows)):
        for k in range(H // 2):
            for t in range(tiles):
                tile = msg[k * tiles + t]
                v[base + 2 * k, 8 * t : 8 * t + 8] = tile
                v[base + 2 * k + 1, 8 * t : 8 * t + 8] = tile


def post_kernel(v_in, rows_own, up1, down1, kept, spread, out, v, t256):
    b, wx, wy, wz, rdiag = (kept.at[i] for i in range(5))
    rows, cols, depth = out.shape
    rows1, wide1, half = rows_own.shape
    er, ec = rows + 2 * H, cols + 2 * H
    h = H // 2
    ec1 = cols // 2 + 2 * h
    n1 = rows1 + 2 * h
    t256[0:h] = up1[...]
    t256[h : h + rows1] = rows_own[...]
    t256[h + rows1 :] = down1[...]
    wide = dot_exact(t256[...].reshape(n1 * t256.shape[1], half), spread[...])
    wide = wide.reshape(n1, t256.shape[1], depth)
    for n in range(n1):
        line = wide[n, 0:ec1]
        line = jnp.broadcast_to(line[:, None, :], (ec1, 2, depth)).reshape(2 * ec1, depth)
        v[2 * n] = v_in[2 * n] + line
        v[2 * n + 1] = v_in[2 * n + 1] + line
    parity = parity2((ec, depth))
    half_sweep(1, er - 1, 0, parity, v, b, wx, wy, wz, rdiag)
    half_sweep(2, er - 2, 1, parity, v, b, wx, wy, wz, rdiag)
    half_sweep(3, er - 3, 0, parity, v, b, wx, wy, wz, rdiag)
    half_sweep(4, er - 4, 1, parity, v, b, wx, wy, wz, rdiag)
    for r in range(rows):
        out[r] = v[H + r, H : H + cols]


def hartley(rows, columns, length):
    angle = (np.outer(rows, columns) % length) * (2.0 * math.pi / length)
    return np.cos(angle) + np.sin(angle)


def waves(length):
    return 2.0 * (1.0 - np.cos(np.arange(length) * (2.0 * math.pi / length)))


def windows(table, count, step, size):
    pad = -size % 8
    parts = [np.pad(table[i * step : i * step + size], ((0, pad), (0, 0))) for i in range(count)]
    return np.concatenate(parts)


def coarse_correction(chunks, rows, cols, depth):
    nx, ny = lax.axis_size("gx"), lax.axis_size("gy")
    total_rows, total_cols = rows * nx, cols * ny
    count = total_rows * total_cols * depth
    got = lax.all_to_all(chunks, BOTH, 0, 0)
    out_rows, out_cols = 2 * rows + 2 * H, 2 * cols + 2 * H
    rows_ids = (np.arange(-H, 2 * total_rows + H) // 2) % total_rows
    cols_ids = (np.arange(-H, 2 * total_cols + H) // 2) % total_cols
    table_x = hartley(rows_ids, np.arange(total_rows), total_rows)
    table_y = hartley(cols_ids, np.arange(total_cols), total_cols)
    depth_in = hartley(np.arange(depth), np.arange(depth), depth)
    depth_out = np.repeat(depth_in, 2, axis=1)

    def own(table, axis, step, size):
        table = jnp.asarray(table, F32)
        return lax.dynamic_slice_in_dim(table, lax.axis_index(axis) * step, size, 0)

    cells = total_rows * total_cols
    if cells <= 512 and cells == 2 * depth:
        order = np.arange(cells).reshape(nx, rows, ny, cols).transpose(0, 2, 1, 3).reshape(-1)
        forward = np.einsum(
            "ax,by->abxy",
            hartley(np.arange(total_rows), np.arange(total_rows), total_rows),
            hartley(np.arange(total_cols), np.arange(total_cols), total_cols),
        ).reshape(cells, cells)[:, order]
        ones = np.ones((1, depth))
        eig_x = np.repeat(waves(total_rows), total_cols)[:, None] * ones
        eig_y = np.tile(waves(total_cols), total_rows)[:, None] * ones
        eig_z = np.ones((depth, 1)) * waves(depth)[None, :]
        parts = {
            "forward": forward,
            "eig": np.concatenate((eig_x, eig_y), axis=1),
            "depth": np.concatenate((depth_in, eig_z), axis=1),
            "depth_out": depth_out,
            "x": windows(np.repeat(table_x, total_cols, axis=1), nx, 2 * rows, out_rows),
            "y": windows(np.tile(table_y, (1, total_rows)), ny, 2 * cols, out_cols),
        }
        start, size = {}, 0
        for name, part in parts.items():
            start[name] = size
            size += part.shape[0]
            assert size % 8 == 0
        start["depth_in"] = start["depth"]
        table = jnp.asarray(np.concatenate(list(parts.values())), F32)
        return call(
            functools.partial(solve_kernel, count=count, start=start),
            [(out_rows, out_cols, 2 * depth)],
            got, table,
        )[0]

    hi = lax.Precision.HIGHEST
    averages = jnp.sum(got[:, rows * cols, :3], axis=0) / count
    full = got[:, : rows * cols].reshape(nx, ny, rows, cols, depth)
    full = full.transpose(0, 2, 1, 3, 4).reshape(total_rows, total_cols, depth)
    f32 = lambda x: jnp.asarray(x, F32)
    spec = jnp.einsum("abz,zk->abk", full, f32(depth_in), precision=hi)
    spec = jnp.einsum("ij,jbz->ibz", f32(hartley(np.arange(total_rows), np.arange(total_rows), total_rows)), spec, precision=hi)
    spec = jnp.einsum("ij,ajz->aiz", f32(hartley(np.arange(total_cols), np.arange(total_cols), total_cols)), spec, precision=hi)
    lam = (
        MASS
        + averages[0] * f32(waves(total_rows))[:, None, None]
        + averages[1] * f32(waves(total_cols))[None, :, None]
        + averages[2] * f32(waves(depth))[None, None, :]
    )
    spec = spec / (lam * float(count))
    out = jnp.einsum("ij,jbz->ibz", own(table_x, "gx", 2 * rows, out_rows), spec, precision=hi)
    out = jnp.einsum("ij,ajz->aiz", own(table_y, "gy", 2 * cols, out_cols), out, precision=hi)
    return jnp.einsum("abz,zk->abk", out, f32(depth_out), precision=hi)


def shards(source, face_coef):
    rows, cols, depth = source.shape
    rows1, cols1, depth1 = rows // 2, cols // 2, depth // 2
    er, ec, er1, ec1 = rows + 2 * H, cols + 2 * H, rows1 + 2 * H, cols1 + 2 * H

    nx_tiles = 4 * H * (cols // 8) + 3 * (H // 2)
    ny_tiles = 2 * rows + rows // 4 + (rows // 2 + 3) // 4
    corner_tiles = len(CORNER0) // 8 + 1
    to_right, to_left, to_up, to_down, w1, source, face_coef, pairs = call(
        pack_kernel,
        [(ny_tiles, 8, depth)] * 2
        + [(nx_tiles, 8, depth)] * 2
        + [(3, rows1, cols1, depth1), (rows, cols, depth)]
        + [jax.ShapeDtypeStruct((3, rows, cols, depth), BF16), jax.ShapeDtypeStruct((depth, depth1), BF16)],
        source, face_coef,
        remote=(0, 1),
        limit=K1LIMIT,
        scratch=[
            pltpu.VMEM((depth, depth1), BF16),
            (depth1 // 128, cols, 128),
            pltpu.SemaphoreType.DMA((2,)),
        ],
    )
    right, left = moved(to_right, 0, 1), moved(to_left, 0, -1)
    up, down = moved(to_up, 1, 0), moved(to_down, -1, 0)
    to_up, to_down = call(
        functools.partial(forward_kernel, rows=rows), [(2 * corner_tiles, 8, depth)] * 2, right, left
    )
    corners = moved(to_up, 1, 0), moved(to_down, -1, 0)
    state = call(
        assemble_kernel,
        [(7, er, ec, depth), (3, er1, ec1, depth1)],
        source, face_coef, w1, up, down, right, left,
    )
    merged = [(rows * (H // 2) // 8, 8, depth)] * 2
    kept, w1e, v0, right1, to_right, to_left, rdiag1, diag1, merged_right, merged_left = call(
        pre_kernel,
        [(5, er, ec, depth), (3, er1, ec1, depth1), (rows, cols, depth), (rows1, cols1, depth1)]
        + [(rows1 // 2, 8, depth1)] * 2
        + [(er1, ec1, depth1), (er1, ec1, depth1)]
        + merged,
        *corners, pairs, *state,
        scratch=[(rows1, ec, depth), (depth1 // 128, rows1 * ec, 128)] + [(er, ec, depth)] * 2,
    )

    right, left = moved(to_right, 0, 1), moved(to_left, 0, -1)
    rows_own, to_up, to_down = call(
        pack1_kernel, [(rows1, ec1, depth1)] + [(H, ec1, depth1)] * 2, right1, right, left, rdiag1, near=(kept,)
    )
    up, down = moved(to_up, 1, 0), moved(to_down, -1, 0)
    y_tiles = merged[0][0] + (rows1 + 3) // 4
    kept1, chunks, to_right, to_left = call(
        pre1_kernel,
        [(6, er1, ec1, depth1), (lax.axis_size(BOTH), rows1 * cols1 // 4 + 1, depth1 // 2)]
        + [(y_tiles, 8, depth)] * 2,
        rows_own, up, down, w1e, rdiag1, diag1, jnp.asarray(pair_table(depth1)), merged_right, merged_left,
        near=(kept,),
        scratch=[(rows1 // 2, ec1, depth1), (depth1 // 256, rows1 // 2 * ec1, 128)],
    )

    right, left = moved(to_right, 0, 1), moved(to_left, 0, -1)
    correction2 = coarse_correction(chunks, rows1 // 2, cols1 // 2, depth1 // 2)
    x_tiles = (H // 2) * (ec // 8 + ec1 // 8)
    v_rows, to_up, to_down = call(
        pack_v_kernel,
        [(rows + rows1 // 2, ec, depth)] + [(x_tiles, 8, depth)] * 2,
        kept1, right, left, v0,
        scratch=[(rows1, ec1, depth1)],
    )
    up, down = moved(to_up, 1, 0), moved(to_down, -1, 0)
    h = H // 2
    v1, to_right, to_left = call(
        post1_kernel,
        [(rows1, cols1, depth1)] + [(rows1 // 4, 8, depth1)] * 2,
        v_rows, up, down, correction2, kept1,
        scratch=[(er1, ec1, depth1)],
    )

    (v0e,) = call(spread_kernel, [(er, ec, depth)], v_rows, up, down)
    right1, left1 = moved(to_right, 0, 1), moved(to_left, 0, -1)
    wide1 = -(-(cols1 + 2 * h) // 8) * 8
    rows_own, to_up, to_down = call(
        pack2_kernel, [(rows1, wide1, depth1)] + [(h, wide1, depth1)] * 2, v1, right1, left1
    )
    up1, down1 = moved(to_up, 1, 0), moved(to_down, -1, 0)
    (out,) = call(
        post_kernel,
        [(rows, cols, depth)],
        v0e, rows_own, up1, down1, kept,
        jnp.asarray(np.ascontiguousarray(pair_table(depth).T)),
        scratch=[(er, ec, depth), (rows1 + 2 * h, wide1, depth1)],
    )
    return out


def solution(mesh):
    return jax.shard_map(
        shards,
        mesh=mesh,
        in_specs=(P("gx", "gy", None), P(None, "gx", "gy", None)),
        out_specs=P("gx", "gy", None),
        check_vma=False,
    )
```

```python
import functools
import math

import jax
import jax.numpy as jnp
import ml_dtypes
import numpy as np
from jax import lax
from jax.experimental import pallas as pl
from jax.experimental.pallas import tpu as pltpu
from jax.sharding import PartitionSpec as P

LEVELS = 3
SWEEPS = 2
MASS = 0.002
BOTH = ("gx", "gy")
H = 2 * SWEEPS
F32 = jnp.float32
UNROLL = 4
VMEM_LIMIT = 12 * 1024 * 1024
K1LIMIT = 12 * 1024 * 1024
BF16 = jnp.bfloat16
VMEM = pl.BlockSpec(memory_space=pltpu.VMEM)
HBM = pl.BlockSpec(memory_space=pltpu.HBM)

CORNER0 = (
    (0, 1, 1), (0, 1, 2), (0, 1, 3), (1, 2, 3), (3, 1, 1), (3, 1, 2), (3, 1, 3), (2, 2, 3),
    (1, 1, 1), (1, 1, 2), (1, 1, 3), (1, 1, 4), (2, 1, 1), (2, 1, 2), (2, 1, 3), (2, 1, 4),
    (0, 2, 1), (0, 2, 2), (0, 3, 1), (1, 4, 1), (3, 2, 1), (3, 2, 2), (3, 3, 1), (2, 4, 1),
    (1, 2, 1), (1, 2, 2), (1, 3, 1), (1, 3, 2), (2, 2, 1), (2, 2, 2), (2, 3, 1), (2, 3, 2),
)
CORNER1 = (
    (0, 1, 1), (0, 1, 2), (0, 1, 3), (0, 2, 1), (0, 2, 2), (0, 3, 1), (2, 1, 1), (2, 1, 2),
    (1, 1, 1), (1, 1, 2), (1, 1, 3), (1, 2, 1), (1, 2, 2), (1, 3, 1), (2, 2, 1), None,
)


def call(kernel, out, *args, scratch=(), remote=(), limit=VMEM_LIMIT, near=()):
    count = len(args)
    args = (*args, *near)

    def body(*refs):
        kernel(*refs[:count], *refs[len(args) :])

    return pl.pallas_call(
        body,
        out_shape=[s if hasattr(s, "dtype") else jax.ShapeDtypeStruct(s, F32) for s in out],
        in_specs=[HBM if i in remote else VMEM for i in range(len(args))],
        out_specs=[VMEM] * len(out),
        scratch_shapes=[pltpu.VMEM(s, F32) if isinstance(s, tuple) else s for s in scratch],
        compiler_params=pltpu.CompilerParams(vmem_limit_bytes=limit),
    )(*args)


def moved(block, dx, dy):
    nx, ny = lax.axis_size("gx"), lax.axis_size("gy")
    if dy == 0:
        return lax.ppermute(block, "gx", [(i, (i + dx) % nx) for i in range(nx)])
    if dx == 0:
        return lax.ppermute(block, "gy", [(j, (j + dy) % ny) for j in range(ny)])
    route = []
    for i in range(nx):
        for j in range(ny):
            route.append((i * ny + j, ((i + dx) % nx) * ny + (j + dy) % ny))
    return lax.ppermute(block, BOTH, route)


def split3(x):
    high = x.astype(BF16)
    rest = x - high.astype(F32)
    middle = rest.astype(BF16)
    return high, middle, (rest - middle.astype(F32)).astype(BF16)


def dot(a, b):
    return jnp.dot(a, b, preferred_element_type=F32)


def dot_exact(x, table):
    high, middle, low = split3(x)
    return dot(high, table) + (dot(middle, table) + dot(low, table))


def pair_table(depth):
    table = np.zeros((depth, depth // 2), ml_dtypes.bfloat16)
    table[np.arange(depth), np.arange(depth) // 2] = 1
    return table


def put_tiles(tiles, x):
    for k in range(tiles.shape[0]):
        tiles[k] = x[:, 128 * k : 128 * k + 128]


def every_other(tiles, start, size):
    return jnp.concatenate(
        [tiles[k, pl.ds(start, size, stride=2), :] for k in range(tiles.shape[0])], axis=1
    )


def back(x, axis):
    return pltpu.roll(x, 1, axis)


def ahead(x, axis):
    return pltpu.roll(x, x.shape[axis] - 1, axis)


def parity2(shape):
    return (lax.broadcasted_iota(jnp.int32, shape, 0) + lax.broadcasted_iota(jnp.int32, shape, 1)) & 1


def row_sum(r, v, wx, wy, wz):
    centre = v[r]
    y, z = wy[r], wz[r]
    total = wx[r] * v[r + 1] + wx[r - 1] * v[r - 1]
    total = total + y * ahead(centre, 0) + back(y * centre, 0)
    return centre, total + z * ahead(centre, 1) + back(z * centre, 1)


def half_sweep(first, last, colour, parity, v, b, wx, wy, wz, rdiag):
    unroll = UNROLL if v.shape[-1] > 256 else last - first

    def body(r, carry):
        centre, total = row_sum(r, v, wx, wy, wz)
        mine = parity == ((r + colour) & 1)
        v[r] = jnp.where(mine, (b[r] + total) * rdiag[r], centre)
        return carry

    lax.fori_loop(first, last, body, 0, unroll=unroll)


def pack_kernel(src_in, face_in, to_right, to_left, to_up, to_down, w1, src, face, pairs, *scratch):
    odds, tx, sem = scratch
    rows, cols, depth = src.shape
    half = depth // 2
    copies = [pltpu.make_async_copy(src_in, src, sem.at[0]), pltpu.make_async_copy(face_in, face, sem.at[1])]
    for copy in copies:
        copy.start()
    fine = lax.broadcasted_iota(jnp.int32, pairs.shape, 0)
    coarse = 2 * lax.broadcasted_iota(jnp.int32, pairs.shape, 1)
    pairs[...] = jnp.where((fine & -2) == coarse, 1.0, 0.0).astype(BF16)
    odds[...] = jnp.where(fine == coarse + 1, 1.0, 0.0).astype(BF16)
    for copy in copies:
        copy.wait()

    for i in range(rows // 2):
        put_tiles(tx, dot(face[0, 2 * i + 1], pairs[...]))
        w1[0, i] = 0.0625 * (every_other(tx, 0, cols // 2) + every_other(tx, 1, cols // 2))
        put_tiles(tx, dot(face[1, 2 * i], pairs[...]) + dot(face[1, 2 * i + 1], pairs[...]))
        w1[1, i] = 0.0625 * every_other(tx, 1, cols // 2)
        put_tiles(tx, dot(face[2, 2 * i], odds[...]) + dot(face[2, 2 * i + 1], odds[...]))
        w1[2, i] = 0.0625 * (every_other(tx, 0, cols // 2) + every_other(tx, 1, cols // 2))

    def plane(a, r):
        return src[r] if a == 0 else face[a - 1, r].astype(F32)

    for out, base, base1 in ((to_right, cols - H, cols // 2 - H), (to_left, 0, 0)):
        for r in range(rows):
            for t, pair in enumerate(((0, 3), (1, 2))):
                for s, a in enumerate(pair):
                    value = plane(a, r)
                    if out is to_right and a == 3:
                        value_all = value + back(value, 1) + back(plane(2, r), 0)
                        first = lax.broadcasted_iota(jnp.int32, value.shape, 0) == base
                        value = jnp.where(first, value_all, value)
                    out[2 * r + t, H * s : H * s + H] = value[base : base + H]
        for i in range(rows // 2):
            k, lane = 2 * rows + i // 2, half * (i % 2)
            out[k, 0:H, lane : lane + half] = w1[0, i, base1 : base1 + H]
            out[k, H : 2 * H, lane : lane + half] = w1[1, i, base1 : base1 + H]
            k = 2 * rows + rows // 4 + i // 4
            s = H * (i % 2)
            lane = half * ((i // 2) % 2)
            out[k, s : s + H, lane : lane + half] = w1[2, i, base1 : base1 + H]

    for out, base in ((to_up, rows - H), (to_down, 0)):
        for a in range(4):
            for k in range(H):
                value = plane(a, base + k)
                if out is to_up and a == 3 and k == 0:
                    value = value + back(value, 1) + plane(1, base - 1)
                for t in range(cols // 8):
                    out[(a * H + k) * (cols // 8) + t] = value[8 * t : 8 * t + 8]
        base1 = 4 * H * (cols // 8)
        for d in range(3):
            for i in range(H // 2):
                out[base1 + d * (H // 2) + i] = jnp.concatenate((w1[d, 2 * i], w1[d, 2 * i + 1]), axis=1)


def forward_kernel(right, left, to_up, to_down, *, rows):
    half = right.shape[2] // 2
    tiles = to_up.shape[0] // 2
    place = {0: (0, 0), 3: (0, 1), 1: (1, 0), 2: (1, 1)}
    for msg, sy in ((right, 1), (left, -1)):
        start = 0 if sy > 0 else tiles
        for out, sx in ((to_up, 1), (to_down, -1)):
            for n, (a, dx, dy) in enumerate(CORNER0):
                r = rows - dx if sx > 0 else dx - 1
                t, s = place[a]
                s = H * s + (H - dy if sy > 0 else dy - 1)
                out[start + n // 8, n % 8 : n % 8 + 1] = msg[2 * r + t, s : s + 1]
            for n, entry in enumerate(CORNER1):
                if entry is None:
                    continue
                d, dx, dy = entry
                i = rows // 2 - dx if sx > 0 else dx - 1
                c = H - dy if sy > 0 else dy - 1
                if d == 2:
                    k, s, lane = 2 * rows + rows // 4 + i // 4, H * (i % 2) + c, half * ((i // 2) % 2)
                else:
                    k, s, lane = 2 * rows + i // 2, H * d + c, half * (i % 2)
                to = half * (n // 8)
                out[start + tiles - 1, n % 8 : n % 8 + 1, to : to + half] = msg[k, s : s + 1, lane : lane + half]


def diagonal_row(r, parity, low_col, b, wx, wy, wz, diag, rdiag, v):
    y, z = wy[r], wz[r]
    if isinstance(r, int) and r == 0:
        total = MASS + wx[r] + z + y + back(y, 0)
    else:
        total = MASS + wx[r] + wx[r - 1] + y
        total = total + jnp.where(low_col, z, z + back(z, 1) + back(y, 0))
    diag[r] = total
    inverse = 1.0 / total
    rdiag[r] = inverse
    v[r] = jnp.where(parity == (r & 1), b[r] * inverse, 0.0)


def assemble_kernel(src, face, w1, up, down, right, left, state, w1e):
    b, wx, wy, wz, rdiag, diag, v = (state.at[i] for i in range(7))
    rows, cols, depth = src.shape
    half = depth // 2
    ext = (b, wx, wy, wz)
    er, ec = rows + 2 * H, cols + 2 * H
    rows1, cols1 = rows // 2, cols // 2

    for r in range(rows):
        b[H + r, H : H + cols] = src[r]
        for d in range(3):
            ext[1 + d][H + r, H : H + cols] = face[d, r].astype(F32)
    for d in range(3):
        for i in range(rows1):
            w1e[d, H + i, H : H + cols1] = w1[d, i]
    tiles = cols // 8
    for msg, base, base1 in ((up, 0, 0), (down, H + rows, H + rows1)):
        for a in range(4):
            for k in range(H):
                for t in range(tiles):
                    ext[a][base + k, H + 8 * t : H + 8 * t + 8] = msg[(a * H + k) * tiles + t]
        n = 4 * H * tiles
        for d in range(3):
            for i in range(H):
                lane = half * (i % 2)
                w1e[d, base1 + i, H : H + cols1] = msg[n + d * (H // 2) + i // 2, :, lane : lane + half]
    for msg, base, base1 in ((right, 0, 0), (left, H + cols, H + cols1)):
        for r in range(rows):
            for t, pair in enumerate(((0, 3), (1, 2))):
                for s, a in enumerate(pair):
                    ext[a][H + r, base : base + H] = msg[2 * r + t, H * s : H * s + H]
        for i in range(rows1):
            k, lane = 2 * rows + i // 2, half * (i % 2)
            w1e[0, H + i, base1 : base1 + H] = msg[k, 0:H, lane : lane + half]
            w1e[1, H + i, base1 : base1 + H] = msg[k, H : 2 * H, lane : lane + half]
            k = 2 * rows + rows // 4 + i // 4
            s = H * (i % 2)
            lane = half * ((i // 2) % 2)
            w1e[2, H + i, base1 : base1 + H] = msg[k, s : s + H, lane : lane + half]
    parity = parity2((ec, depth))
    low_col = lax.broadcasted_iota(jnp.int32, (ec, depth), 0) == 0

    def body(r, carry):
        diagonal_row(r, parity, low_col, b, wx, wy, wz, diag, rdiag, v)
        return carry

    lax.fori_loop(H + 1, H + rows, body, 0)


def pre_kernel(up, down, pairs, *rest):
    state, w1_in, kept, w1e = rest[:4]
    (v_own, right1, to_right, to_left, rdiag1, diag1, merged_right, merged_left) = rest[4:12]
    t512, t256, diag, v = rest[12:]
    b, wx, wy, wz, rdiag = (kept.at[i] for i in range(5))
    kept[...] = state[0:5]
    diag[...] = state[5]
    v[...] = state[6]
    w1e[...] = w1_in[...]
    ext = (b, wx, wy, wz)
    rows, cols, depth = v_own.shape
    half = depth // 2
    er, ec = rows + 2 * H, cols + 2 * H
    rows1, cols1 = rows // 2, cols // 2
    tiles = len(CORNER0) // 8 + 1
    for msg, sx, sy in ((up, 1, 1), (up, 1, -1), (down, -1, 1), (down, -1, -1)):
        start = 0 if sy > 0 else tiles

        def at(distance, size, sign):
            return H - distance if sign > 0 else H + size + distance - 1

        for n, (a, dx, dy) in enumerate(CORNER0):
            r, c = at(dx, rows, sx), at(dy, cols, sy)
            ext[a][r, c : c + 1] = msg[start + n // 8, n % 8 : n % 8 + 1]
        for n, entry in enumerate(CORNER1):
            if entry is None:
                continue
            d, dx, dy = entry
            r, c = at(dx, rows1, sx), at(dy, cols1, sy)
            lane = half * (n // 8)
            w1e[d, r, c : c + 1] = msg[start + tiles - 1, n % 8 : n % 8 + 1, lane : lane + half]

    parity = parity2((ec, depth))
    low_col = lax.broadcasted_iota(jnp.int32, (ec, depth), 0) == 0
    for r in (*range(H + 1), *range(H + rows, er)):
        diagonal_row(r, parity, low_col, b, wx, wy, wz, diag, rdiag, v)
    half_sweep(1, er - 1, 1, parity, v, b, wx, wy, wz, rdiag)
    half_sweep(2, er - 2, 0, parity, v, b, wx, wy, wz, rdiag)
    half_sweep(3, er - 3, 1, parity, v, b, wx, wy, wz, rdiag)

    def residual_body(i, carry):
        total = 0.0
        for k in range(2):
            r = H + 2 * i + k
            centre, around = row_sum(r, v, wx, wy, wz)
            total = total + (b[r] - (diag[r] * centre - around))
        t512[i] = total
        return carry

    lax.fori_loop(0, rows1, residual_body, 0, unroll=UNROLL)
    put_tiles(t256, dot_exact(t512[...].reshape(rows1 * ec, depth), pairs[...]))
    for i in range(rows1):
        start = i * ec + H
        right1[i] = 0.125 * (every_other(t256, start, cols1) + every_other(t256, start + 1, cols1))

    for r in range(rows1 + 2 * H):
        y, z = w1e[1, r], w1e[2, r]
        total = MASS + w1e[0, r] + w1e[0, max(r - 1, 0)] + y + back(y, 0) + z + back(z, 1)
        diag1[r] = total
        rdiag1[r] = 1.0 / total
    for i in range(rows1):
        value, inverse = right1[i], rdiag1[H + i, H : H + cols1]
        col = lax.broadcasted_iota(jnp.int32, value.shape, 0)
        place = (i // 2, slice(H * (i % 2), H * (i % 2) + H))
        to_right[place] = jnp.where(col == cols1 - H, value * inverse, value)[cols1 - H :]
        to_left[place] = jnp.where(col == H - 1, value * inverse, value)[:H]

    own_parity = parity2((cols, depth))
    for r in range(rows):
        value = v[H + r, H : H + cols]
        v_own[r] = value
        value = jnp.where(own_parity == ((r + 1) & 1), value, ahead(value, 0))
        for p in range(H // 2):
            n = p * rows + r
            for out, base in ((merged_right, cols - H), (merged_left, 0)):
                out[n // 8, n % 8 : n % 8 + 1] = value[base + 2 * p : base + 2 * p + 1]


def pack1_kernel(own, right, left, rdiag1, rows_own, to_up, to_down):
    rows, cols, depth = own.shape
    for i in range(rows):
        rows_own[i, H : H + cols] = own[i]
        rows_own[i, 0:H] = right[i // 2, H * (i % 2) : H * (i % 2) + H]
        rows_own[i, H + cols : 2 * H + cols] = left[i // 2, H * (i % 2) : H * (i % 2) + H]
    shape = rows_own.shape[1:]
    col = lax.broadcasted_iota(jnp.int32, shape, 0)
    col_distance = jnp.maximum(jnp.maximum(H - col, col - (H + cols - 1)), 0)
    for k in range(H):
        for out, i, distance in ((to_up, rows - H + k, H - k), (to_down, k, k + 1)):
            edge = col_distance + distance == H
            value = rows_own[i]
            out[k] = jnp.where(edge, value * rdiag1[H + i], value)


def sums_kernel(w1, out):
    _, rows, cols, depth = w1.shape
    lane = lax.broadcasted_iota(jnp.int32, out.shape, 1)
    row_odd = lax.broadcasted_iota(jnp.int32, (cols, depth), 0) & 1
    depth_odd = lax.broadcasted_iota(jnp.int32, (cols, depth), 1) & 1
    parts = [0.0, 0.0, 0.0]
    for i in range(rows):
        if i % 2 == 1:
            parts[0] = parts[0] + w1[0, i]
        parts[1] = parts[1] + jnp.where(row_odd == 1, w1[1, i], 0.0)
        parts[2] = parts[2] + jnp.where(depth_odd == 1, w1[2, i], 0.0)
    line = jnp.zeros(out.shape, F32)
    for d in range(3):
        line = jnp.where(lane == d, 0.0625 * jnp.sum(parts[d]), line)
    out[...] = line


def pre1_kernel(rows_own, up, down, w1e, rdiag1, merged_right, merged_left, *rest):
    kept, to_right, to_left = rest
    b1, v = kept.at[4], kept.at[5]
    kept[0:3] = w1e[...]
    kept[3] = rdiag1[...]
    rows, _, depth = rows_own.shape
    cols = rows_own.shape[1] - 2 * H
    er, ec = rows + 2 * H, cols + 2 * H
    half = depth // 2
    wx, wy, wz = w1e.at[0], w1e.at[1], w1e.at[2]
    b1[0:H] = up[...]
    b1[H : H + rows] = rows_own[...]
    b1[H + rows :] = down[...]
    parity = parity2((ec, depth))
    col = lax.broadcasted_iota(jnp.int32, (ec, depth), 0)
    col_distance = jnp.maximum(jnp.maximum(H - col, col - (H + cols - 1)), 0)
    for r in range(er):
        distance = max(H - r, r - (H + rows - 1), 0)
        first = jnp.where(col_distance + distance >= H, b1[r], b1[r] * rdiag1[r])
        v[r] = jnp.where(parity == (r & 1), first, 0.0)
    half_sweep(1, er - 1, 1, parity, v, b1, wx, wy, wz, rdiag1)
    half_sweep(2, er - 2, 0, parity, v, b1, wx, wy, wz, rdiag1)
    half_sweep(3, er - 3, 1, parity, v, b1, wx, wy, wz, rdiag1)
    for out, base, merged in ((to_right, cols - H, merged_right), (to_left, 0, merged_left)):
        n = merged.shape[0]
        out[0:n] = merged[...]
        for i in range(rows):
            s, lane = H * (i % 2), depth * ((i // 2) % 2)
            out[n + i // 4, s : s + H, lane : lane + depth] = v[H + i, H + base : 2 * H + base]


def residual1_kernel(kept1, diag1, pairs, sums, chunks, t256, t128):
    wx, wy, wz, _, b1, v = (kept1.at[i] for i in range(6))
    chunk = chunks.at[0]
    er, ec, depth = diag1.shape
    rows, cols, half = er - 2 * H, ec - 2 * H, depth // 2
    for i in range(rows // 2):
        total = 0.0
        for k in range(2):
            r = H + 2 * i + k
            centre, around = row_sum(r, v, wx, wy, wz)
            total = total + (b1[r] - (diag1[r] * centre - around))
        t256[i] = total
    n = rows // 2
    put_tiles(t128, dot_exact(t256[...].reshape(n * ec, depth), pairs[...]))
    for i in range(n):
        start = i * ec + H
        chunk[i * (cols // 2) : (i + 1) * (cols // 2)] = 0.125 * (
            every_other(t128, start, cols // 2) + every_other(t128, start + 1, cols // 2)
        )
    chunk[chunk.shape[0] - 1 :] = sums[0:1]
    for i in range(1, chunks.shape[0]):
        chunks[i] = chunk[...]


def pack_v_kernel(kept1, right, left, v0, rows_out, to_up, to_down, v1_rows):
    rows1, ec1, half = v1_rows.shape
    cols1 = ec1 - 2 * H
    rows, cols, depth = v0.shape
    v0_rows = rows_out.at[0:rows]
    n0 = rows * (H // 2) // 8
    for i in range(rows1):
        s, lane = H * (i % 2), half * ((i // 2) % 2)
        v1_rows[i] = kept1[5, H + i]
        v1_rows[i, 0:H] = right[n0 + i // 4, s : s + H, lane : lane + half]
        v1_rows[i, H + cols1 : 2 * H + cols1] = left[n0 + i // 4, s : s + H, lane : lane + half]
    for r in range(rows):
        v0_rows[r, H : H + cols] = v0[r]
        for msg, base in ((right, 0), (left, H + cols)):
            for p in range(H // 2):
                n = p * rows + r
                line = msg[n // 8, n % 8 : n % 8 + 1]
                v0_rows[r, base + 2 * p : base + 2 * p + 2] = jnp.broadcast_to(line, (2, depth))
    ec = v0_rows.shape[1]
    for i in range(rows1 // 2):
        rows_out[rows + i, 0:ec1] = jnp.concatenate((v1_rows[2 * i], v1_rows[2 * i + 1]), axis=1)
    parity = parity2((ec, depth))
    tiles, tiles1 = ec // 8, ec1 // 8
    for out, base, base1 in ((to_up, rows - H, rows1 - H), (to_down, 0, 0)):
        for k in range(H // 2):
            r = base + 2 * k
            value = jnp.where(parity == ((r + 1) & 1), v0_rows[r], v0_rows[r + 1])
            for t in range(tiles):
                out[k * tiles + t] = value[8 * t : 8 * t + 8]
            start = (H // 2) * tiles + k * tiles1
            value = jnp.concatenate((v1_rows[base1 + 2 * k], v1_rows[base1 + 2 * k + 1]), axis=1)
            for t in range(tiles1):
                out[start + t] = value[8 * t : 8 * t + 8]


def split2(x):
    high = x.astype(BF16)
    return high, (x - high.astype(F32)).astype(BF16)


def dot_split(a, b):
    return dot(a[0], b[0]) + (dot(a[0], b[1]) + dot(a[1], b[0]))


def solve_kernel(got, table, out, *, count, start):
    devices, lines, depth = got.shape
    own = lines - 1
    cells = devices * own
    rx, ry, _ = out.shape

    def part(name, size, lane=0, width=None):
        return table[start[name] : start[name] + size, lane : lane + (width or table.shape[1])]

    values = jnp.concatenate([got[d, 0:own] for d in range(devices)], axis=0)
    sums = got[0, own : own + 1]
    for d in range(1, devices):
        sums = sums + got[d, own : own + 1]
    sums = sums * (1.0 / count)
    lam = MASS + sums[0:1, 0:1] * part("eig", cells, 0, depth)
    lam = lam + sums[0:1, 1:2] * part("eig", cells, depth, depth)
    lam = lam + sums[0:1, 2:3] * part("depth", 1, depth, depth)
    spec = dot_split(split2(values), split2(part("depth_in", depth, 0, depth)))
    spec = dot_split(split2(part("forward", cells)), split2(spec))
    spec = spec / (lam * float(count))
    spec = dot_split(split2(spec), split2(part("depth_out", depth)))
    ix, iy = lax.axis_index("gx"), lax.axis_index("gy")
    x_step, y_step = -(-rx // 8) * 8, -(-ry // 8) * 8
    along_x = table[pl.ds(pl.multiple_of(start["x"] + ix * x_step, 8), x_step), :]
    along_y = table[pl.ds(pl.multiple_of(start["y"] + iy * y_step, 8), y_step), :][0:ry]
    back_table = jnp.concatenate([along_x[i : i + 1] * along_y for i in range(rx)], axis=0)
    out[...] = dot_split(split2(back_table), split2(spec)).reshape(out.shape)


def post1_kernel(v_rows, up, down, correction, kept1, out, to_right, to_left, v):
    rdiag1, b1 = kept1.at[3], kept1.at[4]
    rows, cols, depth = out.shape
    er, ec = rows + 2 * H, cols + 2 * H
    start = v_rows.shape[0] - rows // 2
    for i in range(rows // 2):
        value = v_rows[start + i, 0:ec]
        v[H + 2 * i] = value[:, :depth]
        v[H + 2 * i + 1] = value[:, depth:]
    tiles = ec // 8
    for msg, base in ((up, 0), (down, H + rows)):
        start = msg.shape[0] - (H // 2) * tiles
        for k in range(H // 2):
            for t in range(tiles):
                tile = msg[start + k * tiles + t]
                v[base + 2 * k, 8 * t : 8 * t + 8] = tile[:, :depth]
                v[base + 2 * k + 1, 8 * t : 8 * t + 8] = tile[:, depth:]
    for r in range(er):
        v[r] = v[r] + correction[r]
    parity = parity2((ec, depth))
    wx, wy, wz = kept1.at[0], kept1.at[1], kept1.at[2]
    half_sweep(1, er - 1, 0, parity, v, b1, wx, wy, wz, rdiag1)
    half_sweep(2, er - 2, 1, parity, v, b1, wx, wy, wz, rdiag1)
    half_sweep(3, er - 3, 0, parity, v, b1, wx, wy, wz, rdiag1)
    half_sweep(4, er - 4, 1, parity, v, b1, wx, wy, wz, rdiag1)
    for r in range(rows):
        out[r] = v[H + r, H : H + cols]
    h = H // 2
    for r in range(rows):
        s = h * (r % 4)
        to_right[r // 4, s : s + h] = out[r, cols - h : cols]
        to_left[r // 4, s : s + h] = out[r, 0:h]


def pack2_kernel(own, right, left, rows_own, to_up, to_down):
    rows, cols, depth = own.shape
    h = H // 2
    used = cols + 2 * h
    for r in range(rows):
        s = h * (r % 4)
        rows_own[r, h : h + cols] = own[r]
        rows_own[r, 0:h] = right[r // 4, s : s + h]
        rows_own[r, h + cols : used] = left[r // 4, s : s + h]
        if used < rows_own.shape[1]:
            rows_own[r, used:] = jnp.zeros((rows_own.shape[1] - used, depth), F32)
    to_up[...] = rows_own[rows - h :]
    to_down[...] = rows_own[0:h]


def spread_kernel(v0_rows, up, down, v):
    er, ec, _ = v.shape
    rows = er - 2 * H
    v[H : H + rows] = v0_rows[0:rows]
    tiles = ec // 8
    for msg, base in ((up, 0), (down, H + rows)):
        for k in range(H // 2):
            for t in range(tiles):
                tile = msg[k * tiles + t]
                v[base + 2 * k, 8 * t : 8 * t + 8] = tile
                v[base + 2 * k + 1, 8 * t : 8 * t + 8] = tile


def post_kernel(v_in, rows_own, up1, down1, kept, spread, out, v, t256):
    b, wx, wy, wz, rdiag = (kept.at[i] for i in range(5))
    rows, cols, depth = out.shape
    rows1, wide1, half = rows_own.shape
    er, ec = rows + 2 * H, cols + 2 * H
    h = H // 2
    ec1 = cols // 2 + 2 * h
    n1 = rows1 + 2 * h
    t256[0:h] = up1[...]
    t256[h : h + rows1] = rows_own[...]
    t256[h + rows1 :] = down1[...]
    wide = dot_exact(t256[...].reshape(n1 * t256.shape[1], half), spread[...])
    wide = wide.reshape(n1, t256.shape[1], depth)
    for n in range(n1):
        line = wide[n, 0:ec1]
        line = jnp.broadcast_to(line[:, None, :], (ec1, 2, depth)).reshape(2 * ec1, depth)
        v[2 * n] = v_in[2 * n] + line
        v[2 * n + 1] = v_in[2 * n + 1] + line
    parity = parity2((ec, depth))
    half_sweep(1, er - 1, 0, parity, v, b, wx, wy, wz, rdiag)
    half_sweep(2, er - 2, 1, parity, v, b, wx, wy, wz, rdiag)
    half_sweep(3, er - 3, 0, parity, v, b, wx, wy, wz, rdiag)
    half_sweep(4, er - 4, 1, parity, v, b, wx, wy, wz, rdiag)
    for r in range(rows):
        out[r] = v[H + r, H : H + cols]


def hartley(rows, columns, length):
    angle = (np.outer(rows, columns) % length) * (2.0 * math.pi / length)
    return np.cos(angle) + np.sin(angle)


def waves(length):
    return 2.0 * (1.0 - np.cos(np.arange(length) * (2.0 * math.pi / length)))


def windows(table, count, step, size):
    pad = -size % 8
    parts = [np.pad(table[i * step : i * step + size], ((0, pad), (0, 0))) for i in range(count)]
    return np.concatenate(parts)


def coarse_correction(chunks, rows, cols, depth):
    nx, ny = lax.axis_size("gx"), lax.axis_size("gy")
    total_rows, total_cols = rows * nx, cols * ny
    count = total_rows * total_cols * depth
    got = lax.all_to_all(chunks, BOTH, 0, 0)
    out_rows, out_cols = 2 * rows + 2 * H, 2 * cols + 2 * H
    rows_ids = (np.arange(-H, 2 * total_rows + H) // 2) % total_rows
    cols_ids = (np.arange(-H, 2 * total_cols + H) // 2) % total_cols
    table_x = hartley(rows_ids, np.arange(total_rows), total_rows)
    table_y = hartley(cols_ids, np.arange(total_cols), total_cols)
    depth_in = hartley(np.arange(depth), np.arange(depth), depth)
    depth_out = np.repeat(depth_in, 2, axis=1)

    def own(table, axis, step, size):
        table = jnp.asarray(table, F32)
        return lax.dynamic_slice_in_dim(table, lax.axis_index(axis) * step, size, 0)

    cells = total_rows * total_cols
    if cells <= 512 and cells == 2 * depth:
        order = np.arange(cells).reshape(nx, rows, ny, cols).transpose(0, 2, 1, 3).reshape(-1)
        forward = np.einsum(
            "ax,by->abxy",
            hartley(np.arange(total_rows), np.arange(total_rows), total_rows),
            hartley(np.arange(total_cols), np.arange(total_cols), total_cols),
        ).reshape(cells, cells)[:, order]
        ones = np.ones((1, depth))
        eig_x = np.repeat(waves(total_rows), total_cols)[:, None] * ones
        eig_y = np.tile(waves(total_cols), total_rows)[:, None] * ones
        eig_z = np.ones((depth, 1)) * waves(depth)[None, :]
        parts = {
            "forward": forward,
            "eig": np.concatenate((eig_x, eig_y), axis=1),
            "depth": np.concatenate((depth_in, eig_z), axis=1),
            "depth_out": depth_out,
            "x": windows(np.repeat(table_x, total_cols, axis=1), nx, 2 * rows, out_rows),
            "y": windows(np.tile(table_y, (1, total_rows)), ny, 2 * cols, out_cols),
        }
        start, size = {}, 0
        for name, part in parts.items():
            start[name] = size
            size += part.shape[0]
            assert size % 8 == 0
        start["depth_in"] = start["depth"]
        table = jnp.asarray(np.concatenate(list(parts.values())), F32)
        return call(
            functools.partial(solve_kernel, count=count, start=start),
            [(out_rows, out_cols, 2 * depth)],
            got, table,
        )[0]

    hi = lax.Precision.HIGHEST
    averages = jnp.sum(got[:, rows * cols, :3], axis=0) / count
    full = got[:, : rows * cols].reshape(nx, ny, rows, cols, depth)
    full = full.transpose(0, 2, 1, 3, 4).reshape(total_rows, total_cols, depth)
    f32 = lambda x: jnp.asarray(x, F32)
    spec = jnp.einsum("abz,zk->abk", full, f32(depth_in), precision=hi)
    spec = jnp.einsum("ij,jbz->ibz", f32(hartley(np.arange(total_rows), np.arange(total_rows), total_rows)), spec, precision=hi)
    spec = jnp.einsum("ij,ajz->aiz", f32(hartley(np.arange(total_cols), np.arange(total_cols), total_cols)), spec, precision=hi)
    lam = (
        MASS
        + averages[0] * f32(waves(total_rows))[:, None, None]
        + averages[1] * f32(waves(total_cols))[None, :, None]
        + averages[2] * f32(waves(depth))[None, None, :]
    )
    spec = spec / (lam * float(count))
    out = jnp.einsum("ij,jbz->ibz", own(table_x, "gx", 2 * rows, out_rows), spec, precision=hi)
    out = jnp.einsum("ij,ajz->aiz", own(table_y, "gy", 2 * cols, out_cols), out, precision=hi)
    return jnp.einsum("abz,zk->abk", out, f32(depth_out), precision=hi)


def shards(source, face_coef):
    rows, cols, depth = source.shape
    rows1, cols1, depth1 = rows // 2, cols // 2, depth // 2
    er, ec, er1, ec1 = rows + 2 * H, cols + 2 * H, rows1 + 2 * H, cols1 + 2 * H

    nx_tiles = 4 * H * (cols // 8) + 3 * (H // 2)
    ny_tiles = 2 * rows + rows // 4 + (rows // 2 + 3) // 4
    corner_tiles = len(CORNER0) // 8 + 1
    to_right, to_left, to_up, to_down, w1, source, face_coef, pairs = call(
        pack_kernel,
        [(ny_tiles, 8, depth)] * 2
        + [(nx_tiles, 8, depth)] * 2
        + [(3, rows1, cols1, depth1), (rows, cols, depth)]
        + [jax.ShapeDtypeStruct((3, rows, cols, depth), BF16), jax.ShapeDtypeStruct((depth, depth1), BF16)],
        source, face_coef,
        remote=(0, 1),
        limit=K1LIMIT,
        scratch=[
            pltpu.VMEM((depth, depth1), BF16),
            (depth1 // 128, cols, 128),
            pltpu.SemaphoreType.DMA((2,)),
        ],
    )
    right, left = moved(to_right, 0, 1), moved(to_left, 0, -1)
    up, down = moved(to_up, 1, 0), moved(to_down, -1, 0)
    to_up, to_down = call(
        functools.partial(forward_kernel, rows=rows), [(2 * corner_tiles, 8, depth)] * 2, right, left
    )
    corners = moved(to_up, 1, 0), moved(to_down, -1, 0)
    (sums,) = call(sums_kernel, [(8, depth1 // 2)], w1)
    state = call(
        assemble_kernel,
        [(7, er, ec, depth), (3, er1, ec1, depth1)],
        source, face_coef, w1, up, down, right, left,
    )
    merged = [(rows * (H // 2) // 8, 8, depth)] * 2
    kept, w1e, v0, right1, to_right, to_left, rdiag1, diag1, merged_right, merged_left = call(
        pre_kernel,
        [(5, er, ec, depth), (3, er1, ec1, depth1), (rows, cols, depth), (rows1, cols1, depth1)]
        + [(rows1 // 2, 8, depth1)] * 2
        + [(er1, ec1, depth1), (er1, ec1, depth1)]
        + merged,
        *corners, pairs, *state,
        scratch=[(rows1, ec, depth), (depth1 // 128, rows1 * ec, 128)] + [(er, ec, depth)] * 2,
    )

    right, left = moved(to_right, 0, 1), moved(to_left, 0, -1)
    rows_own, to_up, to_down = call(
        pack1_kernel, [(rows1, ec1, depth1)] + [(H, ec1, depth1)] * 2, right1, right, left, rdiag1, near=(kept,)
    )
    up, down = moved(to_up, 1, 0), moved(to_down, -1, 0)
    y_tiles = merged[0][0] + (rows1 + 3) // 4
    kept1, to_right, to_left = call(
        pre1_kernel,
        [(6, er1, ec1, depth1)] + [(y_tiles, 8, depth)] * 2,
        rows_own, up, down, w1e, rdiag1, merged_right, merged_left,
        near=(kept,),
    )
    right, left = moved(to_right, 0, 1), moved(to_left, 0, -1)
    (chunks,) = call(
        residual1_kernel,
        [(lax.axis_size(BOTH), rows1 * cols1 // 4 + 1, depth1 // 2)],
        kept1, diag1, jnp.asarray(pair_table(depth1)), sums,
        near=(right, left),
        scratch=[(rows1 // 2, ec1, depth1), (depth1 // 256, rows1 // 2 * ec1, 128)],
    )

    correction2 = coarse_correction(chunks, rows1 // 2, cols1 // 2, depth1 // 2)
    x_tiles = (H // 2) * (ec // 8 + ec1 // 8)
    v_rows, to_up, to_down = call(
        pack_v_kernel,
        [(rows + rows1 // 2, ec, depth)] + [(x_tiles, 8, depth)] * 2,
        kept1, right, left, v0,
        scratch=[(rows1, ec1, depth1)],
    )
    up, down = moved(to_up, 1, 0), moved(to_down, -1, 0)
    h = H // 2
    v1, to_right, to_left = call(
        post1_kernel,
        [(rows1, cols1, depth1)] + [(rows1 // 4, 8, depth1)] * 2,
        v_rows, up, down, correction2, kept1,
        scratch=[(er1, ec1, depth1)],
    )

    (v0e,) = call(spread_kernel, [(er, ec, depth)], v_rows, up, down)
    right1, left1 = moved(to_right, 0, 1), moved(to_left, 0, -1)
    wide1 = -(-(cols1 + 2 * h) // 8) * 8
    rows_own, to_up, to_down = call(
        pack2_kernel, [(rows1, wide1, depth1)] + [(h, wide1, depth1)] * 2, v1, right1, left1
    )
    up1, down1 = moved(to_up, 1, 0), moved(to_down, -1, 0)
    (out,) = call(
        post_kernel,
        [(rows, cols, depth)],
        v0e, rows_own, up1, down1, kept,
        jnp.asarray(np.ascontiguousarray(pair_table(depth).T)),
        scratch=[(er, ec, depth), (rows1 + 2 * h, wide1, depth1)],
    )
    return out


def solution(mesh):
    return jax.shard_map(
        shards,
        mesh=mesh,
        in_specs=(P("gx", "gy", None), P(None, "gx", "gy", None)),
        out_specs=P("gx", "gy", None),
        check_vma=False,
    )
```

```python
import functools
import math

import jax
import jax.numpy as jnp
import ml_dtypes
import numpy as np
from jax import lax
from jax.experimental import pallas as pl
from jax.experimental.pallas import tpu as pltpu
from jax.sharding import PartitionSpec as P

LEVELS = 3
SWEEPS = 2
MASS = 0.002
BOTH = ("gx", "gy")
H = 2 * SWEEPS
F32 = jnp.float32
UNROLL = 4
VMEM_LIMIT = 12 * 1024 * 1024
BF16 = jnp.bfloat16
VMEM = pl.BlockSpec(memory_space=pltpu.VMEM)
HBM = pl.BlockSpec(memory_space=pltpu.HBM)

CORNER0 = (
    (0, 1, 1), (0, 1, 2), (0, 1, 3), (1, 2, 3), (3, 1, 1), (3, 1, 2), (3, 1, 3), (2, 2, 3),
    (1, 1, 1), (1, 1, 2), (1, 1, 3), (1, 1, 4), (2, 1, 1), (2, 1, 2), (2, 1, 3), (2, 1, 4),
    (0, 2, 1), (0, 2, 2), (0, 3, 1), (1, 4, 1), (3, 2, 1), (3, 2, 2), (3, 3, 1), (2, 4, 1),
    (1, 2, 1), (1, 2, 2), (1, 3, 1), (1, 3, 2), (2, 2, 1), (2, 2, 2), (2, 3, 1), (2, 3, 2),
)

def call(kernel, out, *args, scratch=(), remote=(), limit=VMEM_LIMIT, near=()):
    count = len(args)
    args = (*args, *near)

    def body(*refs):
        kernel(*refs[:count], *refs[len(args) :])

    return pl.pallas_call(
        body,
        out_shape=[s if hasattr(s, "dtype") else jax.ShapeDtypeStruct(s, F32) for s in out],
        in_specs=[HBM if i in remote else VMEM for i in range(len(args))],
        out_specs=[VMEM] * len(out),
        scratch_shapes=[pltpu.VMEM(s, F32) if isinstance(s, tuple) else s for s in scratch],
        compiler_params=pltpu.CompilerParams(vmem_limit_bytes=limit),
    )(*args)


def moved(block, dx, dy):
    nx, ny = lax.axis_size("gx"), lax.axis_size("gy")
    if dy == 0:
        return lax.ppermute(block, "gx", [(i, (i + dx) % nx) for i in range(nx)])
    if dx == 0:
        return lax.ppermute(block, "gy", [(j, (j + dy) % ny) for j in range(ny)])
    route = []
    for i in range(nx):
        for j in range(ny):
            route.append((i * ny + j, ((i + dx) % nx) * ny + (j + dy) % ny))
    return lax.ppermute(block, BOTH, route)


def split3(x):
    high = x.astype(BF16)
    rest = x - high.astype(F32)
    middle = rest.astype(BF16)
    return high, middle, (rest - middle.astype(F32)).astype(BF16)


def dot(a, b):
    return jnp.dot(a, b, preferred_element_type=F32)


def dot_exact(x, table):
    high, middle, low = split3(x)
    return dot(high, table) + (dot(middle, table) + dot(low, table))


def pair_table(depth):
    table = np.zeros((depth, depth // 2), ml_dtypes.bfloat16)
    table[np.arange(depth), np.arange(depth) // 2] = 1
    return table


def put_tiles(tiles, x):
    for k in range(tiles.shape[0]):
        tiles[k] = x[:, 128 * k : 128 * k + 128]


def every_other(tiles, start, size):
    return jnp.concatenate(
        [tiles[k, pl.ds(start, size, stride=2), :] for k in range(tiles.shape[0])], axis=1
    )


def back(x, axis):
    return pltpu.roll(x, 1, axis)


def ahead(x, axis):
    return pltpu.roll(x, x.shape[axis] - 1, axis)


def parity2(shape):
    return (lax.broadcasted_iota(jnp.int32, shape, 0) + lax.broadcasted_iota(jnp.int32, shape, 1)) & 1


def row_sum(r, v, wx, wy, wz):
    centre = v[r]
    y, z = wy[r], wz[r]
    total = wx[r] * v[r + 1] + wx[r - 1] * v[r - 1]
    total = total + y * ahead(centre, 0) + back(y * centre, 0)
    return centre, total + z * ahead(centre, 1) + back(z * centre, 1)


def half_sweep(first, last, colour, parity, v, b, wx, wy, wz, rdiag):
    unroll = UNROLL if v.shape[-1] > 256 else last - first

    def body(r, carry):
        centre, total = row_sum(r, v, wx, wy, wz)
        mine = parity == ((r + colour) & 1)
        v[r] = jnp.where(mine, (b[r] + total) * rdiag[r], centre)
        return carry

    lax.fori_loop(first, last, body, 0, unroll=unroll)


def pack_kernel(src_in, face_in, to_right, to_left, to_up, to_down, w1, src, face, pairs, *scratch):
    odds, tx, sem = scratch
    rows, cols, depth = src.shape
    copies = [pltpu.make_async_copy(src_in, src, sem.at[0]), pltpu.make_async_copy(face_in, face, sem.at[1])]
    for copy in copies:
        copy.start()
    fine = lax.broadcasted_iota(jnp.int32, pairs.shape, 0)
    coarse = 2 * lax.broadcasted_iota(jnp.int32, pairs.shape, 1)
    pairs[...] = jnp.where((fine & -2) == coarse, 1.0, 0.0).astype(BF16)
    odds[...] = jnp.where(fine == coarse + 1, 1.0, 0.0).astype(BF16)
    for copy in copies:
        copy.wait()

    for i in range(rows // 2):
        put_tiles(tx, dot(face[0, 2 * i + 1], pairs[...]))
        w1[0, i] = 0.0625 * (every_other(tx, 0, cols // 2) + every_other(tx, 1, cols // 2))
        put_tiles(tx, dot(face[1, 2 * i], pairs[...]) + dot(face[1, 2 * i + 1], pairs[...]))
        w1[1, i] = 0.0625 * every_other(tx, 1, cols // 2)
        put_tiles(tx, dot(face[2, 2 * i], odds[...]) + dot(face[2, 2 * i + 1], odds[...]))
        w1[2, i] = 0.0625 * (every_other(tx, 0, cols // 2) + every_other(tx, 1, cols // 2))

    def plane(a, r):
        return src[r] if a == 0 else face[a - 1, r].astype(F32)

    for out, base in ((to_right, cols - H), (to_left, 0)):
        for r in range(rows):
            for t, pair in enumerate(((0, 3), (1, 2))):
                for s, a in enumerate(pair):
                    value = plane(a, r)
                    if out is to_right and a == 3:
                        value_all = value + back(value, 1) + back(plane(2, r), 0)
                        first = lax.broadcasted_iota(jnp.int32, value.shape, 0) == base
                        value = jnp.where(first, value_all, value)
                    out[2 * r + t, H * s : H * s + H] = value[base : base + H]

    tiles = cols // 8
    for out, base in ((to_up, rows - H), (to_down, 0)):
        for a in range(4):
            for k in range(H):
                value = plane(a, base + k)
                if out is to_up and a == 3 and k == 0:
                    value = value + back(value, 1) + plane(1, base - 1)
                for t in range(tiles):
                    out[(a * H + k) * tiles + t] = value[8 * t : 8 * t + 8]
    last = w1[0, rows // 2 - 1]
    to_up[4 * H * tiles] = jnp.concatenate((last, last), axis=1)


def forward_kernel(right, left, to_up, to_down, *, rows):
    tiles = to_up.shape[0] // 2
    place = {0: (0, 0), 3: (0, 1), 1: (1, 0), 2: (1, 1)}
    for msg, sy in ((right, 1), (left, -1)):
        start = 0 if sy > 0 else tiles
        for out, sx in ((to_up, 1), (to_down, -1)):
            for n, (a, dx, dy) in enumerate(CORNER0):
                r = rows - dx if sx > 0 else dx - 1
                t, s = place[a]
                s = H * s + (H - dy if sy > 0 else dy - 1)
                out[start + n // 8, n % 8 : n % 8 + 1] = msg[2 * r + t, s : s + 1]


def diagonal_row(r, parity, low_col, b, wx, wy, wz, diag, rdiag, v):
    y, z = wy[r], wz[r]
    if isinstance(r, int) and r == 0:
        total = MASS + wx[r] + z + y + back(y, 0)
    else:
        total = MASS + wx[r] + wx[r - 1] + y
        total = total + jnp.where(low_col, z, z + back(z, 1) + back(y, 0))
    diag[r] = total
    inverse = 1.0 / total
    rdiag[r] = inverse
    v[r] = jnp.where(parity == (r & 1), b[r] * inverse, 0.0)


def assemble_kernel(src, face, up, down, right, left, state):
    b, wx, wy, wz, rdiag, diag, v = (state.at[i] for i in range(7))
    rows, cols, depth = src.shape
    ext = (b, wx, wy, wz)
    ec = cols + 2 * H
    for r in range(rows):
        b[H + r, H : H + cols] = src[r]
        for d in range(3):
            ext[1 + d][H + r, H : H + cols] = face[d, r].astype(F32)
    tiles = cols // 8
    for msg, base in ((up, 0), (down, H + rows)):
        for a in range(4):
            for k in range(H):
                for t in range(tiles):
                    ext[a][base + k, H + 8 * t : H + 8 * t + 8] = msg[(a * H + k) * tiles + t]
    for msg, base in ((right, 0), (left, H + cols)):
        for r in range(rows):
            for t, pair in enumerate(((0, 3), (1, 2))):
                for s, a in enumerate(pair):
                    ext[a][H + r, base : base + H] = msg[2 * r + t, H * s : H * s + H]
    parity = parity2((ec, depth))
    low_col = lax.broadcasted_iota(jnp.int32, (ec, depth), 0) == 0

    def body(r, carry):
        diagonal_row(r, parity, low_col, b, wx, wy, wz, diag, rdiag, v)
        return carry

    lax.fori_loop(H + 1, H + rows, body, 0)


def pre_kernel(up, down, pairs, state, kept, v_own, right1, to_right, to_left, *scratch):
    t512, t256, diag, v = scratch
    b, wx, wy, wz, rdiag = (kept.at[i] for i in range(5))
    kept[...] = state[0:5]
    diag[...] = state[5]
    v[...] = state[6]
    ext = (b, wx, wy, wz)
    rows, cols, depth = v_own.shape
    er, ec = rows + 2 * H, cols + 2 * H
    rows1, cols1 = rows // 2, cols // 2
    tiles = len(CORNER0) // 8
    for msg, sx, sy in ((up, 1, 1), (up, 1, -1), (down, -1, 1), (down, -1, -1)):
        start = 0 if sy > 0 else tiles

        def at(distance, size, sign):
            return H - distance if sign > 0 else H + size + distance - 1

        for n, (a, dx, dy) in enumerate(CORNER0):
            r, c = at(dx, rows, sx), at(dy, cols, sy)
            ext[a][r, c : c + 1] = msg[start + n // 8, n % 8 : n % 8 + 1]
    parity = parity2((ec, depth))
    low_col = lax.broadcasted_iota(jnp.int32, (ec, depth), 0) == 0
    for r in (*range(H + 1), *range(H + rows, er)):
        diagonal_row(r, parity, low_col, b, wx, wy, wz, diag, rdiag, v)
    half_sweep(1, er - 1, 1, parity, v, b, wx, wy, wz, rdiag)
    half_sweep(2, er - 2, 0, parity, v, b, wx, wy, wz, rdiag)
    half_sweep(3, er - 3, 1, parity, v, b, wx, wy, wz, rdiag)

    def residual_body(i, carry):
        total = 0.0
        for k in range(2):
            r = H + 2 * i + k
            centre, around = row_sum(r, v, wx, wy, wz)
            total = total + (b[r] - (diag[r] * centre - around))
        t512[i] = total
        return carry

    lax.fori_loop(0, rows1, residual_body, 0, unroll=UNROLL)
    put_tiles(t256, dot_exact(t512[...].reshape(rows1 * ec, depth), pairs[...]))
    for i in range(rows1):
        start = i * ec + H
        right1[i] = 0.125 * (every_other(t256, start, cols1) + every_other(t256, start + 1, cols1))

    start = to_right.shape[0] - rows1 // 2
    for i in range(rows1 // 2):
        to_right[start + i] = jnp.concatenate((right1[2 * i], right1[2 * i + 1]), axis=1)
        to_left[start + i] = to_right[start + i]

    own_parity = parity2((cols, depth))
    for r in range(rows):
        value = v[H + r, H : H + cols]
        v_own[r] = value
        value = jnp.where(own_parity == ((r + 1) & 1), value, ahead(value, 0))
        for p in range(H // 2):
            n = p * rows + r
            for out, base in ((to_right, cols - H), (to_left, 0)):
                out[n // 8, n % 8 : n % 8 + 1] = value[base + 2 * p : base + 2 * p + 1]


def pack_v_kernel(v0, right, left, v0_rows, to_up, to_down):
    rows, cols, depth = v0.shape
    for r in range(rows):
        v0_rows[r, H : H + cols] = v0[r]
        for msg, base in ((right, 0), (left, H + cols)):
            for p in range(H // 2):
                n = p * rows + r
                line = msg[n // 8, n % 8 : n % 8 + 1]
                v0_rows[r, base + 2 * p : base + 2 * p + 2] = jnp.broadcast_to(line, (2, depth))
    ec = v0_rows.shape[1]
    parity = parity2((ec, depth))
    for out, base in ((to_up, rows - H), (to_down, 0)):
        for k in range(H // 2):
            r = base + 2 * k
            out[k] = jnp.where(parity == ((r + 1) & 1), v0_rows[r], v0_rows[r + 1])


def gather1_kernel(w1, up, out):
    rows, cols, depth = w1.shape[1:]
    for d in range(3):
        for i in range(rows):
            out[d * rows + i] = w1[d, i]
    out[3 * rows] = up[up.shape[0] - 1, :, :depth]


def couplings1_kernel(*refs):
    *blocks, w, rdiag, to_up, to_down, sums = refs
    planes, cols, depth = blocks[0].shape
    rows = planes // 3
    wide = cols * len(blocks)

    def plane(n):
        return jnp.concatenate([block[n] for block in blocks], axis=0)

    before = plane(3 * rows)
    for i in range(rows):
        x, y, z = plane(i), plane(rows + i), plane(2 * rows + i)
        w[0, i], w[1, i], w[2, i] = x, y, z
        rdiag[i] = 1.0 / (MASS + x + before + y + back(y, 0) + z + back(z, 1))
        before = x
    for d in range(3):
        for k in range(H - 1):
            to_up[d * (H - 1) + k] = w[d, rows - H + 1 + k]
            to_down[d * (H - 1) + k] = w[d, k]
    to_up[3 * (H - 1)] = w[0, rows - H]
    lane = lax.broadcasted_iota(jnp.int32, sums.shape, 1)
    row_odd = lax.broadcasted_iota(jnp.int32, (wide, depth), 0) & 1
    depth_odd = lax.broadcasted_iota(jnp.int32, (wide, depth), 1) & 1
    parts = [0.0, 0.0, 0.0]
    for i in range(rows):
        if i % 2 == 1:
            parts[0] = parts[0] + w[0, i]
        parts[1] = parts[1] + jnp.where(row_odd == 1, w[1, i], 0.0)
        parts[2] = parts[2] + jnp.where(depth_odd == 1, w[2, i], 0.0)
    line = jnp.zeros(sums.shape, F32)
    for d in range(3):
        line = jnp.where(lane == d, 0.0625 * jnp.sum(parts[d]), line)
    sums[...] = line


def pack1_kernel(right, left, own1, *refs):
    *between, rdiag, own, to_up, to_down = refs
    rows, cols, depth = own1.shape
    start = right.shape[0] - rows // 2
    for i in range(rows):
        lane = depth * (i % 2)
        parts = [own1[i], left[start + i // 2, :, lane : lane + depth]]
        parts += [block[i] for block in between]
        own[i] = jnp.concatenate(parts + [right[start + i // 2, :, lane : lane + depth]], axis=0)
    for k in range(H):
        value = own[rows - H + k]
        to_up[k] = value * rdiag[rows - H] if k == 0 else value
        value = own[k]
        to_down[k] = value * rdiag[k] if k == H - 1 else value


def pre1_kernel(own, up, down, w, w_up, w_down, v0_up, v0_down, kept, to_up, to_down):
    rows, wide, depth = own.shape
    er = rows + 2 * H
    wx, wy, wz, rdiag, b, v, diag = (kept.at[i] for i in range(7))
    b[0:H] = up[...]
    b[H : H + rows] = own[...]
    b[H + rows :] = down[...]
    for d in range(3):
        kept[d, H : H + rows] = w[d]
        kept[d, 1:H] = w_up[d * (H - 1) : (d + 1) * (H - 1)]
        kept[d, H + rows : er - 1] = w_down[d * (H - 1) : (d + 1) * (H - 1)]
    wx[0] = w_up[3 * (H - 1)]
    parity = parity2((wide, depth))
    for r in range(er):
        if 0 < r < er - 1:
            y, z = wy[r], wz[r]
            total = MASS + wx[r] + wx[r - 1] + y + back(y, 0) + z + back(z, 1)
            diag[r] = total
            inverse = 1.0 / total
            rdiag[r] = inverse
            first = b[r] * inverse
        else:
            first = b[r]
        v[r] = jnp.where(parity == (r & 1), first, 0.0)
    half_sweep(1, er - 1, 1, parity, v, b, wx, wy, wz, rdiag)
    half_sweep(2, er - 2, 0, parity, v, b, wx, wy, wz, rdiag)
    half_sweep(3, er - 3, 1, parity, v, b, wx, wy, wz, rdiag)
    for out, base, v0 in ((to_up, rows, v0_up), (to_down, H, v0_down)):
        n = 0
        for k in range(H // 2):
            value = jnp.concatenate((v[base + 2 * k], v[base + 2 * k + 1]), axis=1)
            for t in range(wide // 8):
                out[n] = value[8 * t : 8 * t + 8]
                n += 1
        for k in range(H // 2):
            for t in range(v0.shape[1] // 8):
                out[n] = v0[k, 8 * t : 8 * t + 8]
                n += 1


def residual1_kernel(kept1, pairs, sums, chunks, t256, t128):
    wx, wy, wz, _, b, v, diag = (kept1.at[i] for i in range(7))
    _, er, wide, depth = kept1.shape
    rows = er - 2 * H
    chunk = chunks.at[0]
    for i in range(rows // 2):
        total = 0.0
        for k in range(2):
            r = H + 2 * i + k
            centre, around = row_sum(r, v, wx, wy, wz)
            total = total + (b[r] - (diag[r] * centre - around))
        t256[i] = total
    n = rows // 2
    put_tiles(t128, dot_exact(t256[...].reshape(n * wide, depth), pairs[...]))
    half = wide // 2
    for i in range(n):
        start = i * wide
        chunk[i * half : (i + 1) * half] = 0.125 * (every_other(t128, start, half) + every_other(t128, start + 1, half))
    chunk[n * half : n * half + 1] = sums[0:1]
    for i in range(1, chunks.shape[0]):
        chunks[i] = chunk[...]


def split2(x):
    high = x.astype(BF16)
    return high, (x - high.astype(F32)).astype(BF16)


def dot_split(a, b):
    return dot(a[0], b[0]) + (dot(a[0], b[1]) + dot(a[1], b[0]))


def solve_kernel(got, table, out, *, count, start):
    devices, lines, depth = got.shape
    own = lines - 1
    cells = devices * own
    rx, ry, _ = out.shape

    def part(name, size, lane=0, width=None):
        return table[start[name] : start[name] + size, lane : lane + (width or table.shape[1])]

    values = jnp.concatenate([got[d, 0:own] for d in range(devices)], axis=0)
    sums = got[0, own : own + 1]
    for d in range(1, devices):
        sums = sums + got[d, own : own + 1]
    sums = sums * (1.0 / count)
    lam = MASS + sums[0:1, 0:1] * part("eig", cells, 0, depth)
    lam = lam + sums[0:1, 1:2] * part("eig", cells, depth, depth)
    lam = lam + sums[0:1, 2:3] * part("depth", 1, depth, depth)
    spec = dot_split(split2(values), split2(part("depth", depth, 0, depth)))
    spec = dot_split(split2(part("forward", cells)), split2(spec))
    spec = spec / (lam * float(count))
    spec = dot_split(split2(spec), split2(part("depth_out", depth)))
    step = -(-rx // 8) * 8
    along_x = table[pl.ds(pl.multiple_of(start["x"] + lax.axis_index("gx") * step, 8), step), :]
    along_y = part("y", ry)
    back_table = jnp.concatenate([along_x[i : i + 1] * along_y for i in range(rx)], axis=0)
    out[...] = dot_split(split2(back_table), split2(spec)).reshape(out.shape)


def post1_kernel(kept1, up, down, correction, own, to_up, to_down, v, *, cols):
    wx, wy, wz, rdiag, b, before, _ = (kept1.at[i] for i in range(7))
    er, wide, depth = before.shape
    rows = er - 2 * H
    for r in range(rows):
        v[H + r] = before[H + r] + correction[H + r]
    for msg, base in ((up, 0), (down, H + rows)):
        for k in range(H // 2):
            n = k * (wide // 8)
            value = jnp.concatenate([msg[n + t] for t in range(wide // 8)], axis=0)
            v[base + 2 * k] = value[:, :depth] + correction[base + 2 * k]
            v[base + 2 * k + 1] = value[:, depth:] + correction[base + 2 * k + 1]
    parity = parity2((wide, depth))
    half_sweep(1, er - 1, 0, parity, v, b, wx, wy, wz, rdiag)
    half_sweep(2, er - 2, 1, parity, v, b, wx, wy, wz, rdiag)
    half_sweep(3, er - 3, 0, parity, v, b, wx, wy, wz, rdiag)
    half_sweep(4, er - 4, 1, parity, v, b, wx, wy, wz, rdiag)
    h = H // 2
    used = cols + 2 * h
    for r in range(rows):
        value = v[H + r]
        own[r, 0:h] = value[wide - h :]
        own[r, h:used] = value[0 : cols + h]
        if used < own.shape[1]:
            own[r, used:] = jnp.zeros((own.shape[1] - used, depth), F32)
    to_up[...] = own[rows - h :]
    to_down[...] = own[0:h]


def spread_kernel(v0_rows, up, down, v):
    er, ec, _ = v.shape
    rows = er - 2 * H
    v[H : H + rows] = v0_rows[...]
    tiles = ec // 8
    for msg, base in ((up, 0), (down, H + rows)):
        start = msg.shape[0] - (H // 2) * tiles
        for k in range(H // 2):
            for t in range(tiles):
                tile = msg[start + k * tiles + t]
                v[base + 2 * k, 8 * t : 8 * t + 8] = tile
                v[base + 2 * k + 1, 8 * t : 8 * t + 8] = tile


def post_kernel(v_in, rows_own, up1, down1, kept, spread, out, v, t256):
    b, wx, wy, wz, rdiag = (kept.at[i] for i in range(5))
    rows, cols, depth = out.shape
    rows1, wide1, half = rows_own.shape
    er, ec = rows + 2 * H, cols + 2 * H
    h = H // 2
    ec1 = cols // 2 + 2 * h
    n1 = rows1 + 2 * h
    t256[0:h] = up1[...]
    t256[h : h + rows1] = rows_own[...]
    t256[h + rows1 :] = down1[...]
    wide = dot_exact(t256[...].reshape(n1 * t256.shape[1], half), spread[...])
    wide = wide.reshape(n1, t256.shape[1], depth)
    for n in range(n1):
        line = wide[n, 0:ec1]
        line = jnp.broadcast_to(line[:, None, :], (ec1, 2, depth)).reshape(2 * ec1, depth)
        v[2 * n] = v_in[2 * n] + line
        v[2 * n + 1] = v_in[2 * n + 1] + line
    parity = parity2((ec, depth))
    half_sweep(1, er - 1, 0, parity, v, b, wx, wy, wz, rdiag)
    half_sweep(2, er - 2, 1, parity, v, b, wx, wy, wz, rdiag)
    half_sweep(3, er - 3, 0, parity, v, b, wx, wy, wz, rdiag)
    half_sweep(4, er - 4, 1, parity, v, b, wx, wy, wz, rdiag)
    for r in range(rows):
        out[r] = v[H + r, H : H + cols]


def hartley(rows, columns, length):
    angle = (np.outer(rows, columns) % length) * (2.0 * math.pi / length)
    return np.cos(angle) + np.sin(angle)


def waves(length):
    return 2.0 * (1.0 - np.cos(np.arange(length) * (2.0 * math.pi / length)))


def windows(table, count, step, size):
    pad = -size % 8
    parts = [np.pad(table[i * step : i * step + size], ((0, pad), (0, 0))) for i in range(count)]
    return np.concatenate(parts)


def coarse_correction(chunks, rows, cols, depth):
    nx = lax.axis_size("gx")
    total_rows = rows * nx
    count = total_rows * cols * depth
    got = lax.all_to_all(chunks, "gx", 0, 0)
    out_rows = 2 * rows + 2 * H
    rows_ids = (np.arange(-H, 2 * total_rows + H) // 2) % total_rows
    table_x = hartley(rows_ids, np.arange(total_rows), total_rows)
    table_y = hartley(np.arange(2 * cols) // 2, np.arange(cols), cols)
    forward_x = hartley(np.arange(total_rows), np.arange(total_rows), total_rows)
    forward_y = hartley(np.arange(cols), np.arange(cols), cols)
    depth_in = hartley(np.arange(depth), np.arange(depth), depth)
    depth_out = np.repeat(depth_in, 2, axis=1)
    cells = total_rows * cols
    if cells <= 512 and cells == 2 * depth:
        ones = np.ones((1, depth))
        eig_x = np.repeat(waves(total_rows), cols)[:, None] * ones
        eig_y = np.tile(waves(cols), total_rows)[:, None] * ones
        eig_z = np.ones((depth, 1)) * waves(depth)[None, :]
        parts = {
            "forward": np.kron(forward_x, forward_y),
            "eig": np.concatenate((eig_x, eig_y), axis=1),
            "depth": np.concatenate((depth_in, eig_z), axis=1),
            "depth_out": depth_out,
            "x": windows(np.repeat(table_x, cols, axis=1), nx, 2 * rows, out_rows),
            "y": np.tile(table_y, (1, total_rows)),
        }
        start, size = {}, 0
        for name, part in parts.items():
            start[name] = size
            size += part.shape[0]
            assert size % 8 == 0
        table = jnp.asarray(np.concatenate(list(parts.values())), F32)
        return call(
            functools.partial(solve_kernel, count=count, start=start),
            [(out_rows, 2 * cols, 2 * depth)],
            got, table,
        )[0]

    hi = lax.Precision.HIGHEST
    f32 = lambda x: jnp.asarray(x, F32)
    averages = jnp.sum(got[:, rows * cols, :3], axis=0) / count
    full = got[:, : rows * cols].reshape(total_rows, cols, depth)
    spec = jnp.einsum("abz,zk->abk", full, f32(depth_in), precision=hi)
    spec = jnp.einsum("ij,jbz->ibz", f32(forward_x), spec, precision=hi)
    spec = jnp.einsum("ij,ajz->aiz", f32(forward_y), spec, precision=hi)
    lam = (
        MASS
        + averages[0] * f32(waves(total_rows))[:, None, None]
        + averages[1] * f32(waves(cols))[None, :, None]
        + averages[2] * f32(waves(depth))[None, None, :]
    )
    spec = spec / (lam * float(count))
    own_x = lax.dynamic_slice_in_dim(f32(table_x), lax.axis_index("gx") * 2 * rows, out_rows, 0)
    out = jnp.einsum("ij,jbz->ibz", own_x, spec, precision=hi)
    out = jnp.einsum("ij,ajz->aiz", f32(table_y), out, precision=hi)
    return jnp.einsum("abz,zk->abk", out, f32(depth_out), precision=hi)


def gathered(block):
    return [block] + [moved(block, 0, -k) for k in range(1, lax.axis_size("gy"))]


def shards(source, face_coef):
    rows, cols, depth = source.shape
    rows1, cols1, depth1 = rows // 2, cols // 2, depth // 2
    er, ec, er1 = rows + 2 * H, cols + 2 * H, rows1 + 2 * H
    wide = cols1 * lax.axis_size("gy")
    h = H // 2
    limit = VMEM_LIMIT if wide * depth1 <= 8192 else 5 * VMEM_LIMIT

    x_tiles = 4 * H * (cols // 8) + 1
    corner_tiles = len(CORNER0) // 8
    to_right, to_left, to_up, to_down, w1, source, face_coef, pairs = call(
        pack_kernel,
        [(2 * rows, 8, depth)] * 2
        + [(x_tiles, 8, depth)] * 2
        + [(3, rows1, cols1, depth1), (rows, cols, depth)]
        + [jax.ShapeDtypeStruct((3, rows, cols, depth), BF16), jax.ShapeDtypeStruct((depth, depth1), BF16)],
        source, face_coef,
        remote=(0, 1),
        scratch=[
            pltpu.VMEM((depth, depth1), BF16),
            (depth1 // 128, cols, 128),
            pltpu.SemaphoreType.DMA((2,)),
        ],
    )
    right, left = moved(to_right, 0, 1), moved(to_left, 0, -1)
    up, down = moved(to_up, 1, 0), moved(to_down, -1, 0)
    to_up, to_down = call(
        functools.partial(forward_kernel, rows=rows), [(2 * corner_tiles, 8, depth)] * 2, right, left
    )
    corners = moved(to_up, 1, 0), moved(to_down, -1, 0)
    (block,) = call(gather1_kernel, [(3 * rows1 + 1, cols1, depth1)], w1, up, near=(to_up,))
    blocks = gathered(block)
    (state,) = call(assemble_kernel, [(7, er, ec, depth)], source, face_coef, up, down, right, left)
    kept, v0, right1, to_right, to_left = call(
        pre_kernel,
        [(5, er, ec, depth), (rows, cols, depth), (rows1, cols1, depth1)]
        + [(rows * h // 8 + rows1 // 2, 8, depth)] * 2,
        *corners, pairs, state,
        scratch=[(rows1, ec, depth), (depth1 // 128, rows1 * ec, 128)] + [(er, ec, depth)] * 2,
    )

    count = lax.axis_size("gy")
    left = moved(to_left, 0, -1)
    between = [moved(right1, 0, -k) for k in range(2, count - 1)]
    right = moved(to_right, 0, 1)
    w_own, rdiag_own, to_up, to_down, sums = call(
        couplings1_kernel,
        [(3, rows1, wide, depth1), (rows1, wide, depth1), (3 * H - 2, wide, depth1), (3 * H - 3, wide, depth1)]
        + [(8, depth1 // 2)],
        *blocks,
        near=(right1,), limit=limit,
    )
    w_up, w_down = moved(to_up, 1, 0), moved(to_down, -1, 0)
    own, to_up, to_down = call(
        pack1_kernel,
        [(rows1, wide, depth1)] + [(H, wide, depth1)] * 2,
        right, left, right1, *between, rdiag_own,
        near=(kept,), limit=limit,
    )
    up, down = moved(to_up, 1, 0), moved(to_down, -1, 0)
    v0_rows, v0_up, v0_down = call(pack_v_kernel, [(rows, ec, depth)] + [(h, ec, depth)] * 2, v0, right, left)
    tiles = h * (wide // 8 + ec // 8)
    kept1, to_up, to_down = call(
        pre1_kernel,
        [(7, er1, wide, depth1)] + [(tiles, 8, depth)] * 2,
        own, up, down, w_own, w_up, w_down, v0_up, v0_down,
        near=(kept,), limit=limit,
    )
    up, down = moved(to_up, 1, 0), moved(to_down, -1, 0)
    (chunks,) = call(
        residual1_kernel,
        [(lax.axis_size("gx"), rows1 * wide // 4 + 1, depth1 // 2)],
        kept1, jnp.asarray(pair_table(depth1)), sums,
        scratch=[(rows1 // 2, wide, depth1), (depth1 // 256, rows1 // 2 * wide, 128)],
        limit=limit,
    )
    correction2 = coarse_correction(chunks, rows1 // 2, wide // 2, depth1 // 2)
    used = -(-(cols1 + 2 * h) // 8) * 8
    own, to_up, to_down = call(
        functools.partial(post1_kernel, cols=cols1),
        [(rows1, used, depth1)] + [(h, used, depth1)] * 2,
        kept1, up, down, correction2,
        scratch=[(er1, wide, depth1)],
        limit=limit,
    )

    (v0e,) = call(spread_kernel, [(er, ec, depth)], v0_rows, up, down)
    up1, down1 = moved(to_up, 1, 0), moved(to_down, -1, 0)
    (out,) = call(
        post_kernel,
        [(rows, cols, depth)],
        v0e, own, up1, down1, kept,
        jnp.asarray(np.ascontiguousarray(pair_table(depth).T)),
        scratch=[(er, ec, depth), (rows1 + 2 * h, used, depth1)],
    )
    return out


def solution(mesh):
    return jax.shard_map(
        shards,
        mesh=mesh,
        in_specs=(P("gx", "gy", None), P(None, "gx", "gy", None)),
        out_specs=P("gx", "gy", None),
        check_vma=False,
    )
```

```python
import functools
import math

import jax
import jax.numpy as jnp
import ml_dtypes
import numpy as np
from jax import lax
from jax.experimental import pallas as pl
from jax.experimental.pallas import tpu as pltpu
from jax.sharding import PartitionSpec as P

LEVELS = 3
SWEEPS = 2
MASS = 0.002
BOTH = ("gx", "gy")
H = 2 * SWEEPS
F32 = jnp.float32
UNROLL = 4
VMEM_LIMIT = 12 * 1024 * 1024
BF16 = jnp.bfloat16
VMEM = pl.BlockSpec(memory_space=pltpu.VMEM)
HBM = pl.BlockSpec(memory_space=pltpu.HBM)

CORNER0 = (
    (0, 1, 1), (0, 1, 2), (0, 1, 3), (1, 2, 3), (3, 1, 1), (3, 1, 2), (3, 1, 3), (2, 2, 3),
    (1, 1, 1), (1, 1, 2), (1, 1, 3), (1, 1, 4), (2, 1, 1), (2, 1, 2), (2, 1, 3), (2, 1, 4),
    (0, 2, 1), (0, 2, 2), (0, 3, 1), (1, 4, 1), (3, 2, 1), (3, 2, 2), (3, 3, 1), (2, 4, 1),
    (1, 2, 1), (1, 2, 2), (1, 3, 1), (1, 3, 2), (2, 2, 1), (2, 2, 2), (2, 3, 1), (2, 3, 2),
)

def moved(block, axis, distance):
    count = lax.axis_size(axis)
    return lax.ppermute(block, axis, [(i, (i + distance) % count) for i in range(count)])


class Beside:
    def __init__(self, axis, shape, outer=None, inner=None):
        self.axis, self.shape, self.outer, self.inner = axis, shape, outer, inner

    def exchanged(self):
        count = lax.axis_size(self.axis)
        assert count % 2 == 0
        got = []
        for block, first in ((self.outer, 1), (self.inner, 0)):
            route = []
            for i in range(first, count + first, 2):
                a, b = i % count, (i + 1) % count
                route += [(a, b), (b, a)]
            got.append(lax.ppermute(block, self.axis, route))
        return Beside(self.axis, self.shape, *got)


def call(kernel, out, *args, scratch=(), remote=(), limit=VMEM_LIMIT, near=()):
    flat, pairs_in, pairs_out, shapes = [], [], [], []
    for i, arg in enumerate(args):
        if isinstance(arg, Beside):
            pairs_in.append((len(flat), arg))
            flat += [arg.outer, arg.inner]
        else:
            flat.append(arg)
    for item in out:
        if isinstance(item, Beside):
            pairs_out.append((len(shapes), item))
            shapes += [item.shape] * 2
        else:
            shapes.append(item)
    count = len(flat)
    for item in near:
        flat += [item.outer, item.inner] if isinstance(item, Beside) else [item]
    total = len(flat)
    own = [pltpu.VMEM(p.shape, F32) for _, p in pairs_in + pairs_out for _ in range(2)]

    def body(*refs):
        refs_in, refs_out = list(refs[:count]), list(refs[total : total + len(shapes)])
        rest = list(refs[total + len(shapes) :])
        held, rest = rest[: len(own)], rest[len(own) :]
        sends = []
        for n, (i, pair) in enumerate(pairs_in + pairs_out):
            forward, backward = held[2 * n], held[2 * n + 1]
            is_in = n < len(pairs_in)
            refs_here = refs_in if is_in else refs_out
            outer, inner = refs_here[i], refs_here[i + 1]
            refs_here[i], refs_here[i + 1] = forward, backward
            if is_in:
                odd = lax.axis_index(pair.axis) & 1

                @pl.when(odd == 0)
                def _():
                    forward[...] = outer[...]
                    backward[...] = inner[...]

                @pl.when(odd == 1)
                def _():
                    forward[...] = inner[...]
                    backward[...] = outer[...]

            else:
                sends.append((pair.axis, outer, inner, forward, backward))
        kernel(*refs_in, *refs_out, *rest)
        for axis, outer, inner, forward, backward in sends:
            odd = lax.axis_index(axis) & 1

            @pl.when(odd == 0)
            def _():
                outer[...] = backward[...]
                inner[...] = forward[...]

            @pl.when(odd == 1)
            def _():
                outer[...] = forward[...]
                inner[...] = backward[...]

    results = pl.pallas_call(
        body,
        out_shape=[s if hasattr(s, "dtype") else jax.ShapeDtypeStruct(s, F32) for s in shapes],
        in_specs=[HBM if i in remote else VMEM for i in range(total)],
        out_specs=[VMEM] * len(shapes),
        scratch_shapes=own + [pltpu.VMEM(s, F32) if isinstance(s, tuple) else s for s in scratch],
        compiler_params=pltpu.CompilerParams(vmem_limit_bytes=limit),
    )(*flat)
    results, joined = list(results), []
    for item in out:
        if isinstance(item, Beside):
            joined.append(Beside(item.axis, item.shape, results.pop(0), results.pop(0)))
        else:
            joined.append(results.pop(0))
    return joined


def split3(x):
    high = x.astype(BF16)
    rest = x - high.astype(F32)
    middle = rest.astype(BF16)
    return high, middle, (rest - middle.astype(F32)).astype(BF16)


def dot(a, b):
    return jnp.dot(a, b, preferred_element_type=F32)


def dot_exact(x, table):
    high, middle, low = split3(x)
    return dot(high, table) + (dot(middle, table) + dot(low, table))


def pair_table(depth):
    table = np.zeros((depth, depth // 2), ml_dtypes.bfloat16)
    table[np.arange(depth), np.arange(depth) // 2] = 1
    return table


def put_tiles(tiles, x):
    for k in range(tiles.shape[0]):
        tiles[k] = x[:, 128 * k : 128 * k + 128]


def every_other(tiles, start, size):
    return jnp.concatenate(
        [tiles[k, pl.ds(start, size, stride=2), :] for k in range(tiles.shape[0])], axis=1
    )


def back(x, axis):
    return pltpu.roll(x, 1, axis)


def ahead(x, axis):
    return pltpu.roll(x, x.shape[axis] - 1, axis)


def parity2(shape):
    return (lax.broadcasted_iota(jnp.int32, shape, 0) + lax.broadcasted_iota(jnp.int32, shape, 1)) & 1


def row_sum(r, v, wx, wy, wz):
    centre = v[r]
    y, z = wy[r], wz[r]
    total = wx[r] * v[r + 1] + wx[r - 1] * v[r - 1]
    total = total + y * ahead(centre, 0) + back(y * centre, 0)
    return centre, total + z * ahead(centre, 1) + back(z * centre, 1)


def half_sweep(first, last, colour, parity, v, b, wx, wy, wz, rdiag):
    unroll = UNROLL if v.shape[-1] > 256 else last - first

    def body(r, carry):
        centre, total = row_sum(r, v, wx, wy, wz)
        mine = parity == ((r + colour) & 1)
        v[r] = jnp.where(mine, (b[r] + total) * rdiag[r], centre)
        return carry

    lax.fori_loop(first, last, body, 0, unroll=unroll)


def plane(src, face, a, r):
    return src[r] if a == 0 else face[a - 1, r].astype(F32)


def pack_y_kernel(src_in, face_in, to_right, to_left, src, face, sem):
    rows, cols, depth = src.shape
    copies = [pltpu.make_async_copy(src_in, src, sem.at[0]), pltpu.make_async_copy(face_in, face, sem.at[1])]
    for copy in copies:
        copy.start()
    for copy in copies:
        copy.wait()
    for out, base in ((to_right, cols - H), (to_left, 0)):
        for r in range(rows):
            for t, pair in enumerate(((0, 3), (1, 2))):
                for s, a in enumerate(pair):
                    value = plane(src, face, a, r)
                    if out is to_right and a == 3:
                        value_all = value + back(value, 1) + back(plane(src, face, 2, r), 0)
                        first = lax.broadcasted_iota(jnp.int32, value.shape, 0) == base
                        value = jnp.where(first, value_all, value)
                    out[2 * r + t, H * s : H * s + H] = value[base : base + H]


def pack_x_kernel(src, face, to_up, to_down):
    rows, cols, depth = src.shape
    tiles = cols // 8
    for out, base in ((to_up, rows - H), (to_down, 0)):
        for a in range(4):
            for k in range(H):
                value = plane(src, face, a, base + k)
                if out is to_up and a == 3 and k == 0:
                    value = value + back(value, 1) + plane(src, face, 1, base - 1)
                for t in range(tiles):
                    out[(a * H + k) * tiles + t] = value[8 * t : 8 * t + 8]


def coarsen_kernel(face, out, pairs, odds, tx):
    _, rows, cols, depth = face.shape
    fine = lax.broadcasted_iota(jnp.int32, pairs.shape, 0)
    coarse = 2 * lax.broadcasted_iota(jnp.int32, pairs.shape, 1)
    pairs[...] = jnp.where((fine & -2) == coarse, 1.0, 0.0).astype(BF16)
    odds[...] = jnp.where(fine == coarse + 1, 1.0, 0.0).astype(BF16)
    half, n = cols // 2, rows // 2

    def both(x):
        put_tiles(tx, x)
        return 0.0625 * (every_other(tx, 0, half) + every_other(tx, 1, half))

    for i in range(n):
        out[i] = both(dot(face[0, 2 * i + 1], pairs[...]))
        put_tiles(tx, dot(face[1, 2 * i], pairs[...]) + dot(face[1, 2 * i + 1], pairs[...]))
        out[n + i] = 0.0625 * every_other(tx, 1, half)
        out[2 * n + i] = both(dot(face[2, 2 * i], odds[...]) + dot(face[2, 2 * i + 1], odds[...]))


def forward_kernel(right, left, to_up, to_down, *, rows):
    tiles = to_up.shape[0] // 2
    place = {0: (0, 0), 3: (0, 1), 1: (1, 0), 2: (1, 1)}
    for msg, sy in ((right, 1), (left, -1)):
        start = 0 if sy > 0 else tiles
        for out, sx in ((to_up, 1), (to_down, -1)):
            for n, (a, dx, dy) in enumerate(CORNER0):
                r = rows - dx if sx > 0 else dx - 1
                t, s = place[a]
                s = H * s + (H - dy if sy > 0 else dy - 1)
                out[start + n // 8, n % 8 : n % 8 + 1] = msg[2 * r + t, s : s + 1]


def diagonal_row(r, parity, low_col, b, wx, wy, wz, diag, rdiag, v):
    y, z = wy[r], wz[r]
    if isinstance(r, int) and r == 0:
        total = MASS + wx[r] + z + y + back(y, 0)
    else:
        total = MASS + wx[r] + wx[r - 1] + y
        total = total + jnp.where(low_col, z, z + back(z, 1) + back(y, 0))
    diag[r] = total
    inverse = 1.0 / total
    rdiag[r] = inverse
    v[r] = jnp.where(parity == (r & 1), b[r] * inverse, 0.0)


def assemble_kernel(src, face, up, down, right, left, state):
    b, wx, wy, wz, rdiag, diag, v = (state.at[i] for i in range(7))
    rows, cols, depth = src.shape
    ext = (b, wx, wy, wz)
    ec = cols + 2 * H
    for r in range(rows):
        b[H + r, H : H + cols] = src[r]
        for d in range(3):
            ext[1 + d][H + r, H : H + cols] = face[d, r].astype(F32)
    tiles = cols // 8
    for msg, base in ((up, 0), (down, H + rows)):
        for a in range(4):
            for k in range(H):
                for t in range(tiles):
                    ext[a][base + k, H + 8 * t : H + 8 * t + 8] = msg[(a * H + k) * tiles + t]
    for msg, base in ((right, 0), (left, H + cols)):
        for r in range(rows):
            for t, pair in enumerate(((0, 3), (1, 2))):
                for s, a in enumerate(pair):
                    ext[a][H + r, base : base + H] = msg[2 * r + t, H * s : H * s + H]
    parity = parity2((ec, depth))
    low_col = lax.broadcasted_iota(jnp.int32, (ec, depth), 0) == 0

    def body(r, carry):
        diagonal_row(r, parity, low_col, b, wx, wy, wz, diag, rdiag, v)
        return carry

    lax.fori_loop(H + 1, H + rows, body, 0)


def pre_kernel(up, down, pairs, state, kept, v_own, right1, to_right, to_left, *scratch):
    t512, t256, diag, v = scratch
    b, wx, wy, wz, rdiag = (kept.at[i] for i in range(5))
    kept[...] = state[0:5]
    diag[...] = state[5]
    v[...] = state[6]
    ext = (b, wx, wy, wz)
    rows, cols, depth = v_own.shape
    er, ec = rows + 2 * H, cols + 2 * H
    rows1, cols1 = rows // 2, cols // 2
    tiles = len(CORNER0) // 8
    for msg, sx, sy in ((up, 1, 1), (up, 1, -1), (down, -1, 1), (down, -1, -1)):
        start = 0 if sy > 0 else tiles

        def at(distance, size, sign):
            return H - distance if sign > 0 else H + size + distance - 1

        for n, (a, dx, dy) in enumerate(CORNER0):
            r, c = at(dx, rows, sx), at(dy, cols, sy)
            ext[a][r, c : c + 1] = msg[start + n // 8, n % 8 : n % 8 + 1]
    parity = parity2((ec, depth))
    low_col = lax.broadcasted_iota(jnp.int32, (ec, depth), 0) == 0
    for r in (*range(H + 1), *range(H + rows, er)):
        diagonal_row(r, parity, low_col, b, wx, wy, wz, diag, rdiag, v)
    half_sweep(1, er - 1, 1, parity, v, b, wx, wy, wz, rdiag)
    half_sweep(2, er - 2, 0, parity, v, b, wx, wy, wz, rdiag)
    half_sweep(3, er - 3, 1, parity, v, b, wx, wy, wz, rdiag)

    def residual_body(i, carry):
        total = 0.0
        for k in range(2):
            r = H + 2 * i + k
            centre, around = row_sum(r, v, wx, wy, wz)
            total = total + (b[r] - (diag[r] * centre - around))
        t512[i] = total
        return carry

    lax.fori_loop(0, rows1, residual_body, 0, unroll=UNROLL)
    put_tiles(t256, dot_exact(t512[...].reshape(rows1 * ec, depth), pairs[...]))
    for i in range(rows1):
        start = i * ec + H
        right1[i] = 0.125 * (every_other(t256, start, cols1) + every_other(t256, start + 1, cols1))

    start = to_right.shape[0] - rows1 // 2
    for i in range(rows1 // 2):
        to_right[start + i] = jnp.concatenate((right1[2 * i], right1[2 * i + 1]), axis=1)
        to_left[start + i] = to_right[start + i]

    own_parity = parity2((cols, depth))
    for r in range(rows):
        value = v[H + r, H : H + cols]
        v_own[r] = value
        value = jnp.where(own_parity == ((r + 1) & 1), value, ahead(value, 0))
        for p in range(H // 2):
            n = p * rows + r
            for out, base in ((to_right, cols - H), (to_left, 0)):
                out[n // 8, n % 8 : n % 8 + 1] = value[base + 2 * p : base + 2 * p + 1]


def pack_v_kernel(v0, right, left, v0_rows, to_up, to_down):
    rows, cols, depth = v0.shape
    for r in range(rows):
        v0_rows[r, H : H + cols] = v0[r]
        for msg, base in ((right, 0), (left, H + cols)):
            for p in range(H // 2):
                n = p * rows + r
                line = msg[n // 8, n % 8 : n % 8 + 1]
                v0_rows[r, base + 2 * p : base + 2 * p + 2] = jnp.broadcast_to(line, (2, depth))
    ec = v0_rows.shape[1]
    parity = parity2((ec, depth))
    for out, base in ((to_up, rows - H), (to_down, 0)):
        for k in range(H // 2):
            r = base + 2 * k
            out[k] = jnp.where(parity == ((r + 1) & 1), v0_rows[r], v0_rows[r + 1])


def before_kernel(x, up, down, pairs, out, tx):
    n, half, _ = x.shape
    tiles = 2 * half // 8
    start = (2 * H - 1) * tiles
    before = jnp.concatenate([up[start + t] for t in range(tiles)], axis=0)
    put_tiles(tx, dot(before.astype(BF16), pairs[...]))
    out[n] = 0.0625 * (every_other(tx, 0, half) + every_other(tx, 1, half))
    out[0:n] = x[...]


def couplings1_kernel(own, before_block, after_block, *refs):
    *between, w, rdiag, to_up, to_down, sums = refs
    blocks = [own, after_block, *between, before_block]
    planes, cols, depth = blocks[0].shape
    rows = planes // 3
    wide = cols * len(blocks)

    def plane(n):
        return jnp.concatenate([block[n] for block in blocks], axis=0)

    before = plane(3 * rows)
    for i in range(rows):
        x, y, z = plane(i), plane(rows + i), plane(2 * rows + i)
        w[0, i], w[1, i], w[2, i] = x, y, z
        rdiag[i] = 1.0 / (MASS + x + before + y + back(y, 0) + z + back(z, 1))
        before = x
    for d in range(3):
        for k in range(H - 1):
            to_up[d * (H - 1) + k] = w[d, rows - H + 1 + k]
            to_down[d * (H - 1) + k] = w[d, k]
    to_up[3 * (H - 1)] = w[0, rows - H]
    lane = lax.broadcasted_iota(jnp.int32, sums.shape, 1)
    row_odd = lax.broadcasted_iota(jnp.int32, (wide, depth), 0) & 1
    depth_odd = lax.broadcasted_iota(jnp.int32, (wide, depth), 1) & 1
    parts = [0.0, 0.0, 0.0]
    for i in range(rows):
        if i % 2 == 1:
            parts[0] = parts[0] + w[0, i]
        parts[1] = parts[1] + jnp.where(row_odd == 1, w[1, i], 0.0)
        parts[2] = parts[2] + jnp.where(depth_odd == 1, w[2, i], 0.0)
    line = jnp.zeros(sums.shape, F32)
    for d in range(3):
        line = jnp.where(lane == d, 0.0625 * jnp.sum(parts[d]), line)
    sums[...] = line


def pack1_kernel(right, left, own1, *refs):
    *between, rdiag, own, to_up, to_down = refs
    rows, cols, depth = own1.shape
    start = right.shape[0] - rows // 2
    for i in range(rows):
        lane = depth * (i % 2)
        parts = [own1[i], left[start + i // 2, :, lane : lane + depth]]
        parts += [block[i] for block in between]
        own[i] = jnp.concatenate(parts + [right[start + i // 2, :, lane : lane + depth]], axis=0)
    for k in range(H):
        value = own[rows - H + k]
        to_up[k] = value * rdiag[rows - H] if k == 0 else value
        value = own[k]
        to_down[k] = value * rdiag[k] if k == H - 1 else value


def pre1_kernel(own, up, down, w, w_up, w_down, v0_up, v0_down, kept, to_up, to_down):
    rows, wide, depth = own.shape
    er = rows + 2 * H
    wx, wy, wz, rdiag, b, v, diag = (kept.at[i] for i in range(7))
    b[0:H] = up[...]
    b[H : H + rows] = own[...]
    b[H + rows :] = down[...]
    for d in range(3):
        kept[d, H : H + rows] = w[d]
        kept[d, 1:H] = w_up[d * (H - 1) : (d + 1) * (H - 1)]
        kept[d, H + rows : er - 1] = w_down[d * (H - 1) : (d + 1) * (H - 1)]
    wx[0] = w_up[3 * (H - 1)]
    parity = parity2((wide, depth))
    for r in range(er):
        if 0 < r < er - 1:
            y, z = wy[r], wz[r]
            total = MASS + wx[r] + wx[r - 1] + y + back(y, 0) + z + back(z, 1)
            diag[r] = total
            inverse = 1.0 / total
            rdiag[r] = inverse
            first = b[r] * inverse
        else:
            first = b[r]
        v[r] = jnp.where(parity == (r & 1), first, 0.0)
    half_sweep(1, er - 1, 1, parity, v, b, wx, wy, wz, rdiag)
    half_sweep(2, er - 2, 0, parity, v, b, wx, wy, wz, rdiag)
    half_sweep(3, er - 3, 1, parity, v, b, wx, wy, wz, rdiag)
    for out, base, v0 in ((to_up, rows, v0_up), (to_down, H, v0_down)):
        n = 0
        for k in range(H // 2):
            value = jnp.concatenate((v[base + 2 * k], v[base + 2 * k + 1]), axis=1)
            for t in range(wide // 8):
                out[n] = value[8 * t : 8 * t + 8]
                n += 1
        for k in range(H // 2):
            for t in range(v0.shape[1] // 8):
                out[n] = v0[k, 8 * t : 8 * t + 8]
                n += 1


def residual1_kernel(kept1, pairs, sums, chunks, t256, t128):
    wx, wy, wz, _, b, v, diag = (kept1.at[i] for i in range(7))
    _, er, wide, depth = kept1.shape
    rows = er - 2 * H
    chunk = chunks.at[0]
    for i in range(rows // 2):
        total = 0.0
        for k in range(2):
            r = H + 2 * i + k
            centre, around = row_sum(r, v, wx, wy, wz)
            total = total + (b[r] - (diag[r] * centre - around))
        t256[i] = total
    n = rows // 2
    put_tiles(t128, dot_exact(t256[...].reshape(n * wide, depth), pairs[...]))
    half = wide // 2
    for i in range(n):
        start = i * wide
        chunk[i * half : (i + 1) * half] = 0.125 * (every_other(t128, start, half) + every_other(t128, start + 1, half))
    chunk[n * half : n * half + 1] = sums[0:1]
    for i in range(1, chunks.shape[0]):
        chunks[i] = chunk[...]


def split2(x):
    high = x.astype(BF16)
    return high, (x - high.astype(F32)).astype(BF16)


def dot_split(a, b):
    return dot(a[0], b[0]) + (dot(a[0], b[1]) + dot(a[1], b[0]))


def solve_kernel(got, table, out, *, count, start):
    devices, lines, depth = got.shape
    own = lines - 1
    cells = devices * own
    rx, ry, _ = out.shape

    def part(name, size, lane=0, width=None):
        return table[start[name] : start[name] + size, lane : lane + (width or table.shape[1])]

    values = jnp.concatenate([got[d, 0:own] for d in range(devices)], axis=0)
    sums = got[0, own : own + 1]
    for d in range(1, devices):
        sums = sums + got[d, own : own + 1]
    sums = sums * (1.0 / count)
    lam = MASS + sums[0:1, 0:1] * part("eig", cells, 0, depth)
    lam = lam + sums[0:1, 1:2] * part("eig", cells, depth, depth)
    lam = lam + sums[0:1, 2:3] * part("depth", 1, depth, depth)
    spec = dot_split(split2(values), split2(part("depth", depth, 0, depth)))
    spec = dot_split(split2(part("forward", cells)), split2(spec))
    spec = spec / (lam * float(count))
    spec = dot_split(split2(spec), split2(part("depth_out", depth)))
    step = -(-rx // 8) * 8
    along_x = table[pl.ds(pl.multiple_of(start["x"] + lax.axis_index("gx") * step, 8), step), :]
    along_y = part("y", ry)
    back_table = jnp.concatenate([along_x[i : i + 1] * along_y for i in range(rx)], axis=0)
    out[...] = dot_split(split2(back_table), split2(spec)).reshape(out.shape)


def post1_kernel(kept1, up, down, correction, own, to_up, to_down, v, *, cols):
    wx, wy, wz, rdiag, b, before, _ = (kept1.at[i] for i in range(7))
    er, wide, depth = before.shape
    rows = er - 2 * H
    for r in range(rows):
        v[H + r] = before[H + r] + correction[H + r]
    for msg, base in ((up, 0), (down, H + rows)):
        for k in range(H // 2):
            n = k * (wide // 8)
            value = jnp.concatenate([msg[n + t] for t in range(wide // 8)], axis=0)
            v[base + 2 * k] = value[:, :depth] + correction[base + 2 * k]
            v[base + 2 * k + 1] = value[:, depth:] + correction[base + 2 * k + 1]
    parity = parity2((wide, depth))
    half_sweep(1, er - 1, 0, parity, v, b, wx, wy, wz, rdiag)
    half_sweep(2, er - 2, 1, parity, v, b, wx, wy, wz, rdiag)
    half_sweep(3, er - 3, 0, parity, v, b, wx, wy, wz, rdiag)
    half_sweep(4, er - 4, 1, parity, v, b, wx, wy, wz, rdiag)
    h = H // 2
    used = cols + 2 * h
    for r in range(rows):
        value = v[H + r]
        own[r, 0:h] = value[wide - h :]
        own[r, h:used] = value[0 : cols + h]
        if used < own.shape[1]:
            own[r, used:] = jnp.zeros((own.shape[1] - used, depth), F32)
    to_up[...] = own[rows - h :]
    to_down[...] = own[0:h]


def spread_kernel(v0_rows, up, down, v):
    er, ec, _ = v.shape
    rows = er - 2 * H
    v[H : H + rows] = v0_rows[...]
    tiles = ec // 8
    for msg, base in ((up, 0), (down, H + rows)):
        start = msg.shape[0] - (H // 2) * tiles
        for k in range(H // 2):
            for t in range(tiles):
                tile = msg[start + k * tiles + t]
                v[base + 2 * k, 8 * t : 8 * t + 8] = tile
                v[base + 2 * k + 1, 8 * t : 8 * t + 8] = tile


def post_kernel(v_in, rows_own, up1, down1, kept, spread, out, v, t256):
    b, wx, wy, wz, rdiag = (kept.at[i] for i in range(5))
    rows, cols, depth = out.shape
    rows1, wide1, half = rows_own.shape
    er, ec = rows + 2 * H, cols + 2 * H
    h = H // 2
    ec1 = cols // 2 + 2 * h
    n1 = rows1 + 2 * h
    t256[0:h] = up1[...]
    t256[h : h + rows1] = rows_own[...]
    t256[h + rows1 :] = down1[...]
    wide = dot_exact(t256[...].reshape(n1 * t256.shape[1], half), spread[...])
    wide = wide.reshape(n1, t256.shape[1], depth)
    for n in range(n1):
        line = wide[n, 0:ec1]
        line = jnp.broadcast_to(line[:, None, :], (ec1, 2, depth)).reshape(2 * ec1, depth)
        v[2 * n] = v_in[2 * n] + line
        v[2 * n + 1] = v_in[2 * n + 1] + line
    parity = parity2((ec, depth))
    half_sweep(1, er - 1, 0, parity, v, b, wx, wy, wz, rdiag)
    half_sweep(2, er - 2, 1, parity, v, b, wx, wy, wz, rdiag)
    half_sweep(3, er - 3, 0, parity, v, b, wx, wy, wz, rdiag)
    half_sweep(4, er - 4, 1, parity, v, b, wx, wy, wz, rdiag)
    for r in range(rows):
        out[r] = v[H + r, H : H + cols]


def hartley(rows, columns, length):
    angle = (np.outer(rows, columns) % length) * (2.0 * math.pi / length)
    return np.cos(angle) + np.sin(angle)


def waves(length):
    return 2.0 * (1.0 - np.cos(np.arange(length) * (2.0 * math.pi / length)))


def windows(table, count, step, size):
    pad = -size % 8
    parts = [np.pad(table[i * step : i * step + size], ((0, pad), (0, 0))) for i in range(count)]
    return np.concatenate(parts)


def coarse_correction(chunks, rows, cols, depth):
    nx = lax.axis_size("gx")
    total_rows = rows * nx
    count = total_rows * cols * depth
    got = lax.all_to_all(chunks, "gx", 0, 0)
    out_rows = 2 * rows + 2 * H
    rows_ids = (np.arange(-H, 2 * total_rows + H) // 2) % total_rows
    table_x = hartley(rows_ids, np.arange(total_rows), total_rows)
    table_y = hartley(np.arange(2 * cols) // 2, np.arange(cols), cols)
    forward_x = hartley(np.arange(total_rows), np.arange(total_rows), total_rows)
    forward_y = hartley(np.arange(cols), np.arange(cols), cols)
    depth_in = hartley(np.arange(depth), np.arange(depth), depth)
    depth_out = np.repeat(depth_in, 2, axis=1)
    cells = total_rows * cols
    if cells <= 512 and cells == 2 * depth:
        ones = np.ones((1, depth))
        eig_x = np.repeat(waves(total_rows), cols)[:, None] * ones
        eig_y = np.tile(waves(cols), total_rows)[:, None] * ones
        eig_z = np.ones((depth, 1)) * waves(depth)[None, :]
        parts = {
            "forward": np.kron(forward_x, forward_y),
            "eig": np.concatenate((eig_x, eig_y), axis=1),
            "depth": np.concatenate((depth_in, eig_z), axis=1),
            "depth_out": depth_out,
            "x": windows(np.repeat(table_x, cols, axis=1), nx, 2 * rows, out_rows),
            "y": np.tile(table_y, (1, total_rows)),
        }
        start, size = {}, 0
        for name, part in parts.items():
            start[name] = size
            size += part.shape[0]
            assert size % 8 == 0
        table = jnp.asarray(np.concatenate(list(parts.values())), F32)
        return call(
            functools.partial(solve_kernel, count=count, start=start),
            [(out_rows, 2 * cols, 2 * depth)],
            got, table,
        )[0]

    hi = lax.Precision.HIGHEST
    f32 = lambda x: jnp.asarray(x, F32)
    averages = jnp.sum(got[:, rows * cols, :3], axis=0) / count
    full = got[:, : rows * cols].reshape(total_rows, cols, depth)
    spec = jnp.einsum("abz,zk->abk", full, f32(depth_in), precision=hi)
    spec = jnp.einsum("ij,jbz->ibz", f32(forward_x), spec, precision=hi)
    spec = jnp.einsum("ij,ajz->aiz", f32(forward_y), spec, precision=hi)
    lam = (
        MASS
        + averages[0] * f32(waves(total_rows))[:, None, None]
        + averages[1] * f32(waves(cols))[None, :, None]
        + averages[2] * f32(waves(depth))[None, None, :]
    )
    spec = spec / (lam * float(count))
    own_x = lax.dynamic_slice_in_dim(f32(table_x), lax.axis_index("gx") * 2 * rows, out_rows, 0)
    out = jnp.einsum("ij,jbz->ibz", own_x, spec, precision=hi)
    out = jnp.einsum("ij,ajz->aiz", f32(table_y), out, precision=hi)
    return jnp.einsum("abz,zk->abk", out, f32(depth_out), precision=hi)


def gathered(block):
    return [block] + [moved(block, 0, -k) for k in range(1, lax.axis_size("gy"))]


def shards(source, face_coef):
    rows, cols, depth = source.shape
    rows1, cols1, depth1 = rows // 2, cols // 2, depth // 2
    er, ec, er1 = rows + 2 * H, cols + 2 * H, rows1 + 2 * H
    wide = cols1 * lax.axis_size("gy")
    h = H // 2
    limit = VMEM_LIMIT if wide * depth1 <= 8192 else 5 * VMEM_LIMIT

    count = lax.axis_size("gy")
    corner_tiles = len(CORNER0) // 8
    y_first, source, face_coef = call(
        pack_y_kernel,
        [Beside("gy", (2 * rows, 8, depth)), (rows, cols, depth), jax.ShapeDtypeStruct((3, rows, cols, depth), BF16)],
        source, face_coef,
        remote=(0, 1),
        scratch=[pltpu.SemaphoreType.DMA((2,))],
    )
    y_first = y_first.exchanged()
    block, pairs = call(
        coarsen_kernel,
        [(3 * rows1, cols1, depth1), jax.ShapeDtypeStruct((depth, depth1), BF16)],
        face_coef,
        scratch=[pltpu.VMEM((depth, depth1), BF16), (depth1 // 128, cols, 128)],
    )
    (x_first,) = call(pack_x_kernel, [Beside("gx", (4 * H * (cols // 8), 8, depth))], source, face_coef, near=(block,))
    x_first = x_first.exchanged()
    (corners,) = call(
        functools.partial(forward_kernel, rows=rows),
        [Beside("gx", (2 * corner_tiles, 8, depth))],
        y_first,
    )
    (block,) = call(
        before_kernel,
        [(3 * rows1 + 1, cols1, depth1)],
        block, x_first, pairs,
        near=(corners,),
        scratch=[(depth1 // 128, cols, 128)],
    )
    corners = corners.exchanged()
    blocks = Beside("gy", block.shape, block, block).exchanged()
    blocks_between = [moved(block, "gy", -k) for k in range(2, count - 1)]
    (state,) = call(assemble_kernel, [(7, er, ec, depth)], source, face_coef, x_first, y_first)
    kept, v0, right1, y_second = call(
        pre_kernel,
        [(5, er, ec, depth), (rows, cols, depth), (rows1, cols1, depth1)]
        + [Beside("gy", (rows * h // 8 + rows1 // 2, 8, depth))],
        corners, pairs, state,
        scratch=[(rows1, ec, depth), (depth1 // 128, rows1 * ec, 128)] + [(er, ec, depth)] * 2,
    )

    y_second = y_second.exchanged()
    between = [moved(right1, "gy", -k) for k in range(2, count - 1)]
    w_own, rdiag_own, w_x, sums = call(
        couplings1_kernel,
        [(3, rows1, wide, depth1), (rows1, wide, depth1), Beside("gx", (3 * H - 2, wide, depth1))]
        + [(8, depth1 // 2)],
        block, blocks, *blocks_between,
        near=(right1,), limit=limit,
    )
    w_x = w_x.exchanged()
    own, x_second = call(
        pack1_kernel,
        [(rows1, wide, depth1), Beside("gx", (H, wide, depth1))],
        y_second, right1, *between, rdiag_own,
        near=(kept,), limit=limit,
    )
    x_second = x_second.exchanged()
    v0_rows, v0_up, v0_down = call(pack_v_kernel, [(rows, ec, depth)] + [(h, ec, depth)] * 2, v0, y_second)
    tiles = h * (wide // 8 + ec // 8)
    kept1, x_third = call(
        pre1_kernel,
        [(7, er1, wide, depth1), Beside("gx", (tiles, 8, depth))],
        own, x_second, w_own, w_x, v0_up, v0_down,
        near=(kept,), limit=limit,
    )
    x_third = x_third.exchanged()
    (chunks,) = call(
        residual1_kernel,
        [(lax.axis_size("gx"), rows1 * wide // 4 + 1, depth1 // 2)],
        kept1, jnp.asarray(pair_table(depth1)), sums,
        scratch=[(rows1 // 2, wide, depth1), (depth1 // 256, rows1 // 2 * wide, 128)],
        limit=limit,
    )
    correction2 = coarse_correction(chunks, rows1 // 2, wide // 2, depth1 // 2)
    used = -(-(cols1 + 2 * h) // 8) * 8
    own, x_fourth = call(
        functools.partial(post1_kernel, cols=cols1),
        [(rows1, used, depth1), Beside("gx", (h, used, depth1))],
        kept1, x_third, correction2,
        scratch=[(er1, wide, depth1)],
        limit=limit,
    )
    x_fourth = x_fourth.exchanged()
    (v0e,) = call(spread_kernel, [(er, ec, depth)], v0_rows, x_third)
    (out,) = call(
        post_kernel,
        [(rows, cols, depth)],
        v0e, own, x_fourth, kept,
        jnp.asarray(np.ascontiguousarray(pair_table(depth).T)),
        scratch=[(er, ec, depth), (rows1 + 2 * h, used, depth1)],
    )
    return out


def solution(mesh):
    return jax.shard_map(
        shards,
        mesh=mesh,
        in_specs=(P("gx", "gy", None), P(None, "gx", "gy", None)),
        out_specs=P("gx", "gy", None),
        check_vma=False,
    )
```

```python
import functools
import math

import jax
import jax.numpy as jnp
import ml_dtypes
import numpy as np
from jax import lax
from jax.experimental import pallas as pl
from jax.experimental.pallas import tpu as pltpu
from jax.sharding import PartitionSpec as P

LEVELS = 3
SWEEPS = 2
MASS = 0.002
BOTH = ("gx", "gy")
H = 2 * SWEEPS
F32 = jnp.float32
UNROLL = 4
VMEM_LIMIT = 12 * 1024 * 1024
BF16 = jnp.bfloat16
VMEM = pl.BlockSpec(memory_space=pltpu.VMEM)
HBM = pl.BlockSpec(memory_space=pltpu.HBM)

CORNER0 = (
    (0, 1, 1), (0, 1, 2), (0, 1, 3), (1, 2, 3), (3, 1, 1), (3, 1, 2), (3, 1, 3), (2, 2, 3),
    (1, 1, 1), (1, 1, 2), (1, 1, 3), (1, 1, 4), (2, 1, 1), (2, 1, 2), (2, 1, 3), (2, 1, 4),
    (0, 2, 1), (0, 2, 2), (0, 3, 1), (1, 4, 1), (3, 2, 1), (3, 2, 2), (3, 3, 1), (2, 4, 1),
    (1, 2, 1), (1, 2, 2), (1, 3, 1), (1, 3, 2), (2, 2, 1), (2, 2, 2), (2, 3, 1), (2, 3, 2),
)

def moved(block, axis, distance):
    count = lax.axis_size(axis)
    return lax.ppermute(block, axis, [(i, (i + distance) % count) for i in range(count)])


class Beside:
    def __init__(self, axis, shape, outer=None, inner=None):
        self.axis, self.shape, self.outer, self.inner = axis, shape, outer, inner

    def exchanged(self):
        count = lax.axis_size(self.axis)
        assert count % 2 == 0
        got = []
        for block, first in ((self.outer, 1), (self.inner, 0)):
            route = []
            for i in range(first, count + first, 2):
                a, b = i % count, (i + 1) % count
                route += [(a, b), (b, a)]
            got.append(lax.ppermute(block, self.axis, route))
        return Beside(self.axis, self.shape, *got)


def call(kernel, out, *args, scratch=(), remote=(), limit=VMEM_LIMIT, near=()):
    flat, pairs_in, pairs_out, shapes = [], [], [], []
    for i, arg in enumerate(args):
        if isinstance(arg, Beside):
            pairs_in.append((len(flat), arg))
            flat += [arg.outer, arg.inner]
        else:
            flat.append(arg)
    for item in out:
        if isinstance(item, Beside):
            pairs_out.append((len(shapes), item))
            shapes += [item.shape] * 2
        else:
            shapes.append(item)
    count = len(flat)
    for item in near:
        flat += [item.outer, item.inner] if isinstance(item, Beside) else [item]
    total = len(flat)
    own = [pltpu.VMEM(p.shape, F32) for _, p in pairs_in + pairs_out for _ in range(2)]

    def body(*refs):
        refs_in, refs_out = list(refs[:count]), list(refs[total : total + len(shapes)])
        rest = list(refs[total + len(shapes) :])
        held, rest = rest[: len(own)], rest[len(own) :]
        sends = []
        for n, (i, pair) in enumerate(pairs_in + pairs_out):
            forward, backward = held[2 * n], held[2 * n + 1]
            is_in = n < len(pairs_in)
            refs_here = refs_in if is_in else refs_out
            outer, inner = refs_here[i], refs_here[i + 1]
            refs_here[i], refs_here[i + 1] = forward, backward
            if is_in:
                odd = lax.axis_index(pair.axis) & 1

                @pl.when(odd == 0)
                def _():
                    forward[...] = outer[...]
                    backward[...] = inner[...]

                @pl.when(odd == 1)
                def _():
                    forward[...] = inner[...]
                    backward[...] = outer[...]

            else:
                sends.append((pair.axis, outer, inner, forward, backward))
        kernel(*refs_in, *refs_out, *rest)
        for axis, outer, inner, forward, backward in sends:
            odd = lax.axis_index(axis) & 1

            @pl.when(odd == 0)
            def _():
                outer[...] = backward[...]
                inner[...] = forward[...]

            @pl.when(odd == 1)
            def _():
                outer[...] = forward[...]
                inner[...] = backward[...]

    results = pl.pallas_call(
        body,
        out_shape=[s if hasattr(s, "dtype") else jax.ShapeDtypeStruct(s, F32) for s in shapes],
        in_specs=[HBM if i in remote else VMEM for i in range(total)],
        out_specs=[VMEM] * len(shapes),
        scratch_shapes=own + [pltpu.VMEM(s, F32) if isinstance(s, tuple) else s for s in scratch],
        compiler_params=pltpu.CompilerParams(vmem_limit_bytes=limit),
    )(*flat)
    results, joined = list(results), []
    for item in out:
        if isinstance(item, Beside):
            joined.append(Beside(item.axis, item.shape, results.pop(0), results.pop(0)))
        else:
            joined.append(results.pop(0))
    return joined


def split3(x):
    high = x.astype(BF16)
    rest = x - high.astype(F32)
    middle = rest.astype(BF16)
    return high, middle, (rest - middle.astype(F32)).astype(BF16)


def dot(a, b):
    return jnp.dot(a, b, preferred_element_type=F32)


def dot_exact(x, table):
    high, middle, low = split3(x)
    return dot(high, table) + (dot(middle, table) + dot(low, table))


def pair_table(depth):
    table = np.zeros((depth, depth // 2), ml_dtypes.bfloat16)
    table[np.arange(depth), np.arange(depth) // 2] = 1
    return table


def put_tiles(tiles, x):
    for k in range(tiles.shape[0]):
        tiles[k] = x[:, 128 * k : 128 * k + 128]


def every_other(tiles, start, size):
    return jnp.concatenate(
        [tiles[k, pl.ds(start, size, stride=2), :] for k in range(tiles.shape[0])], axis=1
    )


def back(x, axis):
    return pltpu.roll(x, 1, axis)


def ahead(x, axis):
    return pltpu.roll(x, x.shape[axis] - 1, axis)


def parity2(shape):
    return (lax.broadcasted_iota(jnp.int32, shape, 0) + lax.broadcasted_iota(jnp.int32, shape, 1)) & 1


def row_sum(r, v, wx, wy, wz):
    centre = v[r]
    y, z = wy[r], wz[r]
    total = wx[r] * v[r + 1] + wx[r - 1] * v[r - 1]
    total = total + y * ahead(centre, 0) + back(y * centre, 0)
    return centre, total + z * ahead(centre, 1) + back(z * centre, 1)


def half_sweep(first, last, colour, parity, v, b, wx, wy, wz, rdiag):
    unroll = UNROLL if v.shape[-1] > 256 else last - first

    def body(r, carry):
        centre, total = row_sum(r, v, wx, wy, wz)
        mine = parity == ((r + colour) & 1)
        v[r] = jnp.where(mine, (b[r] + total) * rdiag[r], centre)
        return carry

    lax.fori_loop(first, last, body, 0, unroll=unroll)


def plane(src, face, a, r):
    return src[r] if a == 0 else face[a - 1, r].astype(F32)


def pack_y_kernel(src_in, face_in, to_right, to_left, src, face, sem):
    rows, cols, depth = src.shape
    copies = [pltpu.make_async_copy(src_in, src, sem.at[0]), pltpu.make_async_copy(face_in, face, sem.at[1])]
    for copy in copies:
        copy.start()
    for copy in copies:
        copy.wait()
    for out, base in ((to_right, cols - H), (to_left, 0)):
        for r in range(rows):
            for t, pair in enumerate(((0, 3), (1, 2))):
                for s, a in enumerate(pair):
                    value = plane(src, face, a, r)
                    if out is to_right and a == 3:
                        value_all = value + back(value, 1) + back(plane(src, face, 2, r), 0)
                        first = lax.broadcasted_iota(jnp.int32, value.shape, 0) == base
                        value = jnp.where(first, value_all, value)
                    out[2 * r + t, H * s : H * s + H] = value[base : base + H]


def pack_x_kernel(src, face, to_up, to_down):
    rows, cols, depth = src.shape
    tiles = cols // 8
    for out, base in ((to_up, rows - H), (to_down, 0)):
        for a in range(4):
            for k in range(H):
                value = plane(src, face, a, base + k)
                if out is to_up and a == 3 and k == 0:
                    value = value + back(value, 1) + plane(src, face, 1, base - 1)
                for t in range(tiles):
                    out[(a * H + k) * tiles + t] = value[8 * t : 8 * t + 8]


def coarsen_kernel(face, out, pairs, odds, tx):
    _, rows, cols, depth = face.shape
    fine = lax.broadcasted_iota(jnp.int32, pairs.shape, 0)
    coarse = 2 * lax.broadcasted_iota(jnp.int32, pairs.shape, 1)
    pairs[...] = jnp.where((fine & -2) == coarse, 1.0, 0.0).astype(BF16)
    odds[...] = jnp.where(fine == coarse + 1, 1.0, 0.0).astype(BF16)
    half, n = cols // 2, rows // 2

    def both(x):
        put_tiles(tx, x)
        return 0.0625 * (every_other(tx, 0, half) + every_other(tx, 1, half))

    for i in range(n):
        out[i] = both(dot(face[0, 2 * i + 1], pairs[...]))
        put_tiles(tx, dot(face[1, 2 * i], pairs[...]) + dot(face[1, 2 * i + 1], pairs[...]))
        out[n + i] = 0.0625 * every_other(tx, 1, half)
        out[2 * n + i] = both(dot(face[2, 2 * i], odds[...]) + dot(face[2, 2 * i + 1], odds[...]))


def forward_kernel(right, left, to_up, to_down, *, rows):
    tiles = to_up.shape[0] // 2
    place = {0: (0, 0), 3: (0, 1), 1: (1, 0), 2: (1, 1)}
    for msg, sy in ((right, 1), (left, -1)):
        start = 0 if sy > 0 else tiles
        for out, sx in ((to_up, 1), (to_down, -1)):
            for n, (a, dx, dy) in enumerate(CORNER0):
                r = rows - dx if sx > 0 else dx - 1
                t, s = place[a]
                s = H * s + (H - dy if sy > 0 else dy - 1)
                out[start + n // 8, n % 8 : n % 8 + 1] = msg[2 * r + t, s : s + 1]


def diagonal_row(r, parity, low_col, b, wx, wy, wz, diag, rdiag, v):
    y, z = wy[r], wz[r]
    if isinstance(r, int) and r == 0:
        total = MASS + wx[r] + z + y + back(y, 0)
    else:
        total = MASS + wx[r] + wx[r - 1] + y
        total = total + jnp.where(low_col, z, z + back(z, 1) + back(y, 0))
    diag[r] = total
    inverse = 1.0 / total
    rdiag[r] = inverse
    v[r] = jnp.where(parity == (r & 1), b[r] * inverse, 0.0)


def assemble_kernel(src, face, up, down, state):
    ext = [state.at[i] for i in range(4)]
    rows, cols, depth = src.shape
    for r in range(rows):
        ext[0][H + r, H : H + cols] = src[r]
        for d in range(3):
            ext[1 + d][H + r, H : H + cols] = face[d, r].astype(F32)
    tiles = cols // 8
    for msg, base in ((up, 0), (down, H + rows)):
        for a in range(4):
            for k in range(H):
                for t in range(tiles):
                    ext[a][base + k, H + 8 * t : H + 8 * t + 8] = msg[(a * H + k) * tiles + t]


def pre_kernel(up, down, right, left, pairs, state, kept, v_own, right1, to_right, to_left, *scratch):
    t512, t256, diag, v = scratch
    b, wx, wy, wz, rdiag = (kept.at[i] for i in range(5))
    kept[0:4] = state[...]
    ext = (b, wx, wy, wz)
    rows, cols, depth = v_own.shape
    er, ec = rows + 2 * H, cols + 2 * H
    rows1, cols1 = rows // 2, cols // 2
    for msg, base in ((right, 0), (left, H + cols)):
        for r in range(rows):
            for t, pair in enumerate(((0, 3), (1, 2))):
                for s, a in enumerate(pair):
                    ext[a][H + r, base : base + H] = msg[2 * r + t, H * s : H * s + H]
    tiles = len(CORNER0) // 8
    for msg, sx, sy in ((up, 1, 1), (up, 1, -1), (down, -1, 1), (down, -1, -1)):
        start = 0 if sy > 0 else tiles

        def at(distance, size, sign):
            return H - distance if sign > 0 else H + size + distance - 1

        for n, (a, dx, dy) in enumerate(CORNER0):
            r, c = at(dx, rows, sx), at(dy, cols, sy)
            ext[a][r, c : c + 1] = msg[start + n // 8, n % 8 : n % 8 + 1]
    parity = parity2((ec, depth))
    low_col = lax.broadcasted_iota(jnp.int32, (ec, depth), 0) == 0
    diagonal_row(0, parity, low_col, b, wx, wy, wz, diag, rdiag, v)

    def diagonal_body(r, carry):
        diagonal_row(r, parity, low_col, b, wx, wy, wz, diag, rdiag, v)
        return carry

    lax.fori_loop(1, er, diagonal_body, 0, unroll=UNROLL)
    half_sweep(1, er - 1, 1, parity, v, b, wx, wy, wz, rdiag)
    half_sweep(2, er - 2, 0, parity, v, b, wx, wy, wz, rdiag)
    half_sweep(3, er - 3, 1, parity, v, b, wx, wy, wz, rdiag)

    def residual_body(i, carry):
        total = 0.0
        for k in range(2):
            r = H + 2 * i + k
            centre, around = row_sum(r, v, wx, wy, wz)
            total = total + (b[r] - (diag[r] * centre - around))
        t512[i] = total
        return carry

    lax.fori_loop(0, rows1, residual_body, 0, unroll=UNROLL)
    put_tiles(t256, dot_exact(t512[...].reshape(rows1 * ec, depth), pairs[...]))
    for i in range(rows1):
        start = i * ec + H
        right1[i] = 0.125 * (every_other(t256, start, cols1) + every_other(t256, start + 1, cols1))

    start = to_right.shape[0] - rows1 // 2
    for i in range(rows1 // 2):
        to_right[start + i] = jnp.concatenate((right1[2 * i], right1[2 * i + 1]), axis=1)
        to_left[start + i] = to_right[start + i]

    own_parity = parity2((cols, depth))
    for r in range(rows):
        value = v[H + r, H : H + cols]
        v_own[r] = value
        value = jnp.where(own_parity == ((r + 1) & 1), value, ahead(value, 0))
        for p in range(H // 2):
            n = p * rows + r
            for out, base in ((to_right, cols - H), (to_left, 0)):
                out[n // 8, n % 8 : n % 8 + 1] = value[base + 2 * p : base + 2 * p + 1]


def pack_v_kernel(v0, right, left, v0_rows, to_up, to_down):
    rows, cols, depth = v0.shape
    for r in range(rows):
        v0_rows[r, H : H + cols] = v0[r]
        for msg, base in ((right, 0), (left, H + cols)):
            for p in range(H // 2):
                n = p * rows + r
                line = msg[n // 8, n % 8 : n % 8 + 1]
                v0_rows[r, base + 2 * p : base + 2 * p + 2] = jnp.broadcast_to(line, (2, depth))
    ec = v0_rows.shape[1]
    parity = parity2((ec, depth))
    for out, base in ((to_up, rows - H), (to_down, 0)):
        for k in range(H // 2):
            r = base + 2 * k
            out[k] = jnp.where(parity == ((r + 1) & 1), v0_rows[r], v0_rows[r + 1])


def before_kernel(x, up, down, pairs, out, tx):
    n, half, _ = x.shape
    tiles = 2 * half // 8
    start = (2 * H - 1) * tiles
    before = jnp.concatenate([up[start + t] for t in range(tiles)], axis=0)
    put_tiles(tx, dot(before.astype(BF16), pairs[...]))
    out[n] = 0.0625 * (every_other(tx, 0, half) + every_other(tx, 1, half))
    out[0:n] = x[...]


def couplings1_kernel(own, before_block, after_block, *refs):
    *between, w, rdiag, to_up, to_down, sums = refs
    blocks = [own, after_block, *between, before_block]
    planes, cols, depth = blocks[0].shape
    rows = planes // 3
    wide = cols * len(blocks)

    def plane(n):
        return jnp.concatenate([block[n] for block in blocks], axis=0)

    before = plane(3 * rows)
    for i in range(rows):
        x, y, z = plane(i), plane(rows + i), plane(2 * rows + i)
        w[0, i], w[1, i], w[2, i] = x, y, z
        rdiag[i] = 1.0 / (MASS + x + before + y + back(y, 0) + z + back(z, 1))
        before = x
    for d in range(3):
        for k in range(H - 1):
            to_up[d * (H - 1) + k] = w[d, rows - H + 1 + k]
            to_down[d * (H - 1) + k] = w[d, k]
    to_up[3 * (H - 1)] = w[0, rows - H]
    lane = lax.broadcasted_iota(jnp.int32, sums.shape, 1)
    row_odd = lax.broadcasted_iota(jnp.int32, (wide, depth), 0) & 1
    depth_odd = lax.broadcasted_iota(jnp.int32, (wide, depth), 1) & 1
    parts = [0.0, 0.0, 0.0]
    for i in range(rows):
        if i % 2 == 1:
            parts[0] = parts[0] + w[0, i]
        parts[1] = parts[1] + jnp.where(row_odd == 1, w[1, i], 0.0)
        parts[2] = parts[2] + jnp.where(depth_odd == 1, w[2, i], 0.0)
    line = jnp.zeros(sums.shape, F32)
    for d in range(3):
        line = jnp.where(lane == d, 0.0625 * jnp.sum(parts[d]), line)
    sums[...] = line


def pack1_kernel(right, left, own1, *refs):
    *between, rdiag, own, to_up, to_down = refs
    rows, cols, depth = own1.shape
    start = right.shape[0] - rows // 2
    for i in range(rows):
        lane = depth * (i % 2)
        parts = [own1[i], left[start + i // 2, :, lane : lane + depth]]
        parts += [block[i] for block in between]
        own[i] = jnp.concatenate(parts + [right[start + i // 2, :, lane : lane + depth]], axis=0)
    for k in range(H):
        value = own[rows - H + k]
        to_up[k] = value * rdiag[rows - H] if k == 0 else value
        value = own[k]
        to_down[k] = value * rdiag[k] if k == H - 1 else value


def pre1_kernel(own, up, down, w, w_up, w_down, v0_up, v0_down, kept, to_up, to_down):
    rows, wide, depth = own.shape
    er = rows + 2 * H
    wx, wy, wz, rdiag, b, v, diag = (kept.at[i] for i in range(7))
    b[0:H] = up[...]
    b[H : H + rows] = own[...]
    b[H + rows :] = down[...]
    for d in range(3):
        kept[d, H : H + rows] = w[d]
        kept[d, 1:H] = w_up[d * (H - 1) : (d + 1) * (H - 1)]
        kept[d, H + rows : er - 1] = w_down[d * (H - 1) : (d + 1) * (H - 1)]
    wx[0] = w_up[3 * (H - 1)]
    parity = parity2((wide, depth))
    for r in range(er):
        if 0 < r < er - 1:
            y, z = wy[r], wz[r]
            total = MASS + wx[r] + wx[r - 1] + y + back(y, 0) + z + back(z, 1)
            diag[r] = total
            inverse = 1.0 / total
            rdiag[r] = inverse
            first = b[r] * inverse
        else:
            first = b[r]
        v[r] = jnp.where(parity == (r & 1), first, 0.0)
    half_sweep(1, er - 1, 1, parity, v, b, wx, wy, wz, rdiag)
    half_sweep(2, er - 2, 0, parity, v, b, wx, wy, wz, rdiag)
    half_sweep(3, er - 3, 1, parity, v, b, wx, wy, wz, rdiag)
    for out, base, v0 in ((to_up, rows, v0_up), (to_down, H, v0_down)):
        n = 0
        for k in range(H // 2):
            value = jnp.concatenate((v[base + 2 * k], v[base + 2 * k + 1]), axis=1)
            for t in range(wide // 8):
                out[n] = value[8 * t : 8 * t + 8]
                n += 1
        for k in range(H // 2):
            for t in range(v0.shape[1] // 8):
                out[n] = v0[k, 8 * t : 8 * t + 8]
                n += 1


def residual1_kernel(kept1, pairs, sums, chunks, t256, t128):
    wx, wy, wz, _, b, v, diag = (kept1.at[i] for i in range(7))
    _, er, wide, depth = kept1.shape
    rows = er - 2 * H
    chunk = chunks.at[0]
    for i in range(rows // 2):
        total = 0.0
        for k in range(2):
            r = H + 2 * i + k
            centre, around = row_sum(r, v, wx, wy, wz)
            total = total + (b[r] - (diag[r] * centre - around))
        t256[i] = total
    n = rows // 2
    put_tiles(t128, dot_exact(t256[...].reshape(n * wide, depth), pairs[...]))
    half = wide // 2
    for i in range(n):
        start = i * wide
        chunk[i * half : (i + 1) * half] = 0.125 * (every_other(t128, start, half) + every_other(t128, start + 1, half))
    chunk[n * half : n * half + 1] = sums[0:1]
    for i in range(1, chunks.shape[0]):
        chunks[i] = chunk[...]


def split2(x):
    high = x.astype(BF16)
    return high, (x - high.astype(F32)).astype(BF16)


def dot_split(a, b):
    return dot(a[0], b[0]) + (dot(a[0], b[1]) + dot(a[1], b[0]))


def solve_kernel(got, table, out, *, count, start):
    devices, lines, depth = got.shape
    own = lines - 1
    cells = devices * own
    rx, ry, _ = out.shape

    def part(name, size, lane=0, width=None):
        return table[start[name] : start[name] + size, lane : lane + (width or table.shape[1])]

    values = jnp.concatenate([got[d, 0:own] for d in range(devices)], axis=0)
    sums = got[0, own : own + 1]
    for d in range(1, devices):
        sums = sums + got[d, own : own + 1]
    sums = sums * (1.0 / count)
    lam = MASS + sums[0:1, 0:1] * part("eig", cells, 0, depth)
    lam = lam + sums[0:1, 1:2] * part("eig", cells, depth, depth)
    lam = lam + sums[0:1, 2:3] * part("depth", 1, depth, depth)
    spec = dot_split(split2(values), split2(part("depth", depth, 0, depth)))
    spec = dot_split(split2(part("forward", cells)), split2(spec))
    spec = spec / (lam * float(count))
    spec = dot_split(split2(spec), split2(part("depth_out", depth)))
    step = -(-rx // 8) * 8
    along_x = table[pl.ds(pl.multiple_of(start["x"] + lax.axis_index("gx") * step, 8), step), :]
    along_y = part("y", ry)
    back_table = jnp.concatenate([along_x[i : i + 1] * along_y for i in range(rx)], axis=0)
    out[...] = dot_split(split2(back_table), split2(spec)).reshape(out.shape)


def post1_kernel(kept1, up, down, correction, own, to_up, to_down, v, *, cols):
    wx, wy, wz, rdiag, b, before, _ = (kept1.at[i] for i in range(7))
    er, wide, depth = before.shape
    rows = er - 2 * H
    for r in range(rows):
        v[H + r] = before[H + r] + correction[H + r]
    for msg, base in ((up, 0), (down, H + rows)):
        for k in range(H // 2):
            n = k * (wide // 8)
            value = jnp.concatenate([msg[n + t] for t in range(wide // 8)], axis=0)
            v[base + 2 * k] = value[:, :depth] + correction[base + 2 * k]
            v[base + 2 * k + 1] = value[:, depth:] + correction[base + 2 * k + 1]
    parity = parity2((wide, depth))
    half_sweep(1, er - 1, 0, parity, v, b, wx, wy, wz, rdiag)
    half_sweep(2, er - 2, 1, parity, v, b, wx, wy, wz, rdiag)
    half_sweep(3, er - 3, 0, parity, v, b, wx, wy, wz, rdiag)
    half_sweep(4, er - 4, 1, parity, v, b, wx, wy, wz, rdiag)
    h = H // 2
    used = cols + 2 * h
    for r in range(rows):
        value = v[H + r]
        own[r, 0:h] = value[wide - h :]
        own[r, h:used] = value[0 : cols + h]
        if used < own.shape[1]:
            own[r, used:] = jnp.zeros((own.shape[1] - used, depth), F32)
    to_up[...] = own[rows - h :]
    to_down[...] = own[0:h]


def spread_rows(lines, spread, used):
    rows, padded, _ = lines.shape
    wide = dot_exact(lines.reshape(rows * padded, lines.shape[2]), spread)
    depth = wide.shape[1]
    wide = wide.reshape(rows, padded, depth)
    out = []
    for n in range(rows):
        line = jnp.broadcast_to(wide[n, 0:used][:, None, :], (used, 2, depth))
        out.append(line.reshape(2 * used, depth))
    return out


def post_sweep(n, rows, v, kept, parity):
    b, wx, wy, wz, rdiag = (kept.at[i] for i in range(5))
    for first, last in rows:
        half_sweep(first, last, n % 2, parity, v, b, wx, wy, wz, rdiag)


def inner_kernel(v0_rows, up, down, own, kept, spread, v):
    er, ec, depth = v.shape
    rows = er - 2 * H
    tiles = ec // 8
    for msg, base in ((up, 0), (down, H + rows)):
        start = msg.shape[0] - (H // 2) * tiles
        for k in range(H // 2):
            for t in range(tiles):
                tile = msg[start + k * tiles + t]
                v[base + 2 * k, 8 * t : 8 * t + 8] = tile
                v[base + 2 * k + 1, 8 * t : 8 * t + 8] = tile
    for n, line in enumerate(spread_rows(own[...], spread[...], ec // 2)):
        v[H + 2 * n] = v0_rows[2 * n] + line
        v[H + 2 * n + 1] = v0_rows[2 * n + 1] + line
    parity = parity2((ec, depth))
    for n in range(H - 1):
        if H + 1 + n < er - H - 1 - n:
            post_sweep(n, ((H + 1 + n, er - H - 1 - n),), v, kept, parity)


def post_kernel(v_in, up1, down1, kept, spread, out, v):
    rows, cols, depth = out.shape
    er, ec = rows + 2 * H, cols + 2 * H
    v[H : H + rows] = v_in[H : H + rows]
    for msg, base in ((up1, 0), (down1, H + rows)):
        for n, line in enumerate(spread_rows(msg[...], spread[...], ec // 2)):
            v[base + 2 * n] = v_in[base + 2 * n] + line
            v[base + 2 * n + 1] = v_in[base + 2 * n + 1] + line
    parity = parity2((ec, depth))
    for n in range(H):
        low, high = H + 1 + n, er - H - 1 - n
        if n < H - 1 and low < high:
            post_sweep(n, ((1 + n, low), (high, er - 1 - n)), v, kept, parity)
        else:
            post_sweep(n, ((1 + n, er - 1 - n),), v, kept, parity)
    for r in range(rows):
        out[r] = v[H + r, H : H + cols]


def hartley(rows, columns, length):
    angle = (np.outer(rows, columns) % length) * (2.0 * math.pi / length)
    return np.cos(angle) + np.sin(angle)


def waves(length):
    return 2.0 * (1.0 - np.cos(np.arange(length) * (2.0 * math.pi / length)))


def windows(table, count, step, size):
    pad = -size % 8
    parts = [np.pad(table[i * step : i * step + size], ((0, pad), (0, 0))) for i in range(count)]
    return np.concatenate(parts)


def coarse_correction(chunks, rows, cols, depth):
    nx = lax.axis_size("gx")
    total_rows = rows * nx
    count = total_rows * cols * depth
    got = lax.all_to_all(chunks, "gx", 0, 0)
    out_rows = 2 * rows + 2 * H
    rows_ids = (np.arange(-H, 2 * total_rows + H) // 2) % total_rows
    table_x = hartley(rows_ids, np.arange(total_rows), total_rows)
    table_y = hartley(np.arange(2 * cols) // 2, np.arange(cols), cols)
    forward_x = hartley(np.arange(total_rows), np.arange(total_rows), total_rows)
    forward_y = hartley(np.arange(cols), np.arange(cols), cols)
    depth_in = hartley(np.arange(depth), np.arange(depth), depth)
    depth_out = np.repeat(depth_in, 2, axis=1)
    cells = total_rows * cols
    if cells <= 512 and cells == 2 * depth:
        ones = np.ones((1, depth))
        eig_x = np.repeat(waves(total_rows), cols)[:, None] * ones
        eig_y = np.tile(waves(cols), total_rows)[:, None] * ones
        eig_z = np.ones((depth, 1)) * waves(depth)[None, :]
        parts = {
            "forward": np.kron(forward_x, forward_y),
            "eig": np.concatenate((eig_x, eig_y), axis=1),
            "depth": np.concatenate((depth_in, eig_z), axis=1),
            "depth_out": depth_out,
            "x": windows(np.repeat(table_x, cols, axis=1), nx, 2 * rows, out_rows),
            "y": np.tile(table_y, (1, total_rows)),
        }
        start, size = {}, 0
        for name, part in parts.items():
            start[name] = size
            size += part.shape[0]
            assert size % 8 == 0
        table = jnp.asarray(np.concatenate(list(parts.values())), F32)
        return call(
            functools.partial(solve_kernel, count=count, start=start),
            [(out_rows, 2 * cols, 2 * depth)],
            got, table,
        )[0]

    hi = lax.Precision.HIGHEST
    f32 = lambda x: jnp.asarray(x, F32)
    averages = jnp.sum(got[:, rows * cols, :3], axis=0) / count
    full = got[:, : rows * cols].reshape(total_rows, cols, depth)
    spec = jnp.einsum("abz,zk->abk", full, f32(depth_in), precision=hi)
    spec = jnp.einsum("ij,jbz->ibz", f32(forward_x), spec, precision=hi)
    spec = jnp.einsum("ij,ajz->aiz", f32(forward_y), spec, precision=hi)
    lam = (
        MASS
        + averages[0] * f32(waves(total_rows))[:, None, None]
        + averages[1] * f32(waves(cols))[None, :, None]
        + averages[2] * f32(waves(depth))[None, None, :]
    )
    spec = spec / (lam * float(count))
    own_x = lax.dynamic_slice_in_dim(f32(table_x), lax.axis_index("gx") * 2 * rows, out_rows, 0)
    out = jnp.einsum("ij,jbz->ibz", own_x, spec, precision=hi)
    out = jnp.einsum("ij,ajz->aiz", f32(table_y), out, precision=hi)
    return jnp.einsum("abz,zk->abk", out, f32(depth_out), precision=hi)


def gathered(block):
    return [block] + [moved(block, 0, -k) for k in range(1, lax.axis_size("gy"))]


def shards(source, face_coef):
    rows, cols, depth = source.shape
    rows1, cols1, depth1 = rows // 2, cols // 2, depth // 2
    er, ec, er1 = rows + 2 * H, cols + 2 * H, rows1 + 2 * H
    wide = cols1 * lax.axis_size("gy")
    h = H // 2
    limit = VMEM_LIMIT if wide * depth1 <= 8192 else 5 * VMEM_LIMIT

    count = lax.axis_size("gy")
    corner_tiles = len(CORNER0) // 8
    y_first, source, face_coef = call(
        pack_y_kernel,
        [Beside("gy", (2 * rows, 8, depth)), (rows, cols, depth), jax.ShapeDtypeStruct((3, rows, cols, depth), BF16)],
        source, face_coef,
        remote=(0, 1),
        scratch=[pltpu.SemaphoreType.DMA((2,))],
    )
    y_first = y_first.exchanged()
    (x_first,) = call(pack_x_kernel, [Beside("gx", (4 * H * (cols // 8), 8, depth))], source, face_coef)
    x_first = x_first.exchanged()
    block, pairs = call(
        coarsen_kernel,
        [(3 * rows1, cols1, depth1), jax.ShapeDtypeStruct((depth, depth1), BF16)],
        face_coef,
        near=(x_first,),
        scratch=[pltpu.VMEM((depth, depth1), BF16), (depth1 // 128, cols, 128)],
    )
    (block,) = call(
        before_kernel,
        [(3 * rows1 + 1, cols1, depth1)],
        block, x_first, pairs,
        scratch=[(depth1 // 128, cols, 128)],
    )
    (corners,) = call(
        functools.partial(forward_kernel, rows=rows),
        [Beside("gx", (2 * corner_tiles, 8, depth))],
        y_first,
        near=(block,),
    )
    corners = corners.exchanged()
    blocks = Beside("gy", block.shape, block, block).exchanged()
    blocks_between = [moved(block, "gy", -k) for k in range(2, count - 1)]
    (state,) = call(assemble_kernel, [(4, er, ec, depth)], source, face_coef, x_first)
    kept, v0, right1, y_second = call(
        pre_kernel,
        [(5, er, ec, depth), (rows, cols, depth), (rows1, cols1, depth1)]
        + [Beside("gy", (rows * h // 8 + rows1 // 2, 8, depth))],
        corners, y_first, pairs, state,
        scratch=[(rows1, ec, depth), (depth1 // 128, rows1 * ec, 128)] + [(er, ec, depth)] * 2,
    )

    y_second = y_second.exchanged()
    between = [moved(right1, "gy", -k) for k in range(2, count - 1)]
    w_own, rdiag_own, w_x, sums = call(
        couplings1_kernel,
        [(3, rows1, wide, depth1), (rows1, wide, depth1), Beside("gx", (3 * H - 2, wide, depth1))]
        + [(8, depth1 // 2)],
        block, blocks, *blocks_between,
        near=(right1,), limit=limit,
    )
    w_x = w_x.exchanged()
    own, x_second = call(
        pack1_kernel,
        [(rows1, wide, depth1), Beside("gx", (H, wide, depth1))],
        y_second, right1, *between, rdiag_own,
        near=(kept,), limit=limit,
    )
    x_second = x_second.exchanged()
    v0_rows, v0_up, v0_down = call(pack_v_kernel, [(rows, ec, depth)] + [(h, ec, depth)] * 2, v0, y_second)
    tiles = h * (wide // 8 + ec // 8)
    kept1, x_third = call(
        pre1_kernel,
        [(7, er1, wide, depth1), Beside("gx", (tiles, 8, depth))],
        own, x_second, w_own, w_x, v0_up, v0_down,
        near=(kept,), limit=limit,
    )
    x_third = x_third.exchanged()
    (chunks,) = call(
        residual1_kernel,
        [(lax.axis_size("gx"), rows1 * wide // 4 + 1, depth1 // 2)],
        kept1, jnp.asarray(pair_table(depth1)), sums,
        scratch=[(rows1 // 2, wide, depth1), (depth1 // 256, rows1 // 2 * wide, 128)],
        limit=limit,
    )
    correction2 = coarse_correction(chunks, rows1 // 2, wide // 2, depth1 // 2)
    used = -(-(cols1 + 2 * h) // 8) * 8
    own, x_fourth = call(
        functools.partial(post1_kernel, cols=cols1),
        [(rows1, used, depth1), Beside("gx", (h, used, depth1))],
        kept1, x_third, correction2,
        scratch=[(er1, wide, depth1)],
        limit=limit,
    )
    x_fourth = x_fourth.exchanged()
    spread = jnp.asarray(np.ascontiguousarray(pair_table(depth).T))
    (v,) = call(inner_kernel, [(er, ec, depth)], v0_rows, x_third, own, kept, spread)
    (out,) = call(post_kernel, [(rows, cols, depth)], v, x_fourth, kept, spread, scratch=[(er, ec, depth)])
    return out


def solution(mesh):
    return jax.shard_map(
        shards,
        mesh=mesh,
        in_specs=(P("gx", "gy", None), P(None, "gx", "gy", None)),
        out_specs=P("gx", "gy", None),
        check_vma=False,
    )
```

```python
import functools
import math

import jax
import jax.numpy as jnp
import ml_dtypes
import numpy as np
from jax import lax
from jax.experimental import pallas as pl
from jax.experimental.pallas import tpu as pltpu
from jax.sharding import PartitionSpec as P

LEVELS = 3
SWEEPS = 2
MASS = 0.002
BOTH = ("gx", "gy")
H = 2 * SWEEPS
F32 = jnp.float32
UNROLL = 4
VMEM_LIMIT = 12 * 1024 * 1024
BF16 = jnp.bfloat16
VMEM = pl.BlockSpec(memory_space=pltpu.VMEM)
HBM = pl.BlockSpec(memory_space=pltpu.HBM)

CORNER0 = (
    (0, 1, 1), (0, 1, 2), (0, 1, 3), (1, 2, 3), (3, 1, 1), (3, 1, 2), (3, 1, 3), (2, 2, 3),
    (1, 1, 1), (1, 1, 2), (1, 1, 3), (1, 1, 4), (2, 1, 1), (2, 1, 2), (2, 1, 3), (2, 1, 4),
    (0, 2, 1), (0, 2, 2), (0, 3, 1), (1, 4, 1), (3, 2, 1), (3, 2, 2), (3, 3, 1), (2, 4, 1),
    (1, 2, 1), (1, 2, 2), (1, 3, 1), (1, 3, 2), (2, 2, 1), (2, 2, 2), (2, 3, 1), (2, 3, 2),
)

def moved(block, axis, distance):
    count = lax.axis_size(axis)
    return lax.ppermute(block, axis, [(i, (i + distance) % count) for i in range(count)])


class Beside:
    def __init__(self, axis, shape, outer=None, inner=None):
        self.axis, self.shape, self.outer, self.inner = axis, shape, outer, inner

    def exchanged(self):
        count = lax.axis_size(self.axis)
        assert count % 2 == 0
        got = []
        for block, first in ((self.outer, 1), (self.inner, 0)):
            route = []
            for i in range(first, count + first, 2):
                a, b = i % count, (i + 1) % count
                route += [(a, b), (b, a)]
            got.append(lax.ppermute(block, self.axis, route))
        return Beside(self.axis, self.shape, *got)


def call(kernel, out, *args, scratch=(), remote=(), limit=VMEM_LIMIT, near=()):
    flat, pairs_in, pairs_out, shapes = [], [], [], []
    for i, arg in enumerate(args):
        if isinstance(arg, Beside):
            pairs_in.append((len(flat), arg))
            flat += [arg.outer, arg.inner]
        else:
            flat.append(arg)
    for item in out:
        if isinstance(item, Beside):
            pairs_out.append((len(shapes), item))
            shapes += [item.shape] * 2
        else:
            shapes.append(item)
    count = len(flat)
    for item in near:
        flat += [item.outer, item.inner] if isinstance(item, Beside) else [item]
    total = len(flat)
    own = [pltpu.VMEM(p.shape, F32) for _, p in pairs_in + pairs_out for _ in range(2)]

    def body(*refs):
        refs_in, refs_out = list(refs[:count]), list(refs[total : total + len(shapes)])
        rest = list(refs[total + len(shapes) :])
        held, rest = rest[: len(own)], rest[len(own) :]
        sends = []
        for n, (i, pair) in enumerate(pairs_in + pairs_out):
            forward, backward = held[2 * n], held[2 * n + 1]
            is_in = n < len(pairs_in)
            refs_here = refs_in if is_in else refs_out
            outer, inner = refs_here[i], refs_here[i + 1]
            refs_here[i], refs_here[i + 1] = forward, backward
            if is_in:
                odd = lax.axis_index(pair.axis) & 1

                @pl.when(odd == 0)
                def _():
                    forward[...] = outer[...]
                    backward[...] = inner[...]

                @pl.when(odd == 1)
                def _():
                    forward[...] = inner[...]
                    backward[...] = outer[...]

            else:
                sends.append((pair.axis, outer, inner, forward, backward))
        kernel(*refs_in, *refs_out, *rest)
        for axis, outer, inner, forward, backward in sends:
            odd = lax.axis_index(axis) & 1

            @pl.when(odd == 0)
            def _():
                outer[...] = backward[...]
                inner[...] = forward[...]

            @pl.when(odd == 1)
            def _():
                outer[...] = forward[...]
                inner[...] = backward[...]

    results = pl.pallas_call(
        body,
        out_shape=[s if hasattr(s, "dtype") else jax.ShapeDtypeStruct(s, F32) for s in shapes],
        in_specs=[HBM if i in remote else VMEM for i in range(total)],
        out_specs=[VMEM] * len(shapes),
        scratch_shapes=own + [pltpu.VMEM(s, F32) if isinstance(s, tuple) else s for s in scratch],
        compiler_params=pltpu.CompilerParams(vmem_limit_bytes=limit),
    )(*flat)
    results, joined = list(results), []
    for item in out:
        if isinstance(item, Beside):
            joined.append(Beside(item.axis, item.shape, results.pop(0), results.pop(0)))
        else:
            joined.append(results.pop(0))
    return joined


def split3(x):
    high = x.astype(BF16)
    rest = x - high.astype(F32)
    middle = rest.astype(BF16)
    return high, middle, (rest - middle.astype(F32)).astype(BF16)


def dot(a, b):
    return jnp.dot(a, b, preferred_element_type=F32)


def dot_exact(x, table):
    high, middle, low = split3(x)
    return dot(high, table) + (dot(middle, table) + dot(low, table))


def pair_table(depth):
    table = np.zeros((depth, depth // 2), ml_dtypes.bfloat16)
    table[np.arange(depth), np.arange(depth) // 2] = 1
    return table


def put_tiles(tiles, x):
    for k in range(tiles.shape[0]):
        tiles[k, 0 : x.shape[0]] = x[:, 128 * k : 128 * k + 128]


def every_other(tiles, start, size):
    return jnp.concatenate(
        [tiles[k, pl.ds(start, size, stride=2), :] for k in range(tiles.shape[0])], axis=1
    )


def back(x, axis):
    return pltpu.roll(x, 1, axis)


def ahead(x, axis):
    return pltpu.roll(x, x.shape[axis] - 1, axis)


def parity2(shape):
    return (lax.broadcasted_iota(jnp.int32, shape, 0) + lax.broadcasted_iota(jnp.int32, shape, 1)) & 1


def row_sum(r, v, wx, wy, wz):
    centre = v[r]
    y, z = wy[r], wz[r]
    total = wx[r] * v[r + 1] + wx[r - 1] * v[r - 1]
    total = total + y * ahead(centre, 0) + back(y * centre, 0)
    return centre, total + z * ahead(centre, 1) + back(z * centre, 1)


def half_sweep(first, last, colour, parity, v, b, wx, wy, wz, rdiag):
    unroll = UNROLL if v.shape[-1] > 256 else last - first

    def body(r, carry):
        centre, total = row_sum(r, v, wx, wy, wz)
        mine = parity == ((r + colour) & 1)
        v[r] = jnp.where(mine, (b[r] + total) * rdiag[r], centre)
        return carry

    lax.fori_loop(first, last, body, 0, unroll=unroll)


def plane(src, face, a, r):
    return src[r] if a == 0 else face[a - 1, r].astype(F32)


def pack_y_kernel(src_in, face_in, to_right, to_left, src, face, sem):
    rows, cols, depth = src.shape
    copies = [pltpu.make_async_copy(src_in, src, sem.at[0]), pltpu.make_async_copy(face_in, face, sem.at[1])]
    for copy in copies:
        copy.start()
    for copy in copies:
        copy.wait()
    for out, base in ((to_right, cols - H), (to_left, 0)):
        for r in range(rows):
            for t, pair in enumerate(((0, 3), (1, 2))):
                for s, a in enumerate(pair):
                    value = plane(src, face, a, r)
                    if out is to_right and a == 3:
                        value_all = value + back(value, 1) + back(plane(src, face, 2, r), 0)
                        first = lax.broadcasted_iota(jnp.int32, value.shape, 0) == base
                        value = jnp.where(first, value_all, value)
                    out[2 * r + t, H * s : H * s + H] = value[base : base + H]


def pack_x_kernel(src, face, to_up, to_down):
    rows, cols, depth = src.shape
    tiles = cols // 8
    for out, base in ((to_up, rows - H), (to_down, 0)):
        for a in range(4):
            for k in range(H):
                value = plane(src, face, a, base + k)
                if out is to_up and a == 3 and k == 0:
                    value = value + back(value, 1) + plane(src, face, 1, base - 1)
                for t in range(tiles):
                    out[(a * H + k) * tiles + t] = value[8 * t : 8 * t + 8]


def coarsen_kernel(face, out, pairs, odds, tx):
    _, rows, cols, depth = face.shape
    fine = lax.broadcasted_iota(jnp.int32, pairs.shape, 0)
    coarse = 2 * lax.broadcasted_iota(jnp.int32, pairs.shape, 1)
    pairs[...] = jnp.where((fine & -2) == coarse, 1.0, 0.0).astype(BF16)
    odds[...] = jnp.where(fine == coarse + 1, 1.0, 0.0).astype(BF16)
    half, n = cols // 2, rows // 2

    def both(x):
        put_tiles(tx, x)
        return 0.0625 * (every_other(tx, 0, half) + every_other(tx, 1, half))

    for i in range(n):
        out[i] = both(dot(face[0, 2 * i + 1], pairs[...]))
        put_tiles(tx, dot(face[1, 2 * i], pairs[...]) + dot(face[1, 2 * i + 1], pairs[...]))
        out[n + i] = 0.0625 * every_other(tx, 1, half)
        out[2 * n + i] = both(dot(face[2, 2 * i], odds[...]) + dot(face[2, 2 * i + 1], odds[...]))


def forward_kernel(right, left, to_up, to_down, *, rows):
    tiles = to_up.shape[0] // 2
    place = {0: (0, 0), 3: (0, 1), 1: (1, 0), 2: (1, 1)}
    for msg, sy in ((right, 1), (left, -1)):
        start = 0 if sy > 0 else tiles
        for out, sx in ((to_up, 1), (to_down, -1)):
            for n, (a, dx, dy) in enumerate(CORNER0):
                r = rows - dx if sx > 0 else dx - 1
                t, s = place[a]
                s = H * s + (H - dy if sy > 0 else dy - 1)
                out[start + n // 8, n % 8 : n % 8 + 1] = msg[2 * r + t, s : s + 1]


def diagonal_row(r, parity, low_col, b, wx, wy, wz, diag, rdiag, v):
    y, z = wy[r], wz[r]
    if isinstance(r, int) and r == 0:
        total = MASS + wx[r] + z + y + back(y, 0)
    else:
        total = MASS + wx[r] + wx[r - 1] + y
        total = total + jnp.where(low_col, z, z + back(z, 1) + back(y, 0))
    diag[r] = total
    inverse = 1.0 / total
    rdiag[r] = inverse
    v[r] = jnp.where(parity == (r & 1), b[r] * inverse, 0.0)


def assemble_kernel(src, face, up, down, state):
    ext = [state.at[i] for i in range(4)]
    rows, cols, depth = src.shape
    for r in range(rows):
        ext[0][H + r, H : H + cols] = src[r]
        for d in range(3):
            ext[1 + d][H + r, H : H + cols] = face[d, r].astype(F32)
    tiles = cols // 8
    for msg, base in ((up, 0), (down, H + rows)):
        for a in range(4):
            for k in range(H):
                for t in range(tiles):
                    ext[a][base + k, H + 8 * t : H + 8 * t + 8] = msg[(a * H + k) * tiles + t]


def pre_kernel(up, down, right, left, pairs, state, kept, v_own, right1, to_right, to_left, *scratch):
    t512, t256, diag, v = scratch
    b, wx, wy, wz, rdiag = (kept.at[i] for i in range(5))
    kept[0:4] = state[...]
    ext = (b, wx, wy, wz)
    rows, cols, depth = v_own.shape
    er, ec = rows + 2 * H, cols + 2 * H
    rows1, cols1 = rows // 2, cols // 2
    for msg, base in ((right, 0), (left, H + cols)):
        for r in range(rows):
            for t, pair in enumerate(((0, 3), (1, 2))):
                for s, a in enumerate(pair):
                    ext[a][H + r, base : base + H] = msg[2 * r + t, H * s : H * s + H]
    tiles = len(CORNER0) // 8
    for msg, sx, sy in ((up, 1, 1), (up, 1, -1), (down, -1, 1), (down, -1, -1)):
        start = 0 if sy > 0 else tiles

        def at(distance, size, sign):
            return H - distance if sign > 0 else H + size + distance - 1

        for n, (a, dx, dy) in enumerate(CORNER0):
            r, c = at(dx, rows, sx), at(dy, cols, sy)
            ext[a][r, c : c + 1] = msg[start + n // 8, n % 8 : n % 8 + 1]
    parity = parity2((ec, depth))
    low_col = lax.broadcasted_iota(jnp.int32, (ec, depth), 0) == 0
    diagonal_row(0, parity, low_col, b, wx, wy, wz, diag, rdiag, v)

    def diagonal_body(r, carry):
        diagonal_row(r, parity, low_col, b, wx, wy, wz, diag, rdiag, v)
        return carry

    lax.fori_loop(1, er, diagonal_body, 0, unroll=UNROLL)
    half_sweep(1, er - 1, 1, parity, v, b, wx, wy, wz, rdiag)
    half_sweep(2, er - 2, 0, parity, v, b, wx, wy, wz, rdiag)
    half_sweep(3, er - 3, 1, parity, v, b, wx, wy, wz, rdiag)

    def residual_body(i, carry):
        total = 0.0
        for k in range(2):
            r = H + 2 * i + k
            centre, around = row_sum(r, v, wx, wy, wz)
            total = total + (b[r] - (diag[r] * centre - around))
        t512[i] = total
        return carry

    lax.fori_loop(0, rows1, residual_body, 0, unroll=UNROLL)
    put_tiles(t256, dot_exact(t512[...].reshape(rows1 * ec, depth), pairs[...]))
    for i in range(rows1):
        start = i * ec + H
        right1[i] = 0.125 * (every_other(t256, start, cols1) + every_other(t256, start + 1, cols1))

    start = to_right.shape[0] - rows1 // 2
    for i in range(rows1 // 2):
        to_right[start + i] = jnp.concatenate((right1[2 * i], right1[2 * i + 1]), axis=1)
        to_left[start + i] = to_right[start + i]

    own_parity = parity2((cols, depth))
    for r in range(rows):
        value = v[H + r, H : H + cols]
        v_own[r] = value
        value = jnp.where(own_parity == ((r + 1) & 1), value, ahead(value, 0))
        for p in range(H // 2):
            n = p * rows + r
            for out, base in ((to_right, cols - H), (to_left, 0)):
                out[n // 8, n % 8 : n % 8 + 1] = value[base + 2 * p : base + 2 * p + 1]


def pack_v_kernel(v0, right, left, v0_rows, to_up, to_down):
    rows, cols, depth = v0.shape
    for r in range(rows):
        v0_rows[r, H : H + cols] = v0[r]
        for msg, base in ((right, 0), (left, H + cols)):
            for p in range(H // 2):
                n = p * rows + r
                line = msg[n // 8, n % 8 : n % 8 + 1]
                v0_rows[r, base + 2 * p : base + 2 * p + 2] = jnp.broadcast_to(line, (2, depth))
    ec = v0_rows.shape[1]
    parity = parity2((ec, depth))
    for out, base in ((to_up, rows - H), (to_down, 0)):
        for k in range(H // 2):
            r = base + 2 * k
            out[k] = jnp.where(parity == ((r + 1) & 1), v0_rows[r], v0_rows[r + 1])


def before_kernel(x, up, down, pairs, out, tx):
    n, half, _ = x.shape
    tiles = 2 * half // 8
    start = (2 * H - 1) * tiles
    before = jnp.concatenate([up[start + t] for t in range(tiles)], axis=0)
    put_tiles(tx, dot(before.astype(BF16), pairs[...]))
    out[n] = 0.0625 * (every_other(tx, 0, half) + every_other(tx, 1, half))
    out[0:n] = x[...]


def couplings1_kernel(own, before_block, after_block, *refs):
    *between, w, rdiag, to_up, to_down, sums = refs
    blocks = [own, after_block, *between, before_block]
    planes, cols, depth = blocks[0].shape
    rows = planes // 3
    wide = cols * len(blocks)

    def plane(n):
        return jnp.concatenate([block[n] for block in blocks], axis=0)

    before = plane(3 * rows)
    for i in range(rows):
        x, y, z = plane(i), plane(rows + i), plane(2 * rows + i)
        w[0, i], w[1, i], w[2, i] = x, y, z
        rdiag[i] = 1.0 / (MASS + x + before + y + back(y, 0) + z + back(z, 1))
        before = x
    for d in range(3):
        for k in range(H - 1):
            to_up[d * (H - 1) + k] = w[d, rows - H + 1 + k]
            to_down[d * (H - 1) + k] = w[d, k]
    to_up[3 * (H - 1)] = w[0, rows - H]
    lane = lax.broadcasted_iota(jnp.int32, sums.shape, 1)
    row_odd = lax.broadcasted_iota(jnp.int32, (wide, depth), 0) & 1
    depth_odd = lax.broadcasted_iota(jnp.int32, (wide, depth), 1) & 1
    parts = [0.0, 0.0, 0.0]
    for i in range(rows):
        if i % 2 == 1:
            parts[0] = parts[0] + w[0, i]
        parts[1] = parts[1] + jnp.where(row_odd == 1, w[1, i], 0.0)
        parts[2] = parts[2] + jnp.where(depth_odd == 1, w[2, i], 0.0)
    line = jnp.zeros(sums.shape, F32)
    for d in range(3):
        line = jnp.where(lane == d, 0.0625 * jnp.sum(parts[d]), line)
    sums[...] = line


def pack1_kernel(right, left, own1, *refs):
    *between, rdiag, own, to_up, to_down = refs
    rows, cols, depth = own1.shape
    start = right.shape[0] - rows // 2
    for i in range(rows):
        lane = depth * (i % 2)
        parts = [own1[i], left[start + i // 2, :, lane : lane + depth]]
        parts += [block[i] for block in between]
        own[i] = jnp.concatenate(parts + [right[start + i // 2, :, lane : lane + depth]], axis=0)
    for k in range(H):
        value = own[rows - H + k]
        to_up[k] = value * rdiag[rows - H] if k == 0 else value
        value = own[k]
        to_down[k] = value * rdiag[k] if k == H - 1 else value


def pre1_kernel(own, up, down, w, w_up, w_down, v0_up, v0_down, kept, to_up, to_down):
    rows, wide, depth = own.shape
    er = rows + 2 * H
    wx, wy, wz, rdiag, b, v, diag = (kept.at[i] for i in range(7))
    b[0:H] = up[...]
    b[H : H + rows] = own[...]
    b[H + rows :] = down[...]
    for d in range(3):
        kept[d, H : H + rows] = w[d]
        kept[d, 1:H] = w_up[d * (H - 1) : (d + 1) * (H - 1)]
        kept[d, H + rows : er - 1] = w_down[d * (H - 1) : (d + 1) * (H - 1)]
    wx[0] = w_up[3 * (H - 1)]
    parity = parity2((wide, depth))
    for r in range(er):
        if 0 < r < er - 1:
            y, z = wy[r], wz[r]
            total = MASS + wx[r] + wx[r - 1] + y + back(y, 0) + z + back(z, 1)
            diag[r] = total
            inverse = 1.0 / total
            rdiag[r] = inverse
            first = b[r] * inverse
        else:
            first = b[r]
        v[r] = jnp.where(parity == (r & 1), first, 0.0)
    half_sweep(1, er - 1, 1, parity, v, b, wx, wy, wz, rdiag)
    half_sweep(2, er - 2, 0, parity, v, b, wx, wy, wz, rdiag)
    half_sweep(3, er - 3, 1, parity, v, b, wx, wy, wz, rdiag)
    for out, base, v0 in ((to_up, rows, v0_up), (to_down, H, v0_down)):
        n = 0
        for k in range(H // 2):
            value = jnp.concatenate((v[base + 2 * k], v[base + 2 * k + 1]), axis=1)
            for t in range(wide // 8):
                out[n] = value[8 * t : 8 * t + 8]
                n += 1
        for k in range(H // 2):
            for t in range(v0.shape[1] // 8):
                out[n] = v0[k, 8 * t : 8 * t + 8]
                n += 1


def residual1_kernel(kept1, pairs, sums, chunks, t256, t128):
    wx, wy, wz, _, b, v, diag = (kept1.at[i] for i in range(7))
    _, er, wide, depth = kept1.shape
    rows = er - 2 * H
    chunk = chunks.at[0]
    for i in range(rows // 2):
        total = 0.0
        for k in range(2):
            r = H + 2 * i + k
            centre, around = row_sum(r, v, wx, wy, wz)
            total = total + (b[r] - (diag[r] * centre - around))
        t256[i] = total
    n = rows // 2
    put_tiles(t128, dot_exact(t256[...].reshape(n * wide, depth), pairs[...]))
    half = wide // 2
    for i in range(n):
        start = i * wide
        chunk[i * half : (i + 1) * half] = 0.125 * (every_other(t128, start, half) + every_other(t128, start + 1, half))
    chunk[n * half : n * half + 1] = sums[0:1]
    for i in range(1, chunks.shape[0]):
        chunks[i] = chunk[...]


def split2(x):
    high = x.astype(BF16)
    return high, (x - high.astype(F32)).astype(BF16)


def dot_split(a, b):
    return dot(a[0], b[0]) + (dot(a[0], b[1]) + dot(a[1], b[0]))


def solve_kernel(got, table, out, *, count, start):
    devices, lines, depth = got.shape
    own = lines - 1
    cells = devices * own
    rx, ry, _ = out.shape

    def part(name, size, lane=0, width=None):
        return table[start[name] : start[name] + size, lane : lane + (width or table.shape[1])]

    values = jnp.concatenate([got[d, 0:own] for d in range(devices)], axis=0)
    sums = got[0, own : own + 1]
    for d in range(1, devices):
        sums = sums + got[d, own : own + 1]
    sums = sums * (1.0 / count)
    lam = MASS + sums[0:1, 0:1] * part("eig", cells, 0, depth)
    lam = lam + sums[0:1, 1:2] * part("eig", cells, depth, depth)
    lam = lam + sums[0:1, 2:3] * part("depth", 1, depth, depth)
    spec = dot_split(split2(values), split2(part("depth", depth, 0, depth)))
    spec = dot_split(split2(part("forward", cells)), split2(spec))
    spec = spec / (lam * float(count))
    spec = dot_split(split2(spec), split2(part("depth_out", depth)))
    step = -(-rx // 16) * 8
    along_x = table[pl.ds(pl.multiple_of(start["x"] + lax.axis_index("gx") * step, 8), step), :]
    along_y = part("y", ry // 2)
    back_table = jnp.concatenate([along_x[i : i + 1] * along_y for i in range(rx // 2)], axis=0)
    rows = dot_split(split2(back_table), split2(spec)).reshape(rx // 2, ry // 2, out.shape[2])
    for i in range(rx // 2):
        line = jnp.broadcast_to(rows[i][:, None, :], (ry // 2, 2, out.shape[2])).reshape(out.shape[1:])
        out[2 * i] = line
        out[2 * i + 1] = line


def post1_kernel(kept1, up, down, correction, own, to_up, to_down, v, *, cols):
    wx, wy, wz, rdiag, b, before, _ = (kept1.at[i] for i in range(7))
    er, wide, depth = before.shape
    rows = er - 2 * H
    for r in range(rows):
        v[H + r] = before[H + r] + correction[H + r]
    for msg, base in ((up, 0), (down, H + rows)):
        for k in range(H // 2):
            n = k * (wide // 8)
            value = jnp.concatenate([msg[n + t] for t in range(wide // 8)], axis=0)
            v[base + 2 * k] = value[:, :depth] + correction[base + 2 * k]
            v[base + 2 * k + 1] = value[:, depth:] + correction[base + 2 * k + 1]
    parity = parity2((wide, depth))
    half_sweep(1, er - 1, 0, parity, v, b, wx, wy, wz, rdiag)
    half_sweep(2, er - 2, 1, parity, v, b, wx, wy, wz, rdiag)
    half_sweep(3, er - 3, 0, parity, v, b, wx, wy, wz, rdiag)
    half_sweep(4, er - 4, 1, parity, v, b, wx, wy, wz, rdiag)
    h = H // 2
    used = cols + 2 * h
    for r in range(rows):
        value = v[H + r]
        own[r, 0:h] = value[wide - h :]
        own[r, h:used] = value[0 : cols + h]
        if used < own.shape[1]:
            own[r, used:] = jnp.zeros((own.shape[1] - used, depth), F32)
    to_up[...] = own[rows - h :]
    to_down[...] = own[0:h]


def spread_rows(lines, spread, used):
    rows, padded, _ = lines.shape
    wide = dot_exact(lines.reshape(rows * padded, lines.shape[2]), spread)
    depth = wide.shape[1]
    wide = wide.reshape(rows, padded, depth)
    out = []
    for n in range(rows):
        line = jnp.broadcast_to(wide[n, 0:used][:, None, :], (used, 2, depth))
        out.append(line.reshape(2 * used, depth))
    return out


def post_sweep(n, rows, v, kept, parity):
    b, wx, wy, wz, rdiag = (kept.at[i] for i in range(5))
    for first, last in rows:
        half_sweep(first, last, n % 2, parity, v, b, wx, wy, wz, rdiag)


def inner_kernel(v0_rows, up, down, own, kept, spread, v):
    er, ec, depth = v.shape
    rows = er - 2 * H
    tiles = ec // 8
    for msg, base in ((up, 0), (down, H + rows)):
        start = msg.shape[0] - (H // 2) * tiles
        for k in range(H // 2):
            for t in range(tiles):
                tile = msg[start + k * tiles + t]
                v[base + 2 * k, 8 * t : 8 * t + 8] = tile
                v[base + 2 * k + 1, 8 * t : 8 * t + 8] = tile
    for n, line in enumerate(spread_rows(own[...], spread[...], ec // 2)):
        v[H + 2 * n] = v0_rows[2 * n] + line
        v[H + 2 * n + 1] = v0_rows[2 * n + 1] + line
    parity = parity2((ec, depth))
    for n in range(H - 1):
        if H + 1 + n < er - H - 1 - n:
            post_sweep(n, ((H + 1 + n, er - H - 1 - n),), v, kept, parity)


def post_kernel(v_in, up1, down1, kept, spread, out, v):
    rows, cols, depth = out.shape
    er, ec = rows + 2 * H, cols + 2 * H
    v[H : H + rows] = v_in[H : H + rows]
    for msg, base in ((up1, 0), (down1, H + rows)):
        for n, line in enumerate(spread_rows(msg[...], spread[...], ec // 2)):
            v[base + 2 * n] = v_in[base + 2 * n] + line
            v[base + 2 * n + 1] = v_in[base + 2 * n + 1] + line
    parity = parity2((ec, depth))
    for n in range(H):
        low, high = H + 1 + n, er - H - 1 - n
        if n < H - 1 and low < high:
            post_sweep(n, ((1 + n, low), (high, er - 1 - n)), v, kept, parity)
        else:
            post_sweep(n, ((1 + n, er - 1 - n),), v, kept, parity)
    for r in range(rows):
        out[r] = v[H + r, H : H + cols]


def hartley(rows, columns, length):
    angle = (np.outer(rows, columns) % length) * (2.0 * math.pi / length)
    return np.cos(angle) + np.sin(angle)


def waves(length):
    return 2.0 * (1.0 - np.cos(np.arange(length) * (2.0 * math.pi / length)))


def windows(table, count, step, size):
    pad = -size % 8
    parts = [np.pad(table[i * step : i * step + size], ((0, pad), (0, 0))) for i in range(count)]
    return np.concatenate(parts)


def coarse_correction(chunks, rows, cols, depth):
    nx = lax.axis_size("gx")
    total_rows = rows * nx
    count = total_rows * cols * depth
    got = lax.all_to_all(chunks, "gx", 0, 0)
    out_rows = 2 * rows + 2 * H
    rows_ids = (np.arange(-H, 2 * total_rows + H) // 2) % total_rows
    table_x = hartley(rows_ids, np.arange(total_rows), total_rows)
    table_y = hartley(np.arange(2 * cols) // 2, np.arange(cols), cols)
    forward_x = hartley(np.arange(total_rows), np.arange(total_rows), total_rows)
    forward_y = hartley(np.arange(cols), np.arange(cols), cols)
    depth_in = hartley(np.arange(depth), np.arange(depth), depth)
    depth_out = np.repeat(depth_in, 2, axis=1)
    cells = total_rows * cols
    if cells <= 512 and cells == 2 * depth:
        ones = np.ones((1, depth))
        eig_x = np.repeat(waves(total_rows), cols)[:, None] * ones
        eig_y = np.tile(waves(cols), total_rows)[:, None] * ones
        eig_z = np.ones((depth, 1)) * waves(depth)[None, :]
        parts = {
            "forward": np.kron(forward_x, forward_y),
            "eig": np.concatenate((eig_x, eig_y), axis=1),
            "depth": np.concatenate((depth_in, eig_z), axis=1),
            "depth_out": depth_out,
            "x": windows(np.repeat(table_x[::2], cols, axis=1), nx, rows, out_rows // 2),
            "y": np.tile(forward_y, (1, total_rows)),
        }
        start, size = {}, 0
        for name, part in parts.items():
            start[name] = size
            size += part.shape[0]
            assert size % 8 == 0
        table = jnp.asarray(np.concatenate(list(parts.values())), F32)
        return call(
            functools.partial(solve_kernel, count=count, start=start),
            [(out_rows, 2 * cols, 2 * depth)],
            got, table,
        )[0]

    hi = lax.Precision.HIGHEST
    f32 = lambda x: jnp.asarray(x, F32)
    averages = jnp.sum(got[:, rows * cols, :3], axis=0) / count
    full = got[:, : rows * cols].reshape(total_rows, cols, depth)
    spec = jnp.einsum("abz,zk->abk", full, f32(depth_in), precision=hi)
    spec = jnp.einsum("ij,jbz->ibz", f32(forward_x), spec, precision=hi)
    spec = jnp.einsum("ij,ajz->aiz", f32(forward_y), spec, precision=hi)
    lam = (
        MASS
        + averages[0] * f32(waves(total_rows))[:, None, None]
        + averages[1] * f32(waves(cols))[None, :, None]
        + averages[2] * f32(waves(depth))[None, None, :]
    )
    spec = spec / (lam * float(count))
    own_x = lax.dynamic_slice_in_dim(f32(table_x), lax.axis_index("gx") * 2 * rows, out_rows, 0)
    out = jnp.einsum("ij,jbz->ibz", own_x, spec, precision=hi)
    out = jnp.einsum("ij,ajz->aiz", f32(table_y), out, precision=hi)
    return jnp.einsum("abz,zk->abk", out, f32(depth_out), precision=hi)


def gathered(block):
    return [block] + [moved(block, 0, -k) for k in range(1, lax.axis_size("gy"))]


def shards(source, face_coef):
    rows, cols, depth = source.shape
    rows1, cols1, depth1 = rows // 2, cols // 2, depth // 2
    er, ec, er1 = rows + 2 * H, cols + 2 * H, rows1 + 2 * H
    wide = cols1 * lax.axis_size("gy")
    h = H // 2
    limit = VMEM_LIMIT if wide * depth1 <= 8192 else 5 * VMEM_LIMIT

    count = lax.axis_size("gy")
    corner_tiles = len(CORNER0) // 8
    y_first, source, face_coef = call(
        pack_y_kernel,
        [Beside("gy", (2 * rows, 8, depth)), (rows, cols, depth), jax.ShapeDtypeStruct((3, rows, cols, depth), BF16)],
        source, face_coef,
        remote=(0, 1),
        scratch=[pltpu.SemaphoreType.DMA((2,))],
    )
    y_first = y_first.exchanged()
    (x_first,) = call(pack_x_kernel, [Beside("gx", (4 * H * (cols // 8), 8, depth))], source, face_coef)
    x_first = x_first.exchanged()
    block, pairs = call(
        coarsen_kernel,
        [(3 * rows1, cols1, depth1), jax.ShapeDtypeStruct((depth, depth1), BF16)],
        face_coef,
        near=(x_first,),
        scratch=[pltpu.VMEM((depth, depth1), BF16), (depth1 // 128, cols + 8, 128)],
    )
    (block,) = call(
        before_kernel,
        [(3 * rows1 + 1, cols1, depth1)],
        block, x_first, pairs,
        scratch=[(depth1 // 128, cols + 8, 128)],
    )
    (state,) = call(assemble_kernel, [(4, er, ec, depth)], source, face_coef, x_first)
    (corners,) = call(
        functools.partial(forward_kernel, rows=rows),
        [Beside("gx", (2 * corner_tiles, 8, depth))],
        y_first,
        near=(block, state),
    )
    corners = corners.exchanged()
    blocks = Beside("gy", block.shape, block, block).exchanged()
    blocks_between = [moved(block, "gy", -k) for k in range(2, count - 1)]
    kept, v0, right1, y_second = call(
        pre_kernel,
        [(5, er, ec, depth), (rows, cols, depth), (rows1, cols1, depth1)]
        + [Beside("gy", (rows * h // 8 + rows1 // 2, 8, depth))],
        corners, y_first, pairs, state,
        scratch=[(rows1, ec, depth), (depth1 // 128, rows1 * ec + 8, 128)] + [(er, ec, depth)] * 2,
    )

    y_second = y_second.exchanged()
    between = [moved(right1, "gy", -k) for k in range(2, count - 1)]
    w_own, rdiag_own, w_x, sums = call(
        couplings1_kernel,
        [(3, rows1, wide, depth1), (rows1, wide, depth1), Beside("gx", (3 * H - 2, wide, depth1))]
        + [(8, depth1 // 2)],
        block, blocks, *blocks_between,
        near=(right1,), limit=limit,
    )
    w_x = w_x.exchanged()
    own, x_second = call(
        pack1_kernel,
        [(rows1, wide, depth1), Beside("gx", (H, wide, depth1))],
        y_second, right1, *between, rdiag_own,
        near=(kept,), limit=limit,
    )
    x_second = x_second.exchanged()
    v0_rows, v0_up, v0_down = call(pack_v_kernel, [(rows, ec, depth)] + [(h, ec, depth)] * 2, v0, y_second)
    tiles = h * (wide // 8 + ec // 8)
    kept1, x_third = call(
        pre1_kernel,
        [(7, er1, wide, depth1), Beside("gx", (tiles, 8, depth))],
        own, x_second, w_own, w_x, v0_up, v0_down,
        near=(kept,), limit=limit,
    )
    x_third = x_third.exchanged()
    (chunks,) = call(
        residual1_kernel,
        [(lax.axis_size("gx"), rows1 * wide // 4 + 1, depth1 // 2)],
        kept1, jnp.asarray(pair_table(depth1)), sums,
        scratch=[(rows1 // 2, wide, depth1), (depth1 // 256, rows1 // 2 * wide + 8, 128)],
        limit=limit,
    )
    correction2 = coarse_correction(chunks, rows1 // 2, wide // 2, depth1 // 2)
    used = -(-(cols1 + 2 * h) // 8) * 8
    own, x_fourth = call(
        functools.partial(post1_kernel, cols=cols1),
        [(rows1, used, depth1), Beside("gx", (h, used, depth1))],
        kept1, x_third, correction2,
        scratch=[(er1, wide, depth1)],
        limit=limit,
    )
    x_fourth = x_fourth.exchanged()
    spread = jnp.asarray(np.ascontiguousarray(pair_table(depth).T))
    (v,) = call(inner_kernel, [(er, ec, depth)], v0_rows, x_third, own, kept, spread)
    (out,) = call(post_kernel, [(rows, cols, depth)], v, x_fourth, kept, spread, scratch=[(er, ec, depth)])
    return out


def solution(mesh):
    return jax.shard_map(
        shards,
        mesh=mesh,
        in_specs=(P("gx", "gy", None), P(None, "gx", "gy", None)),
        out_specs=P("gx", "gy", None),
        check_vma=False,
    )
```

```python
import functools
import math

import jax
import jax.numpy as jnp
import ml_dtypes
import numpy as np
from jax import lax
from jax.experimental import pallas as pl
from jax.experimental.pallas import tpu as pltpu
from jax.sharding import PartitionSpec as P

LEVELS = 3
SWEEPS = 2
MASS = 0.002
BOTH = ("gx", "gy")
H = 2 * SWEEPS
F32 = jnp.float32
UNROLL = 4
VMEM_LIMIT = 12 * 1024 * 1024
BF16 = jnp.bfloat16
VMEM = pl.BlockSpec(memory_space=pltpu.VMEM)
HBM = pl.BlockSpec(memory_space=pltpu.HBM)

CORNER0 = (
    (0, 1, 1), (0, 1, 2), (0, 1, 3), (1, 2, 3), (3, 1, 1), (3, 1, 2), (3, 1, 3), (2, 2, 3),
    (1, 1, 1), (1, 1, 2), (1, 1, 3), (1, 1, 4), (2, 1, 1), (2, 1, 2), (2, 1, 3), (2, 1, 4),
    (0, 2, 1), (0, 2, 2), (0, 3, 1), (1, 4, 1), (3, 2, 1), (3, 2, 2), (3, 3, 1), (2, 4, 1),
    (1, 2, 1), (1, 2, 2), (1, 3, 1), (1, 3, 2), (2, 2, 1), (2, 2, 2), (2, 3, 1), (2, 3, 2),
)

def moved(block, axis, distance):
    count = lax.axis_size(axis)
    return lax.ppermute(block, axis, [(i, (i + distance) % count) for i in range(count)])


class Beside:
    def __init__(self, axis, shape, outer=None, inner=None):
        self.axis, self.shape, self.outer, self.inner = axis, shape, outer, inner

    def exchanged(self):
        count = lax.axis_size(self.axis)
        assert count % 2 == 0
        got = []
        for block, first in ((self.outer, 1), (self.inner, 0)):
            route = []
            for i in range(first, count + first, 2):
                a, b = i % count, (i + 1) % count
                route += [(a, b), (b, a)]
            got.append(lax.ppermute(block, self.axis, route))
        return Beside(self.axis, self.shape, *got)


def call(kernel, out, *args, scratch=(), remote=(), limit=VMEM_LIMIT, near=()):
    flat, pairs_in, pairs_out, shapes = [], [], [], []
    for i, arg in enumerate(args):
        if isinstance(arg, Beside):
            pairs_in.append((len(flat), arg))
            flat += [arg.outer, arg.inner]
        else:
            flat.append(arg)
    for item in out:
        if isinstance(item, Beside):
            pairs_out.append((len(shapes), item))
            shapes += [item.shape] * 2
        else:
            shapes.append(item)
    count = len(flat)
    for item in near:
        flat += [item.outer, item.inner] if isinstance(item, Beside) else [item]
    total = len(flat)
    own = [pltpu.VMEM(p.shape, F32) for _, p in pairs_in + pairs_out for _ in range(2)]

    def body(*refs):
        refs_in, refs_out = list(refs[:count]), list(refs[total : total + len(shapes)])
        rest = list(refs[total + len(shapes) :])
        held, rest = rest[: len(own)], rest[len(own) :]
        sends = []
        for n, (i, pair) in enumerate(pairs_in + pairs_out):
            forward, backward = held[2 * n], held[2 * n + 1]
            is_in = n < len(pairs_in)
            refs_here = refs_in if is_in else refs_out
            outer, inner = refs_here[i], refs_here[i + 1]
            refs_here[i], refs_here[i + 1] = forward, backward
            if is_in:
                odd = lax.axis_index(pair.axis) & 1

                @pl.when(odd == 0)
                def _():
                    forward[...] = outer[...]
                    backward[...] = inner[...]

                @pl.when(odd == 1)
                def _():
                    forward[...] = inner[...]
                    backward[...] = outer[...]

            else:
                sends.append((pair.axis, outer, inner, forward, backward))
        kernel(*refs_in, *refs_out, *rest)
        for axis, outer, inner, forward, backward in sends:
            odd = lax.axis_index(axis) & 1

            @pl.when(odd == 0)
            def _():
                outer[...] = backward[...]
                inner[...] = forward[...]

            @pl.when(odd == 1)
            def _():
                outer[...] = forward[...]
                inner[...] = backward[...]

    results = pl.pallas_call(
        body,
        out_shape=[s if hasattr(s, "dtype") else jax.ShapeDtypeStruct(s, F32) for s in shapes],
        in_specs=[HBM if i in remote else VMEM for i in range(total)],
        out_specs=[VMEM] * len(shapes),
        scratch_shapes=own + [pltpu.VMEM(s, F32) if isinstance(s, tuple) else s for s in scratch],
        compiler_params=pltpu.CompilerParams(vmem_limit_bytes=limit),
    )(*flat)
    results, joined = list(results), []
    for item in out:
        if isinstance(item, Beside):
            joined.append(Beside(item.axis, item.shape, results.pop(0), results.pop(0)))
        else:
            joined.append(results.pop(0))
    return joined


def split3(x):
    high = x.astype(BF16)
    rest = x - high.astype(F32)
    middle = rest.astype(BF16)
    return high, middle, (rest - middle.astype(F32)).astype(BF16)


def dot(a, b):
    return jnp.dot(a, b, preferred_element_type=F32)


def dot_exact(x, table):
    high, middle, low = split3(x)
    return dot(high, table) + (dot(middle, table) + dot(low, table))


def pair_table(depth):
    table = np.zeros((depth, depth // 2), ml_dtypes.bfloat16)
    table[np.arange(depth), np.arange(depth) // 2] = 1
    return table


def put_tiles(tiles, x):
    for k in range(tiles.shape[0]):
        tiles[k, 0 : x.shape[0]] = x[:, 128 * k : 128 * k + 128]


def every_other(tiles, start, size):
    return jnp.concatenate(
        [tiles[k, pl.ds(start, size, stride=2), :] for k in range(tiles.shape[0])], axis=1
    )


def back(x, axis):
    return pltpu.roll(x, 1, axis)


def ahead(x, axis):
    return pltpu.roll(x, x.shape[axis] - 1, axis)


def parity2(shape):
    return (lax.broadcasted_iota(jnp.int32, shape, 0) + lax.broadcasted_iota(jnp.int32, shape, 1)) & 1


def row_sum(r, v, wx, wy, wz):
    centre = v[r]
    y, z = wy[r], wz[r]
    total = wx[r] * v[r + 1] + wx[r - 1] * v[r - 1]
    total = total + y * ahead(centre, 0) + back(y * centre, 0)
    return centre, total + z * ahead(centre, 1) + back(z * centre, 1)


def half_sweep(first, last, colour, parity, v, b, wx, wy, wz, rdiag):
    unroll = UNROLL if v.shape[-1] > 256 else last - first

    def body(r, carry):
        centre, total = row_sum(r, v, wx, wy, wz)
        mine = parity == ((r + colour) & 1)
        v[r] = jnp.where(mine, (b[r] + total) * rdiag[r], centre)
        return carry

    lax.fori_loop(first, last, body, 0, unroll=unroll)


def plane(src, face, a, r):
    return src[r] if a == 0 else face[a - 1, r].astype(F32)


def pack_y_kernel(src_in, face_in, to_right, to_left, src, face, sem):
    rows, cols, depth = src.shape
    copies = [pltpu.make_async_copy(src_in, src, sem.at[0]), pltpu.make_async_copy(face_in, face, sem.at[1])]
    for copy in copies:
        copy.start()
    for copy in copies:
        copy.wait()
    for out, base in ((to_right, cols - H), (to_left, 0)):
        for r in range(rows):
            for t, pair in enumerate(((0, 3), (1, 2))):
                for s, a in enumerate(pair):
                    value = plane(src, face, a, r)
                    if out is to_right and a == 3:
                        value_all = value + back(value, 1) + back(plane(src, face, 2, r), 0)
                        first = lax.broadcasted_iota(jnp.int32, value.shape, 0) == base
                        value = jnp.where(first, value_all, value)
                    out[2 * r + t, H * s : H * s + H] = value[base : base + H]


def pack_x_kernel(src, face, to_up, to_down):
    rows, cols, depth = src.shape
    tiles = cols // 8
    for out, base in ((to_up, rows - H), (to_down, 0)):
        for a in range(4):
            for k in range(H):
                value = plane(src, face, a, base + k)
                if out is to_up and a == 3 and k == 0:
                    value = value + back(value, 1) + plane(src, face, 1, base - 1)
                for t in range(tiles):
                    out[(a * H + k) * tiles + t] = value[8 * t : 8 * t + 8]


def coarsen_kernel(face, out, pairs, odds, tx):
    _, rows, cols, depth = face.shape
    fine = lax.broadcasted_iota(jnp.int32, pairs.shape, 0)
    coarse = 2 * lax.broadcasted_iota(jnp.int32, pairs.shape, 1)
    pairs[...] = jnp.where((fine & -2) == coarse, 1.0, 0.0).astype(BF16)
    odds[...] = jnp.where(fine == coarse + 1, 1.0, 0.0).astype(BF16)
    half, n = cols // 2, rows // 2

    def both(x):
        put_tiles(tx, x)
        return 0.0625 * (every_other(tx, 0, half) + every_other(tx, 1, half))

    for i in range(n):
        out[i] = both(dot(face[0, 2 * i + 1], pairs[...]))
        put_tiles(tx, dot(face[1, 2 * i], pairs[...]) + dot(face[1, 2 * i + 1], pairs[...]))
        out[n + i] = 0.0625 * every_other(tx, 1, half)
        out[2 * n + i] = both(dot(face[2, 2 * i], odds[...]) + dot(face[2, 2 * i + 1], odds[...]))


def forward_kernel(right, left, to_up, to_down, *, rows):
    tiles = to_up.shape[0] // 2
    place = {0: (0, 0), 3: (0, 1), 1: (1, 0), 2: (1, 1)}
    for msg, sy in ((right, 1), (left, -1)):
        start = 0 if sy > 0 else tiles
        for out, sx in ((to_up, 1), (to_down, -1)):
            for n, (a, dx, dy) in enumerate(CORNER0):
                r = rows - dx if sx > 0 else dx - 1
                t, s = place[a]
                s = H * s + (H - dy if sy > 0 else dy - 1)
                out[start + n // 8, n % 8 : n % 8 + 1] = msg[2 * r + t, s : s + 1]


def diagonal_row(r, parity, low_col, b, wx, wy, wz, diag, rdiag, v):
    y, z = wy[r], wz[r]
    if isinstance(r, int) and r == 0:
        total = MASS + wx[r] + z + y + back(y, 0)
    else:
        total = MASS + wx[r] + wx[r - 1] + y
        total = total + jnp.where(low_col, z, z + back(z, 1) + back(y, 0))
    diag[r] = total
    inverse = 1.0 / total
    rdiag[r] = inverse
    v[r] = jnp.where(parity == (r & 1), b[r] * inverse, 0.0)


def assemble_kernel(src, face, up, down, state):
    ext = [state.at[i] for i in range(4)]
    rows, cols, depth = src.shape
    for r in range(rows):
        ext[0][H + r, H : H + cols] = src[r]
        for d in range(3):
            ext[1 + d][H + r, H : H + cols] = face[d, r].astype(F32)
    tiles = cols // 8
    for msg, base in ((up, 0), (down, H + rows)):
        for a in range(4):
            for k in range(H):
                for t in range(tiles):
                    ext[a][base + k, H + 8 * t : H + 8 * t + 8] = msg[(a * H + k) * tiles + t]


def pre_kernel(up, down, right, left, pairs, state, kept, v_own, right1, to_right, to_left, *scratch):
    t512, t256, diag, v = scratch
    b, wx, wy, wz, rdiag = (kept.at[i] for i in range(5))
    kept[0:4] = state[...]
    ext = (b, wx, wy, wz)
    rows, cols, depth = v_own.shape
    er, ec = rows + 2 * H, cols + 2 * H
    rows1, cols1 = rows // 2, cols // 2
    for msg, base in ((right, 0), (left, H + cols)):
        for r in range(rows):
            for t, pair in enumerate(((0, 3), (1, 2))):
                for s, a in enumerate(pair):
                    ext[a][H + r, base : base + H] = msg[2 * r + t, H * s : H * s + H]
    tiles = len(CORNER0) // 8
    for msg, sx, sy in ((up, 1, 1), (up, 1, -1), (down, -1, 1), (down, -1, -1)):
        start = 0 if sy > 0 else tiles

        def at(distance, size, sign):
            return H - distance if sign > 0 else H + size + distance - 1

        for n, (a, dx, dy) in enumerate(CORNER0):
            r, c = at(dx, rows, sx), at(dy, cols, sy)
            ext[a][r, c : c + 1] = msg[start + n // 8, n % 8 : n % 8 + 1]
    parity = parity2((ec, depth))
    low_col = lax.broadcasted_iota(jnp.int32, (ec, depth), 0) == 0
    diagonal_row(0, parity, low_col, b, wx, wy, wz, diag, rdiag, v)

    def diagonal_body(r, carry):
        diagonal_row(r, parity, low_col, b, wx, wy, wz, diag, rdiag, v)
        return carry

    lax.fori_loop(1, er, diagonal_body, 0, unroll=UNROLL)
    half_sweep(1, er - 1, 1, parity, v, b, wx, wy, wz, rdiag)
    half_sweep(2, er - 2, 0, parity, v, b, wx, wy, wz, rdiag)
    half_sweep(3, er - 3, 1, parity, v, b, wx, wy, wz, rdiag)

    def residual_body(i, carry):
        total = 0.0
        for k in range(2):
            r = H + 2 * i + k
            centre, around = row_sum(r, v, wx, wy, wz)
            total = total + (b[r] - (diag[r] * centre - around))
        t512[i] = total
        return carry

    lax.fori_loop(0, rows1, residual_body, 0, unroll=UNROLL)
    put_tiles(t256, dot_exact(t512[...].reshape(rows1 * ec, depth), pairs[...]))
    for i in range(rows1):
        start = i * ec + H
        right1[i] = 0.125 * (every_other(t256, start, cols1) + every_other(t256, start + 1, cols1))

    start = to_right.shape[0] - rows1 // 2
    for i in range(rows1 // 2):
        to_right[start + i] = jnp.concatenate((right1[2 * i], right1[2 * i + 1]), axis=1)
        to_left[start + i] = to_right[start + i]

    own_parity = parity2((cols, depth))
    for r in range(rows):
        value = v[H + r, H : H + cols]
        v_own[r] = value
        value = jnp.where(own_parity == ((r + 1) & 1), value, ahead(value, 0))
        for p in range(H // 2):
            n = p * rows + r
            for out, base in ((to_right, cols - H), (to_left, 0)):
                out[n // 8, n % 8 : n % 8 + 1] = value[base + 2 * p : base + 2 * p + 1]


def pack_v_kernel(v0, right, left, v0_rows, to_up, to_down):
    rows, cols, depth = v0.shape
    for r in range(rows):
        v0_rows[r, H : H + cols] = v0[r]
        for msg, base in ((right, 0), (left, H + cols)):
            for p in range(H // 2):
                n = p * rows + r
                line = msg[n // 8, n % 8 : n % 8 + 1]
                v0_rows[r, base + 2 * p : base + 2 * p + 2] = jnp.broadcast_to(line, (2, depth))
    ec = v0_rows.shape[1]
    parity = parity2((ec, depth))
    for out, base in ((to_up, rows - H), (to_down, 0)):
        for k in range(H // 2):
            r = base + 2 * k
            out[k] = jnp.where(parity == ((r + 1) & 1), v0_rows[r], v0_rows[r + 1])


def before_kernel(x, up, down, pairs, out, tx):
    n, half, _ = x.shape
    tiles = 2 * half // 8
    start = (2 * H - 1) * tiles
    before = jnp.concatenate([up[start + t] for t in range(tiles)], axis=0)
    put_tiles(tx, dot(before.astype(BF16), pairs[...]))
    out[n] = 0.0625 * (every_other(tx, 0, half) + every_other(tx, 1, half))
    out[0:n] = x[...]


def couplings1_kernel(own, before_block, after_block, *refs):
    *between, w, rdiag, to_up, to_down, sums = refs
    blocks = [own, after_block, *between, before_block]
    planes, cols, depth = blocks[0].shape
    rows = planes // 3
    wide = cols * len(blocks)

    def plane(n):
        return jnp.concatenate([block[n] for block in blocks], axis=0)

    before = plane(3 * rows)
    for i in range(rows):
        x, y, z = plane(i), plane(rows + i), plane(2 * rows + i)
        w[0, i], w[1, i], w[2, i] = x, y, z
        rdiag[i] = 1.0 / (MASS + x + before + y + back(y, 0) + z + back(z, 1))
        before = x
    for d in range(3):
        for k in range(H - 1):
            to_up[d * (H - 1) + k] = w[d, rows - H + 1 + k]
            to_down[d * (H - 1) + k] = w[d, k]
    to_up[3 * (H - 1)] = w[0, rows - H]
    lane = lax.broadcasted_iota(jnp.int32, sums.shape, 1)
    row_odd = lax.broadcasted_iota(jnp.int32, (wide, depth), 0) & 1
    depth_odd = lax.broadcasted_iota(jnp.int32, (wide, depth), 1) & 1
    parts = [0.0, 0.0, 0.0]
    for i in range(rows):
        if i % 2 == 1:
            parts[0] = parts[0] + w[0, i]
        parts[1] = parts[1] + jnp.where(row_odd == 1, w[1, i], 0.0)
        parts[2] = parts[2] + jnp.where(depth_odd == 1, w[2, i], 0.0)
    line = jnp.zeros(sums.shape, F32)
    for d in range(3):
        line = jnp.where(lane == d, 0.0625 * jnp.sum(parts[d]), line)
    sums[...] = line


def pack1_kernel(right, left, own1, *refs):
    *between, rdiag, own, to_up, to_down = refs
    rows, cols, depth = own1.shape
    start = right.shape[0] - rows // 2
    for i in range(rows):
        lane = depth * (i % 2)
        parts = [own1[i], left[start + i // 2, :, lane : lane + depth]]
        parts += [block[i] for block in between]
        own[i] = jnp.concatenate(parts + [right[start + i // 2, :, lane : lane + depth]], axis=0)
    for k in range(H):
        value = own[rows - H + k]
        to_up[k] = value * rdiag[rows - H] if k == 0 else value
        value = own[k]
        to_down[k] = value * rdiag[k] if k == H - 1 else value


def pre1_kernel(own, up, down, w, w_up, w_down, v0_up, v0_down, kept, to_up, to_down):
    rows, wide, depth = own.shape
    er = rows + 2 * H
    wx, wy, wz, rdiag, b, v, diag = (kept.at[i] for i in range(7))
    b[0:H] = up[...]
    b[H : H + rows] = own[...]
    b[H + rows :] = down[...]
    for d in range(3):
        kept[d, H : H + rows] = w[d]
        kept[d, 1:H] = w_up[d * (H - 1) : (d + 1) * (H - 1)]
        kept[d, H + rows : er - 1] = w_down[d * (H - 1) : (d + 1) * (H - 1)]
    wx[0] = w_up[3 * (H - 1)]
    parity = parity2((wide, depth))
    for r in range(er):
        if 0 < r < er - 1:
            y, z = wy[r], wz[r]
            total = MASS + wx[r] + wx[r - 1] + y + back(y, 0) + z + back(z, 1)
            diag[r] = total
            inverse = 1.0 / total
            rdiag[r] = inverse
            first = b[r] * inverse
        else:
            first = b[r]
        v[r] = jnp.where(parity == (r & 1), first, 0.0)
    half_sweep(1, er - 1, 1, parity, v, b, wx, wy, wz, rdiag)
    half_sweep(2, er - 2, 0, parity, v, b, wx, wy, wz, rdiag)
    half_sweep(3, er - 3, 1, parity, v, b, wx, wy, wz, rdiag)
    for out, base, v0 in ((to_up, rows, v0_up), (to_down, H, v0_down)):
        n = 0
        for k in range(H // 2):
            value = jnp.concatenate((v[base + 2 * k], v[base + 2 * k + 1]), axis=1)
            for t in range(wide // 8):
                out[n] = value[8 * t : 8 * t + 8]
                n += 1
        for k in range(H // 2):
            for t in range(v0.shape[1] // 8):
                out[n] = v0[k, 8 * t : 8 * t + 8]
                n += 1


def residual1_kernel(kept1, pairs, sums, chunks, t256, t128):
    wx, wy, wz, _, b, v, diag = (kept1.at[i] for i in range(7))
    _, er, wide, depth = kept1.shape
    rows = er - 2 * H
    chunk = chunks.at[0]
    for i in range(rows // 2):
        total = 0.0
        for k in range(2):
            r = H + 2 * i + k
            centre, around = row_sum(r, v, wx, wy, wz)
            total = total + (b[r] - (diag[r] * centre - around))
        t256[i] = total
    n = rows // 2
    put_tiles(t128, dot_exact(t256[...].reshape(n * wide, depth), pairs[...]))
    half = wide // 2
    for i in range(n):
        start = i * wide
        chunk[i * half : (i + 1) * half] = 0.125 * (every_other(t128, start, half) + every_other(t128, start + 1, half))
    chunk[n * half : n * half + 1] = sums[0:1]
    for i in range(1, chunks.shape[0]):
        chunks[i] = chunk[...]


def split2(x):
    high = x.astype(BF16)
    return high, (x - high.astype(F32)).astype(BF16)


def dot_split(a, b):
    return dot(a[0], b[0]) + (dot(a[0], b[1]) + dot(a[1], b[0]))


def solve_kernel(got, table, out, *, count, start):
    devices, lines, depth = got.shape
    own = lines - 1
    cells = devices * own
    rx, ry, _ = out.shape

    def part(name, size, lane=0, width=None):
        return table[start[name] : start[name] + size, lane : lane + (width or table.shape[1])]

    values = jnp.concatenate([got[d, 0:own] for d in range(devices)], axis=0)
    sums = got[0, own : own + 1]
    for d in range(1, devices):
        sums = sums + got[d, own : own + 1]
    sums = sums * (1.0 / count)
    lam = MASS + sums[0:1, 0:1] * part("eig", cells, 0, depth)
    lam = lam + sums[0:1, 1:2] * part("eig", cells, depth, depth)
    lam = lam + sums[0:1, 2:3] * part("depth", 1, depth, depth)
    spec = dot_split(split2(values), split2(part("depth", depth, 0, depth)))
    spec = dot_split(split2(part("forward", cells)), split2(spec))
    spec = spec / (lam * float(count))
    spec = dot_split(split2(spec), split2(part("depth_out", depth)))
    step = -(-rx // 16) * 8
    along_x = table[pl.ds(pl.multiple_of(start["x"] + lax.axis_index("gx") * step, 8), step), :]
    along_y = part("y", ry // 2)
    back_table = jnp.concatenate([along_x[i : i + 1] * along_y for i in range(rx // 2)], axis=0)
    rows = dot_split(split2(back_table), split2(spec)).reshape(rx // 2, ry // 2, out.shape[2])
    for i in range(rx // 2):
        line = jnp.broadcast_to(rows[i][:, None, :], (ry // 2, 2, out.shape[2])).reshape(out.shape[1:])
        out[2 * i] = line
        out[2 * i + 1] = line


def post1_kernel(kept1, up, down, correction, own, to_up, to_down, v, *, cols):
    wx, wy, wz, rdiag, b, before, _ = (kept1.at[i] for i in range(7))
    er, wide, depth = before.shape
    rows = er - 2 * H
    for r in range(rows):
        v[H + r] = before[H + r] + correction[H + r]
    for msg, base in ((up, 0), (down, H + rows)):
        for k in range(H // 2):
            n = k * (wide // 8)
            value = jnp.concatenate([msg[n + t] for t in range(wide // 8)], axis=0)
            v[base + 2 * k] = value[:, :depth] + correction[base + 2 * k]
            v[base + 2 * k + 1] = value[:, depth:] + correction[base + 2 * k + 1]
    parity = parity2((wide, depth))
    half_sweep(1, er - 1, 0, parity, v, b, wx, wy, wz, rdiag)
    half_sweep(2, er - 2, 1, parity, v, b, wx, wy, wz, rdiag)
    half_sweep(3, er - 3, 0, parity, v, b, wx, wy, wz, rdiag)
    half_sweep(4, er - 4, 1, parity, v, b, wx, wy, wz, rdiag)
    h = H // 2
    used = cols + 2 * h
    for r in range(rows):
        value = v[H + r]
        own[r, 0:h] = value[wide - h :]
        own[r, h:used] = value[0 : cols + h]
        if used < own.shape[1]:
            own[r, used:] = jnp.zeros((own.shape[1] - used, depth), F32)
    to_up[...] = own[rows - h :]
    to_down[...] = own[0:h]


def solve_post1_kernel(kept1, up, down, got, table, own, to_up, to_down, v, correction, *, cols, count, start):
    solve_kernel(got, table, correction, count=count, start=start)
    post1_kernel(kept1, up, down, correction, own, to_up, to_down, v, cols=cols)


def spread_rows(lines, spread, used):
    rows, padded, _ = lines.shape
    wide = dot_exact(lines.reshape(rows * padded, lines.shape[2]), spread)
    depth = wide.shape[1]
    wide = wide.reshape(rows, padded, depth)
    out = []
    for n in range(rows):
        line = jnp.broadcast_to(wide[n, 0:used][:, None, :], (used, 2, depth))
        out.append(line.reshape(2 * used, depth))
    return out


def post_sweep(n, rows, v, kept, parity):
    b, wx, wy, wz, rdiag = (kept.at[i] for i in range(5))
    for first, last in rows:
        half_sweep(first, last, n % 2, parity, v, b, wx, wy, wz, rdiag)


def inner_kernel(v0_rows, up, down, own, kept, spread, v):
    er, ec, depth = v.shape
    rows = er - 2 * H
    tiles = ec // 8
    for msg, base in ((up, 0), (down, H + rows)):
        start = msg.shape[0] - (H // 2) * tiles
        for k in range(H // 2):
            for t in range(tiles):
                tile = msg[start + k * tiles + t]
                v[base + 2 * k, 8 * t : 8 * t + 8] = tile
                v[base + 2 * k + 1, 8 * t : 8 * t + 8] = tile
    for n, line in enumerate(spread_rows(own[...], spread[...], ec // 2)):
        v[H + 2 * n] = v0_rows[2 * n] + line
        v[H + 2 * n + 1] = v0_rows[2 * n + 1] + line
    parity = parity2((ec, depth))
    for n in range(H - 1):
        if H + 1 + n < er - H - 1 - n:
            post_sweep(n, ((H + 1 + n, er - H - 1 - n),), v, kept, parity)


def post_kernel(v_in, up1, down1, kept, spread, out, v):
    rows, cols, depth = out.shape
    er, ec = rows + 2 * H, cols + 2 * H
    v[H : H + rows] = v_in[H : H + rows]
    for msg, base in ((up1, 0), (down1, H + rows)):
        for n, line in enumerate(spread_rows(msg[...], spread[...], ec // 2)):
            v[base + 2 * n] = v_in[base + 2 * n] + line
            v[base + 2 * n + 1] = v_in[base + 2 * n + 1] + line
    parity = parity2((ec, depth))
    for n in range(H):
        low, high = H + 1 + n, er - H - 1 - n
        if n < H - 1 and low < high:
            post_sweep(n, ((1 + n, low), (high, er - 1 - n)), v, kept, parity)
        else:
            post_sweep(n, ((1 + n, er - 1 - n),), v, kept, parity)
    for r in range(rows):
        out[r] = v[H + r, H : H + cols]


def hartley(rows, columns, length):
    angle = (np.outer(rows, columns) % length) * (2.0 * math.pi / length)
    return np.cos(angle) + np.sin(angle)


def waves(length):
    return 2.0 * (1.0 - np.cos(np.arange(length) * (2.0 * math.pi / length)))


def windows(table, count, step, size):
    pad = -size % 8
    parts = [np.pad(table[i * step : i * step + size], ((0, pad), (0, 0))) for i in range(count)]
    return np.concatenate(parts)


def coarse_correction(chunks, rows, cols, depth):
    nx = lax.axis_size("gx")
    total_rows = rows * nx
    count = total_rows * cols * depth
    got = lax.all_to_all(chunks, "gx", 0, 0)
    out_rows = 2 * rows + 2 * H
    rows_ids = (np.arange(-H, 2 * total_rows + H) // 2) % total_rows
    table_x = hartley(rows_ids, np.arange(total_rows), total_rows)
    table_y = hartley(np.arange(2 * cols) // 2, np.arange(cols), cols)
    forward_x = hartley(np.arange(total_rows), np.arange(total_rows), total_rows)
    forward_y = hartley(np.arange(cols), np.arange(cols), cols)
    depth_in = hartley(np.arange(depth), np.arange(depth), depth)
    depth_out = np.repeat(depth_in, 2, axis=1)
    cells = total_rows * cols
    if cells <= 512 and cells == 2 * depth:
        ones = np.ones((1, depth))
        eig_x = np.repeat(waves(total_rows), cols)[:, None] * ones
        eig_y = np.tile(waves(cols), total_rows)[:, None] * ones
        eig_z = np.ones((depth, 1)) * waves(depth)[None, :]
        parts = {
            "forward": np.kron(forward_x, forward_y),
            "eig": np.concatenate((eig_x, eig_y), axis=1),
            "depth": np.concatenate((depth_in, eig_z), axis=1),
            "depth_out": depth_out,
            "x": windows(np.repeat(table_x[::2], cols, axis=1), nx, rows, out_rows // 2),
            "y": np.tile(forward_y, (1, total_rows)),
        }
        start, size = {}, 0
        for name, part in parts.items():
            start[name] = size
            size += part.shape[0]
            assert size % 8 == 0
        table = jnp.asarray(np.concatenate(list(parts.values())), F32)
        kernel = functools.partial(solve_post1_kernel, count=count, start=start)
        return kernel, (got, table), [(out_rows, 2 * cols, 2 * depth)]

    hi = lax.Precision.HIGHEST
    f32 = lambda x: jnp.asarray(x, F32)
    averages = jnp.sum(got[:, rows * cols, :3], axis=0) / count
    full = got[:, : rows * cols].reshape(total_rows, cols, depth)
    spec = jnp.einsum("abz,zk->abk", full, f32(depth_in), precision=hi)
    spec = jnp.einsum("ij,jbz->ibz", f32(forward_x), spec, precision=hi)
    spec = jnp.einsum("ij,ajz->aiz", f32(forward_y), spec, precision=hi)
    lam = (
        MASS
        + averages[0] * f32(waves(total_rows))[:, None, None]
        + averages[1] * f32(waves(cols))[None, :, None]
        + averages[2] * f32(waves(depth))[None, None, :]
    )
    spec = spec / (lam * float(count))
    own_x = lax.dynamic_slice_in_dim(f32(table_x), lax.axis_index("gx") * 2 * rows, out_rows, 0)
    out = jnp.einsum("ij,jbz->ibz", own_x, spec, precision=hi)
    out = jnp.einsum("ij,ajz->aiz", f32(table_y), out, precision=hi)
    return post1_kernel, (jnp.einsum("abz,zk->abk", out, f32(depth_out), precision=hi),), []


def gathered(block):
    return [block] + [moved(block, 0, -k) for k in range(1, lax.axis_size("gy"))]


def shards(source, face_coef):
    rows, cols, depth = source.shape
    rows1, cols1, depth1 = rows // 2, cols // 2, depth // 2
    er, ec, er1 = rows + 2 * H, cols + 2 * H, rows1 + 2 * H
    wide = cols1 * lax.axis_size("gy")
    h = H // 2
    limit = VMEM_LIMIT if wide * depth1 <= 8192 else 5 * VMEM_LIMIT

    count = lax.axis_size("gy")
    corner_tiles = len(CORNER0) // 8
    y_first, source, face_coef = call(
        pack_y_kernel,
        [Beside("gy", (2 * rows, 8, depth)), (rows, cols, depth), jax.ShapeDtypeStruct((3, rows, cols, depth), BF16)],
        source, face_coef,
        remote=(0, 1),
        scratch=[pltpu.SemaphoreType.DMA((2,))],
    )
    y_first = y_first.exchanged()
    (x_first,) = call(pack_x_kernel, [Beside("gx", (4 * H * (cols // 8), 8, depth))], source, face_coef)
    x_first = x_first.exchanged()
    block, pairs = call(
        coarsen_kernel,
        [(3 * rows1, cols1, depth1), jax.ShapeDtypeStruct((depth, depth1), BF16)],
        face_coef,
        near=(x_first,),
        scratch=[pltpu.VMEM((depth, depth1), BF16), (depth1 // 128, cols + 8, 128)],
    )
    (block,) = call(
        before_kernel,
        [(3 * rows1 + 1, cols1, depth1)],
        block, x_first, pairs,
        scratch=[(depth1 // 128, cols + 8, 128)],
    )
    (state,) = call(assemble_kernel, [(4, er, ec, depth)], source, face_coef, x_first)
    (corners,) = call(
        functools.partial(forward_kernel, rows=rows),
        [Beside("gx", (2 * corner_tiles, 8, depth))],
        y_first,
        near=(block, state),
    )
    corners = corners.exchanged()
    blocks = Beside("gy", block.shape, block, block).exchanged()
    blocks_between = [moved(block, "gy", -k) for k in range(2, count - 1)]
    kept, v0, right1, y_second = call(
        pre_kernel,
        [(5, er, ec, depth), (rows, cols, depth), (rows1, cols1, depth1)]
        + [Beside("gy", (rows * h // 8 + rows1 // 2, 8, depth))],
        corners, y_first, pairs, state,
        scratch=[(rows1, ec, depth), (depth1 // 128, rows1 * ec + 8, 128)] + [(er, ec, depth)] * 2,
    )

    y_second = y_second.exchanged()
    between = [moved(right1, "gy", -k) for k in range(2, count - 1)]
    w_own, rdiag_own, w_x, sums = call(
        couplings1_kernel,
        [(3, rows1, wide, depth1), (rows1, wide, depth1), Beside("gx", (3 * H - 2, wide, depth1))]
        + [(8, depth1 // 2)],
        block, blocks, *blocks_between,
        near=(right1,), limit=limit,
    )
    w_x = w_x.exchanged()
    own, x_second = call(
        pack1_kernel,
        [(rows1, wide, depth1), Beside("gx", (H, wide, depth1))],
        y_second, right1, *between, rdiag_own,
        near=(kept,), limit=limit,
    )
    x_second = x_second.exchanged()
    v0_rows, v0_up, v0_down = call(pack_v_kernel, [(rows, ec, depth)] + [(h, ec, depth)] * 2, v0, y_second)
    tiles = h * (wide // 8 + ec // 8)
    kept1, x_third = call(
        pre1_kernel,
        [(7, er1, wide, depth1), Beside("gx", (tiles, 8, depth))],
        own, x_second, w_own, w_x, v0_up, v0_down,
        near=(kept,), limit=limit,
    )
    x_third = x_third.exchanged()
    (chunks,) = call(
        residual1_kernel,
        [(lax.axis_size("gx"), rows1 * wide // 4 + 1, depth1 // 2)],
        kept1, jnp.asarray(pair_table(depth1)), sums,
        scratch=[(rows1 // 2, wide, depth1), (depth1 // 256, rows1 // 2 * wide + 8, 128)],
        limit=limit,
    )
    kernel, operands, held = coarse_correction(chunks, rows1 // 2, wide // 2, depth1 // 2)
    used = -(-(cols1 + 2 * h) // 8) * 8
    own, x_fourth = call(
        functools.partial(kernel, cols=cols1),
        [(rows1, used, depth1), Beside("gx", (h, used, depth1))],
        kept1, x_third, *operands,
        scratch=[(er1, wide, depth1)] + held,
        limit=limit,
    )
    x_fourth = x_fourth.exchanged()
    spread = jnp.asarray(np.ascontiguousarray(pair_table(depth).T))
    (v,) = call(inner_kernel, [(er, ec, depth)], v0_rows, x_third, own, kept, spread)
    (out,) = call(post_kernel, [(rows, cols, depth)], v, x_fourth, kept, spread, scratch=[(er, ec, depth)])
    return out


def solution(mesh):
    return jax.shard_map(
        shards,
        mesh=mesh,
        in_specs=(P("gx", "gy", None), P(None, "gx", "gy", None)),
        out_specs=P("gx", "gy", None),
        check_vma=False,
    )
```

```python
import functools
import math

import jax
import jax.numpy as jnp
import ml_dtypes
import numpy as np
from jax import lax
from jax.experimental import pallas as pl
from jax.experimental.pallas import tpu as pltpu
from jax.sharding import PartitionSpec as P

LEVELS = 3
SWEEPS = 2
MASS = 0.002
BOTH = ("gx", "gy")
H = 2 * SWEEPS
F32 = jnp.float32
UNROLL = 4
VMEM_LIMIT = 12 * 1024 * 1024
BF16 = jnp.bfloat16
VMEM = pl.BlockSpec(memory_space=pltpu.VMEM)
HBM = pl.BlockSpec(memory_space=pltpu.HBM)

CORNER0 = (
    (0, 1, 1), (0, 1, 2), (0, 1, 3), (1, 2, 3), (3, 1, 1), (3, 1, 2), (3, 1, 3), (2, 2, 3),
    (1, 1, 1), (1, 1, 2), (1, 1, 3), (1, 1, 4), (2, 1, 1), (2, 1, 2), (2, 1, 3), (2, 1, 4),
    (0, 2, 1), (0, 2, 2), (0, 3, 1), (1, 4, 1), (3, 2, 1), (3, 2, 2), (3, 3, 1), (2, 4, 1),
    (1, 2, 1), (1, 2, 2), (1, 3, 1), (1, 3, 2), (2, 2, 1), (2, 2, 2), (2, 3, 1), (2, 3, 2),
)

def moved(block, axis, distance):
    count = lax.axis_size(axis)
    return lax.ppermute(block, axis, [(i, (i + distance) % count) for i in range(count)])


class Beside:
    def __init__(self, axis, shape, outer=None, inner=None):
        self.axis, self.shape, self.outer, self.inner = axis, shape, outer, inner

    def exchanged(self):
        count = lax.axis_size(self.axis)
        assert count % 2 == 0
        got = []
        for block, first in ((self.outer, 1), (self.inner, 0)):
            route = []
            for i in range(first, count + first, 2):
                a, b = i % count, (i + 1) % count
                route += [(a, b), (b, a)]
            got.append(lax.ppermute(block, self.axis, route))
        return Beside(self.axis, self.shape, *got)


def call(kernel, out, *args, scratch=(), remote=(), limit=VMEM_LIMIT, near=()):
    flat, pairs_in, pairs_out, shapes = [], [], [], []
    for i, arg in enumerate(args):
        if isinstance(arg, Beside):
            pairs_in.append((len(flat), arg))
            flat += [arg.outer, arg.inner]
        else:
            flat.append(arg)
    for item in out:
        if isinstance(item, Beside):
            pairs_out.append((len(shapes), item))
            shapes += [item.shape] * 2
        else:
            shapes.append(item)
    count = len(flat)
    for item in near:
        flat += [item.outer, item.inner] if isinstance(item, Beside) else [item]
    total = len(flat)
    own = [pltpu.VMEM(p.shape, F32) for _, p in pairs_in + pairs_out for _ in range(2)]

    def body(*refs):
        refs_in, refs_out = list(refs[:count]), list(refs[total : total + len(shapes)])
        rest = list(refs[total + len(shapes) :])
        held, rest = rest[: len(own)], rest[len(own) :]
        sends = []
        for n, (i, pair) in enumerate(pairs_in + pairs_out):
            forward, backward = held[2 * n], held[2 * n + 1]
            is_in = n < len(pairs_in)
            refs_here = refs_in if is_in else refs_out
            outer, inner = refs_here[i], refs_here[i + 1]
            refs_here[i], refs_here[i + 1] = forward, backward
            if is_in:
                odd = lax.axis_index(pair.axis) & 1

                @pl.when(odd == 0)
                def _():
                    forward[...] = outer[...]
                    backward[...] = inner[...]

                @pl.when(odd == 1)
                def _():
                    forward[...] = inner[...]
                    backward[...] = outer[...]

            else:
                sends.append((pair.axis, outer, inner, forward, backward))
        kernel(*refs_in, *refs_out, *rest)
        for axis, outer, inner, forward, backward in sends:
            odd = lax.axis_index(axis) & 1

            @pl.when(odd == 0)
            def _():
                outer[...] = backward[...]
                inner[...] = forward[...]

            @pl.when(odd == 1)
            def _():
                outer[...] = forward[...]
                inner[...] = backward[...]

    results = pl.pallas_call(
        body,
        out_shape=[s if hasattr(s, "dtype") else jax.ShapeDtypeStruct(s, F32) for s in shapes],
        in_specs=[HBM if i in remote else VMEM for i in range(total)],
        out_specs=[VMEM] * len(shapes),
        scratch_shapes=own + [pltpu.VMEM(s, F32) if isinstance(s, tuple) else s for s in scratch],
        compiler_params=pltpu.CompilerParams(vmem_limit_bytes=limit),
    )(*flat)
    results, joined = list(results), []
    for item in out:
        if isinstance(item, Beside):
            joined.append(Beside(item.axis, item.shape, results.pop(0), results.pop(0)))
        else:
            joined.append(results.pop(0))
    return joined


def split3(x):
    high = x.astype(BF16)
    rest = x - high.astype(F32)
    middle = rest.astype(BF16)
    return high, middle, (rest - middle.astype(F32)).astype(BF16)


def dot(a, b):
    return jnp.dot(a, b, preferred_element_type=F32)


def dot_exact(x, table):
    high, middle, low = split3(x)
    return dot(high, table) + (dot(middle, table) + dot(low, table))


def pair_table(depth):
    table = np.zeros((depth, depth // 2), ml_dtypes.bfloat16)
    table[np.arange(depth), np.arange(depth) // 2] = 1
    return table


def put_tiles(tiles, x):
    for k in range(tiles.shape[0]):
        tiles[k, 0 : x.shape[0]] = x[:, 128 * k : 128 * k + 128]


def every_other(tiles, start, size):
    return jnp.concatenate(
        [tiles[k, pl.ds(start, size, stride=2), :] for k in range(tiles.shape[0])], axis=1
    )


def back(x, axis):
    return pltpu.roll(x, 1, axis)


def ahead(x, axis):
    return pltpu.roll(x, x.shape[axis] - 1, axis)


def parity2(shape):
    return (lax.broadcasted_iota(jnp.int32, shape, 0) + lax.broadcasted_iota(jnp.int32, shape, 1)) & 1


def row_sum(r, v, wx, wy, wz):
    centre = v[r]
    y, z = wy[r], wz[r]
    total = wx[r] * v[r + 1] + wx[r - 1] * v[r - 1]
    total = total + y * ahead(centre, 0) + back(y * centre, 0)
    return centre, total + z * ahead(centre, 1) + back(z * centre, 1)


def half_sweep(first, last, colour, parity, v, b, wx, wy, wz, rdiag):
    unroll = UNROLL if v.shape[-1] > 256 else last - first

    def body(r, carry):
        centre, total = row_sum(r, v, wx, wy, wz)
        mine = parity == ((r + colour) & 1)
        v[r] = jnp.where(mine, (b[r] + total) * rdiag[r], centre)
        return carry

    lax.fori_loop(first, last, body, 0, unroll=unroll)


def plane(src, face, a, r):
    return src[r] if a == 0 else face[a - 1, r].astype(F32)


def pack_y_kernel(src_in, face_in, to_right, to_left, src, face, sem):
    rows, cols, depth = src.shape
    copies = [pltpu.make_async_copy(src_in, src, sem.at[0]), pltpu.make_async_copy(face_in, face, sem.at[1])]
    for copy in copies:
        copy.start()
    for copy in copies:
        copy.wait()
    for out, base in ((to_right, cols - H), (to_left, 0)):
        for r in range(rows):
            for t, pair in enumerate(((0, 3), (1, 2))):
                for s, a in enumerate(pair):
                    value = plane(src, face, a, r)
                    if out is to_right and a == 3:
                        value_all = value + back(value, 1) + back(plane(src, face, 2, r), 0)
                        first = lax.broadcasted_iota(jnp.int32, value.shape, 0) == base
                        value = jnp.where(first, value_all, value)
                    out[2 * r + t, H * s : H * s + H] = value[base : base + H]


def pack_x_kernel(src, face, to_up, to_down):
    rows, cols, depth = src.shape
    tiles = cols // 8
    for out, base in ((to_up, rows - H), (to_down, 0)):
        for a in range(4):
            for k in range(H):
                value = plane(src, face, a, base + k)
                if out is to_up and a == 3 and k == 0:
                    value = value + back(value, 1) + plane(src, face, 1, base - 1)
                for t in range(tiles):
                    out[(a * H + k) * tiles + t] = value[8 * t : 8 * t + 8]


def coarsen_kernel(face, out, pairs, odds, tx):
    _, rows, cols, depth = face.shape
    fine = lax.broadcasted_iota(jnp.int32, pairs.shape, 0)
    coarse = 2 * lax.broadcasted_iota(jnp.int32, pairs.shape, 1)
    pairs[...] = jnp.where((fine & -2) == coarse, 1.0, 0.0).astype(BF16)
    odds[...] = jnp.where(fine == coarse + 1, 1.0, 0.0).astype(BF16)
    half, n = cols // 2, rows // 2

    def both(x):
        put_tiles(tx, x)
        return 0.0625 * (every_other(tx, 0, half) + every_other(tx, 1, half))

    for i in range(n):
        out[i] = both(dot(face[0, 2 * i + 1], pairs[...]))
        put_tiles(tx, dot(face[1, 2 * i], pairs[...]) + dot(face[1, 2 * i + 1], pairs[...]))
        out[n + i] = 0.0625 * every_other(tx, 1, half)
        out[2 * n + i] = both(dot(face[2, 2 * i], odds[...]) + dot(face[2, 2 * i + 1], odds[...]))


def forward_kernel(right, left, to_up, to_down, *, rows):
    tiles = to_up.shape[0] // 2
    place = {0: (0, 0), 3: (0, 1), 1: (1, 0), 2: (1, 1)}
    for msg, sy in ((right, 1), (left, -1)):
        start = 0 if sy > 0 else tiles
        for out, sx in ((to_up, 1), (to_down, -1)):
            for n, (a, dx, dy) in enumerate(CORNER0):
                r = rows - dx if sx > 0 else dx - 1
                t, s = place[a]
                s = H * s + (H - dy if sy > 0 else dy - 1)
                out[start + n // 8, n % 8 : n % 8 + 1] = msg[2 * r + t, s : s + 1]


def diagonal_row(r, parity, low_col, b, wx, wy, wz, diag, rdiag, v):
    y, z = wy[r], wz[r]
    if isinstance(r, int) and r == 0:
        total = MASS + wx[r] + z + y + back(y, 0)
    else:
        total = MASS + wx[r] + wx[r - 1] + y
        total = total + jnp.where(low_col, z, z + back(z, 1) + back(y, 0))
    diag[r] = total
    inverse = 1.0 / total
    rdiag[r] = inverse
    v[r] = jnp.where(parity == (r & 1), b[r] * inverse, 0.0)


def assemble_kernel(src, face, up, down, state):
    ext = [state.at[i] for i in range(4)]
    rows, cols, depth = src.shape
    for r in range(rows):
        ext[0][H + r, H : H + cols] = src[r]
        for d in range(3):
            ext[1 + d][H + r, H : H + cols] = face[d, r].astype(F32)
    tiles = cols // 8
    for msg, base in ((up, 0), (down, H + rows)):
        for a in range(4):
            for k in range(H):
                for t in range(tiles):
                    ext[a][base + k, H + 8 * t : H + 8 * t + 8] = msg[(a * H + k) * tiles + t]


def pre_kernel(up, down, right, left, pairs, state, kept, v_own, right1, to_right, to_left, *scratch):
    t512, t256, diag, v = scratch
    b, wx, wy, wz, rdiag = (kept.at[i] for i in range(5))
    kept[0:4] = state[...]
    ext = (b, wx, wy, wz)
    rows, cols, depth = v_own.shape
    er, ec = rows + 2 * H, cols + 2 * H
    rows1, cols1 = rows // 2, cols // 2
    for msg, base in ((right, 0), (left, H + cols)):
        for r in range(rows):
            for t, pair in enumerate(((0, 3), (1, 2))):
                for s, a in enumerate(pair):
                    ext[a][H + r, base : base + H] = msg[2 * r + t, H * s : H * s + H]
    tiles = len(CORNER0) // 8
    for msg, sx, sy in ((up, 1, 1), (up, 1, -1), (down, -1, 1), (down, -1, -1)):
        start = 0 if sy > 0 else tiles

        def at(distance, size, sign):
            return H - distance if sign > 0 else H + size + distance - 1

        for n, (a, dx, dy) in enumerate(CORNER0):
            r, c = at(dx, rows, sx), at(dy, cols, sy)
            ext[a][r, c : c + 1] = msg[start + n // 8, n % 8 : n % 8 + 1]
    parity = parity2((ec, depth))
    low_col = lax.broadcasted_iota(jnp.int32, (ec, depth), 0) == 0
    diagonal_row(0, parity, low_col, b, wx, wy, wz, diag, rdiag, v)

    def diagonal_body(r, carry):
        diagonal_row(r, parity, low_col, b, wx, wy, wz, diag, rdiag, v)
        return carry

    lax.fori_loop(1, er, diagonal_body, 0, unroll=UNROLL)
    half_sweep(1, er - 1, 1, parity, v, b, wx, wy, wz, rdiag)
    half_sweep(2, er - 2, 0, parity, v, b, wx, wy, wz, rdiag)
    half_sweep(3, er - 3, 1, parity, v, b, wx, wy, wz, rdiag)

    def residual_body(i, carry):
        total = 0.0
        for k in range(2):
            r = H + 2 * i + k
            centre, around = row_sum(r, v, wx, wy, wz)
            total = total + (b[r] - (diag[r] * centre - around))
        t512[i] = total
        return carry

    lax.fori_loop(0, rows1, residual_body, 0, unroll=UNROLL)
    put_tiles(t256, dot_exact(t512[...].reshape(rows1 * ec, depth), pairs[...]))
    for i in range(rows1):
        start = i * ec + H
        right1[i] = 0.125 * (every_other(t256, start, cols1) + every_other(t256, start + 1, cols1))

    start = to_right.shape[0] - rows1 // 2
    for i in range(rows1 // 2):
        to_right[start + i] = jnp.concatenate((right1[2 * i], right1[2 * i + 1]), axis=1)
        to_left[start + i] = to_right[start + i]

    own_parity = parity2((cols, depth))
    for r in range(rows):
        value = v[H + r, H : H + cols]
        v_own[r] = value
        value = jnp.where(own_parity == ((r + 1) & 1), value, ahead(value, 0))
        for p in range(H // 2):
            n = p * rows + r
            for out, base in ((to_right, cols - H), (to_left, 0)):
                out[n // 8, n % 8 : n % 8 + 1] = value[base + 2 * p : base + 2 * p + 1]


def pack_v_kernel(v0, right, left, v0_rows, to_up, to_down):
    rows, cols, depth = v0.shape
    for r in range(rows):
        v0_rows[r, H : H + cols] = v0[r]
        for msg, base in ((right, 0), (left, H + cols)):
            for p in range(H // 2):
                n = p * rows + r
                line = msg[n // 8, n % 8 : n % 8 + 1]
                v0_rows[r, base + 2 * p : base + 2 * p + 2] = jnp.broadcast_to(line, (2, depth))
    ec = v0_rows.shape[1]
    parity = parity2((ec, depth))
    for out, base in ((to_up, rows - H), (to_down, 0)):
        for k in range(H // 2):
            r = base + 2 * k
            out[k] = jnp.where(parity == ((r + 1) & 1), v0_rows[r], v0_rows[r + 1])


def before_kernel(x, up, down, pairs, out, tx):
    n, half, _ = x.shape
    tiles = 2 * half // 8
    start = (2 * H - 1) * tiles
    before = jnp.concatenate([up[start + t] for t in range(tiles)], axis=0)
    put_tiles(tx, dot(before.astype(BF16), pairs[...]))
    out[n] = 0.0625 * (every_other(tx, 0, half) + every_other(tx, 1, half))
    out[0:n] = x[...]


def couplings1_kernel(own, before_block, after_block, *refs):
    *between, w, rdiag, to_up, to_down, sums = refs
    blocks = [own, after_block, *between, before_block]
    planes, cols, depth = blocks[0].shape
    rows = planes // 3
    wide = cols * len(blocks)

    def plane(n):
        return jnp.concatenate([block[n] for block in blocks], axis=0)

    before = plane(3 * rows)
    for i in range(rows):
        x, y, z = plane(i), plane(rows + i), plane(2 * rows + i)
        w[0, i], w[1, i], w[2, i] = x, y, z
        rdiag[i] = 1.0 / (MASS + x + before + y + back(y, 0) + z + back(z, 1))
        before = x
    for d in range(3):
        for k in range(H - 1):
            to_up[d * (H - 1) + k] = w[d, rows - H + 1 + k]
            to_down[d * (H - 1) + k] = w[d, k]
    to_up[3 * (H - 1)] = w[0, rows - H]
    lane = lax.broadcasted_iota(jnp.int32, sums.shape, 1)
    row_odd = lax.broadcasted_iota(jnp.int32, (wide, depth), 0) & 1
    depth_odd = lax.broadcasted_iota(jnp.int32, (wide, depth), 1) & 1
    parts = [0.0, 0.0, 0.0]
    for i in range(rows):
        if i % 2 == 1:
            parts[0] = parts[0] + w[0, i]
        parts[1] = parts[1] + jnp.where(row_odd == 1, w[1, i], 0.0)
        parts[2] = parts[2] + jnp.where(depth_odd == 1, w[2, i], 0.0)
    line = jnp.zeros(sums.shape, F32)
    for d in range(3):
        line = jnp.where(lane == d, 0.0625 * jnp.sum(parts[d]), line)
    sums[...] = line


def pack1_kernel(right, left, own1, *refs):
    *between, rdiag, own, to_up, to_down = refs
    rows, cols, depth = own1.shape
    start = right.shape[0] - rows // 2
    for i in range(rows):
        lane = depth * (i % 2)
        parts = [own1[i], left[start + i // 2, :, lane : lane + depth]]
        parts += [block[i] for block in between]
        own[i] = jnp.concatenate(parts + [right[start + i // 2, :, lane : lane + depth]], axis=0)
    for k in range(H):
        value = own[rows - H + k]
        to_up[k] = value * rdiag[rows - H] if k == 0 else value
        value = own[k]
        to_down[k] = value * rdiag[k] if k == H - 1 else value


def pre1_kernel(own, up, down, w, w_up, w_down, v0_up, v0_down, kept, to_up, to_down):
    rows, wide, depth = own.shape
    er = rows + 2 * H
    wx, wy, wz, rdiag, b, v, diag = (kept.at[i] for i in range(7))
    b[0:H] = up[...]
    b[H : H + rows] = own[...]
    b[H + rows :] = down[...]
    for d in range(3):
        kept[d, H : H + rows] = w[d]
        kept[d, 1:H] = w_up[d * (H - 1) : (d + 1) * (H - 1)]
        kept[d, H + rows : er - 1] = w_down[d * (H - 1) : (d + 1) * (H - 1)]
    wx[0] = w_up[3 * (H - 1)]
    parity = parity2((wide, depth))
    for r in range(er):
        if 0 < r < er - 1:
            y, z = wy[r], wz[r]
            total = MASS + wx[r] + wx[r - 1] + y + back(y, 0) + z + back(z, 1)
            diag[r] = total
            inverse = 1.0 / total
            rdiag[r] = inverse
            first = b[r] * inverse
        else:
            first = b[r]
        v[r] = jnp.where(parity == (r & 1), first, 0.0)
    half_sweep(1, er - 1, 1, parity, v, b, wx, wy, wz, rdiag)
    half_sweep(2, er - 2, 0, parity, v, b, wx, wy, wz, rdiag)
    half_sweep(3, er - 3, 1, parity, v, b, wx, wy, wz, rdiag)
    for out, base, v0 in ((to_up, rows, v0_up), (to_down, H, v0_down)):
        n = 0
        pair_rows = range(base, base + H, 2)
        value = [jnp.where(parity == ((r + 1) & 1), v[r], v[r + 1]) for r in pair_rows]
        value = jnp.concatenate(value, axis=1)
        for t in range(wide // 8):
            out[n] = value[8 * t : 8 * t + 8]
            n += 1
        for k in range(H // 2):
            for t in range(v0.shape[1] // 8):
                out[n] = v0[k, 8 * t : 8 * t + 8]
                n += 1


def residual1_kernel(kept1, pairs, sums, chunks, t256, t128):
    wx, wy, wz, _, b, v, diag = (kept1.at[i] for i in range(7))
    _, er, wide, depth = kept1.shape
    rows = er - 2 * H
    chunk = chunks.at[0]
    for i in range(rows // 2):
        total = 0.0
        for k in range(2):
            r = H + 2 * i + k
            centre, around = row_sum(r, v, wx, wy, wz)
            total = total + (b[r] - (diag[r] * centre - around))
        t256[i] = total
    n = rows // 2
    put_tiles(t128, dot_exact(t256[...].reshape(n * wide, depth), pairs[...]))
    half = wide // 2
    for i in range(n):
        start = i * wide
        chunk[i * half : (i + 1) * half] = 0.125 * (every_other(t128, start, half) + every_other(t128, start + 1, half))
    chunk[n * half : n * half + 1] = sums[0:1]
    for i in range(1, chunks.shape[0]):
        chunks[i] = chunk[...]


def split2(x):
    high = x.astype(BF16)
    return high, (x - high.astype(F32)).astype(BF16)


def dot_split(a, b):
    return dot(a[0], b[0]) + (dot(a[0], b[1]) + dot(a[1], b[0]))


def solve_kernel(got, table, out, *, count, start):
    devices, lines, depth = got.shape
    own = lines - 1
    cells = devices * own
    rx, ry, _ = out.shape

    def part(name, size, lane=0, width=None):
        return table[start[name] : start[name] + size, lane : lane + (width or table.shape[1])]

    values = jnp.concatenate([got[d, 0:own] for d in range(devices)], axis=0)
    sums = got[0, own : own + 1]
    for d in range(1, devices):
        sums = sums + got[d, own : own + 1]
    sums = sums * (1.0 / count)
    lam = MASS + sums[0:1, 0:1] * part("eig", cells, 0, depth)
    lam = lam + sums[0:1, 1:2] * part("eig", cells, depth, depth)
    lam = lam + sums[0:1, 2:3] * part("depth", 1, depth, depth)
    spec = dot_split(split2(values), split2(part("depth", depth, 0, depth)))
    spec = dot_split(split2(part("forward", cells)), split2(spec))
    spec = spec / (lam * float(count))
    spec = dot_split(split2(spec), split2(part("depth_out", depth)))
    step = -(-rx // 16) * 8
    along_x = table[pl.ds(pl.multiple_of(start["x"] + lax.axis_index("gx") * step, 8), step), :]
    along_y = part("y", ry // 2)
    back_table = jnp.concatenate([along_x[i : i + 1] * along_y for i in range(rx // 2)], axis=0)
    rows = dot_split(split2(back_table), split2(spec)).reshape(rx // 2, ry // 2, out.shape[2])
    for i in range(rx // 2):
        line = jnp.broadcast_to(rows[i][:, None, :], (ry // 2, 2, out.shape[2])).reshape(out.shape[1:])
        out[2 * i] = line
        out[2 * i + 1] = line


def post1_kernel(kept1, up, down, correction, own, to_up, to_down, v, *, cols):
    wx, wy, wz, rdiag, b, before, _ = (kept1.at[i] for i in range(7))
    er, wide, depth = before.shape
    rows = er - 2 * H
    for r in range(rows):
        v[H + r] = before[H + r] + correction[H + r]
    for msg, base in ((up, 0), (down, H + rows)):
        value = jnp.concatenate([msg[t] for t in range(wide // 8)], axis=0)
        for k in range(H // 2):
            part = value[:, k * depth : (k + 1) * depth]
            v[base + 2 * k] = part + correction[base + 2 * k]
            v[base + 2 * k + 1] = part + correction[base + 2 * k + 1]
    parity = parity2((wide, depth))
    half_sweep(1, er - 1, 0, parity, v, b, wx, wy, wz, rdiag)
    half_sweep(2, er - 2, 1, parity, v, b, wx, wy, wz, rdiag)
    half_sweep(3, er - 3, 0, parity, v, b, wx, wy, wz, rdiag)
    half_sweep(4, er - 4, 1, parity, v, b, wx, wy, wz, rdiag)
    h = H // 2
    used = cols + 2 * h
    for r in range(rows):
        value = v[H + r]
        own[r, 0:h] = value[wide - h :]
        own[r, h:used] = value[0 : cols + h]
        if used < own.shape[1]:
            own[r, used:] = jnp.zeros((own.shape[1] - used, depth), F32)
    to_up[...] = own[rows - h :]
    to_down[...] = own[0:h]


def spread_rows(lines, spread, used):
    rows, padded, _ = lines.shape
    wide = dot_exact(lines.reshape(rows * padded, lines.shape[2]), spread)
    depth = wide.shape[1]
    wide = wide.reshape(rows, padded, depth)
    out = []
    for n in range(rows):
        line = jnp.broadcast_to(wide[n, 0:used][:, None, :], (used, 2, depth))
        out.append(line.reshape(2 * used, depth))
    return out


def post_sweep(n, rows, v, kept, parity):
    b, wx, wy, wz, rdiag = (kept.at[i] for i in range(5))
    for first, last in rows:
        half_sweep(first, last, n % 2, parity, v, b, wx, wy, wz, rdiag)


def inner_kernel(v0_rows, up, down, own, kept, spread, v):
    er, ec, depth = v.shape
    rows = er - 2 * H
    tiles = ec // 8
    for msg, base in ((up, 0), (down, H + rows)):
        start = msg.shape[0] - (H // 2) * tiles
        for k in range(H // 2):
            for t in range(tiles):
                tile = msg[start + k * tiles + t]
                v[base + 2 * k, 8 * t : 8 * t + 8] = tile
                v[base + 2 * k + 1, 8 * t : 8 * t + 8] = tile
    for n, line in enumerate(spread_rows(own[...], spread[...], ec // 2)):
        v[H + 2 * n] = v0_rows[2 * n] + line
        v[H + 2 * n + 1] = v0_rows[2 * n + 1] + line
    parity = parity2((ec, depth))
    for n in range(H - 1):
        if H + 1 + n < er - H - 1 - n:
            post_sweep(n, ((H + 1 + n, er - H - 1 - n),), v, kept, parity)


def post_kernel(v_in, up1, down1, kept, spread, out, v):
    rows, cols, depth = out.shape
    er, ec = rows + 2 * H, cols + 2 * H
    v[H : H + rows] = v_in[H : H + rows]
    for msg, base in ((up1, 0), (down1, H + rows)):
        for n, line in enumerate(spread_rows(msg[...], spread[...], ec // 2)):
            v[base + 2 * n] = v_in[base + 2 * n] + line
            v[base + 2 * n + 1] = v_in[base + 2 * n + 1] + line
    parity = parity2((ec, depth))
    for n in range(H):
        low, high = H + 1 + n, er - H - 1 - n
        if n < H - 1 and low < high:
            post_sweep(n, ((1 + n, low), (high, er - 1 - n)), v, kept, parity)
        else:
            post_sweep(n, ((1 + n, er - 1 - n),), v, kept, parity)
    for r in range(rows):
        out[r] = v[H + r, H : H + cols]


def hartley(rows, columns, length):
    angle = (np.outer(rows, columns) % length) * (2.0 * math.pi / length)
    return np.cos(angle) + np.sin(angle)


def waves(length):
    return 2.0 * (1.0 - np.cos(np.arange(length) * (2.0 * math.pi / length)))


def windows(table, count, step, size):
    pad = -size % 8
    parts = [np.pad(table[i * step : i * step + size], ((0, pad), (0, 0))) for i in range(count)]
    return np.concatenate(parts)


def coarse_correction(chunks, rows, cols, depth):
    nx = lax.axis_size("gx")
    total_rows = rows * nx
    count = total_rows * cols * depth
    got = lax.all_to_all(chunks, "gx", 0, 0)
    out_rows = 2 * rows + 2 * H
    rows_ids = (np.arange(-H, 2 * total_rows + H) // 2) % total_rows
    table_x = hartley(rows_ids, np.arange(total_rows), total_rows)
    table_y = hartley(np.arange(2 * cols) // 2, np.arange(cols), cols)
    forward_x = hartley(np.arange(total_rows), np.arange(total_rows), total_rows)
    forward_y = hartley(np.arange(cols), np.arange(cols), cols)
    depth_in = hartley(np.arange(depth), np.arange(depth), depth)
    depth_out = np.repeat(depth_in, 2, axis=1)
    cells = total_rows * cols
    if cells <= 512 and cells == 2 * depth:
        ones = np.ones((1, depth))
        eig_x = np.repeat(waves(total_rows), cols)[:, None] * ones
        eig_y = np.tile(waves(cols), total_rows)[:, None] * ones
        eig_z = np.ones((depth, 1)) * waves(depth)[None, :]
        parts = {
            "forward": np.kron(forward_x, forward_y),
            "eig": np.concatenate((eig_x, eig_y), axis=1),
            "depth": np.concatenate((depth_in, eig_z), axis=1),
            "depth_out": depth_out,
            "x": windows(np.repeat(table_x[::2], cols, axis=1), nx, rows, out_rows // 2),
            "y": np.tile(forward_y, (1, total_rows)),
        }
        start, size = {}, 0
        for name, part in parts.items():
            start[name] = size
            size += part.shape[0]
            assert size % 8 == 0
        table = jnp.asarray(np.concatenate(list(parts.values())), F32)
        return call(
            functools.partial(solve_kernel, count=count, start=start),
            [(out_rows, 2 * cols, 2 * depth)],
            got, table,
        )[0]

    hi = lax.Precision.HIGHEST
    f32 = lambda x: jnp.asarray(x, F32)
    averages = jnp.sum(got[:, rows * cols, :3], axis=0) / count
    full = got[:, : rows * cols].reshape(total_rows, cols, depth)
    spec = jnp.einsum("abz,zk->abk", full, f32(depth_in), precision=hi)
    spec = jnp.einsum("ij,jbz->ibz", f32(forward_x), spec, precision=hi)
    spec = jnp.einsum("ij,ajz->aiz", f32(forward_y), spec, precision=hi)
    lam = (
        MASS
        + averages[0] * f32(waves(total_rows))[:, None, None]
        + averages[1] * f32(waves(cols))[None, :, None]
        + averages[2] * f32(waves(depth))[None, None, :]
    )
    spec = spec / (lam * float(count))
    own_x = lax.dynamic_slice_in_dim(f32(table_x), lax.axis_index("gx") * 2 * rows, out_rows, 0)
    out = jnp.einsum("ij,jbz->ibz", own_x, spec, precision=hi)
    out = jnp.einsum("ij,ajz->aiz", f32(table_y), out, precision=hi)
    return jnp.einsum("abz,zk->abk", out, f32(depth_out), precision=hi)


def gathered(block):
    return [block] + [moved(block, 0, -k) for k in range(1, lax.axis_size("gy"))]


def shards(source, face_coef):
    rows, cols, depth = source.shape
    rows1, cols1, depth1 = rows // 2, cols // 2, depth // 2
    er, ec, er1 = rows + 2 * H, cols + 2 * H, rows1 + 2 * H
    wide = cols1 * lax.axis_size("gy")
    h = H // 2
    limit = VMEM_LIMIT if wide * depth1 <= 8192 else 5 * VMEM_LIMIT

    count = lax.axis_size("gy")
    corner_tiles = len(CORNER0) // 8
    y_first, source, face_coef = call(
        pack_y_kernel,
        [Beside("gy", (2 * rows, 8, depth)), (rows, cols, depth), jax.ShapeDtypeStruct((3, rows, cols, depth), BF16)],
        source, face_coef,
        remote=(0, 1),
        scratch=[pltpu.SemaphoreType.DMA((2,))],
    )
    y_first = y_first.exchanged()
    (x_first,) = call(pack_x_kernel, [Beside("gx", (4 * H * (cols // 8), 8, depth))], source, face_coef)
    x_first = x_first.exchanged()
    block, pairs = call(
        coarsen_kernel,
        [(3 * rows1, cols1, depth1), jax.ShapeDtypeStruct((depth, depth1), BF16)],
        face_coef,
        near=(x_first,),
        scratch=[pltpu.VMEM((depth, depth1), BF16), (depth1 // 128, cols + 8, 128)],
    )
    (block,) = call(
        before_kernel,
        [(3 * rows1 + 1, cols1, depth1)],
        block, x_first, pairs,
        scratch=[(depth1 // 128, cols + 8, 128)],
    )
    (state,) = call(assemble_kernel, [(4, er, ec, depth)], source, face_coef, x_first)
    (corners,) = call(
        functools.partial(forward_kernel, rows=rows),
        [Beside("gx", (2 * corner_tiles, 8, depth))],
        y_first,
        near=(block, state),
    )
    corners = corners.exchanged()
    blocks = Beside("gy", block.shape, block, block).exchanged()
    blocks_between = [moved(block, "gy", -k) for k in range(2, count - 1)]
    kept, v0, right1, y_second = call(
        pre_kernel,
        [(5, er, ec, depth), (rows, cols, depth), (rows1, cols1, depth1)]
        + [Beside("gy", (rows * h // 8 + rows1 // 2, 8, depth))],
        corners, y_first, pairs, state,
        scratch=[(rows1, ec, depth), (depth1 // 128, rows1 * ec + 8, 128)] + [(er, ec, depth)] * 2,
    )

    y_second = y_second.exchanged()
    between = [moved(right1, "gy", -k) for k in range(2, count - 1)]
    w_own, rdiag_own, w_x, sums = call(
        couplings1_kernel,
        [(3, rows1, wide, depth1), (rows1, wide, depth1), Beside("gx", (3 * H - 2, wide, depth1))]
        + [(8, depth1 // 2)],
        block, blocks, *blocks_between,
        near=(right1,), limit=limit,
    )
    w_x = w_x.exchanged()
    own, x_second = call(
        pack1_kernel,
        [(rows1, wide, depth1), Beside("gx", (H, wide, depth1))],
        y_second, right1, *between, rdiag_own,
        near=(kept,), limit=limit,
    )
    x_second = x_second.exchanged()
    v0_rows, v0_up, v0_down = call(pack_v_kernel, [(rows, ec, depth)] + [(h, ec, depth)] * 2, v0, y_second)
    tiles = wide // 8 + h * (ec // 8)
    kept1, x_third = call(
        pre1_kernel,
        [(7, er1, wide, depth1), Beside("gx", (tiles, 8, depth))],
        own, x_second, w_own, w_x, v0_up, v0_down,
        near=(kept,), limit=limit,
    )
    x_third = x_third.exchanged()
    (chunks,) = call(
        residual1_kernel,
        [(lax.axis_size("gx"), rows1 * wide // 4 + 1, depth1 // 2)],
        kept1, jnp.asarray(pair_table(depth1)), sums,
        scratch=[(rows1 // 2, wide, depth1), (depth1 // 256, rows1 // 2 * wide + 8, 128)],
        limit=limit,
    )
    correction2 = coarse_correction(chunks, rows1 // 2, wide // 2, depth1 // 2)
    used = -(-(cols1 + 2 * h) // 8) * 8
    own, x_fourth = call(
        functools.partial(post1_kernel, cols=cols1),
        [(rows1, used, depth1), Beside("gx", (h, used, depth1))],
        kept1, x_third, correction2,
        scratch=[(er1, wide, depth1)],
        limit=limit,
    )
    x_fourth = x_fourth.exchanged()
    spread = jnp.asarray(np.ascontiguousarray(pair_table(depth).T))
    (v,) = call(inner_kernel, [(er, ec, depth)], v0_rows, x_third, own, kept, spread)
    (out,) = call(post_kernel, [(rows, cols, depth)], v, x_fourth, kept, spread, scratch=[(er, ec, depth)])
    return out


def solution(mesh):
    return jax.shard_map(
        shards,
        mesh=mesh,
        in_specs=(P("gx", "gy", None), P(None, "gx", "gy", None)),
        out_specs=P("gx", "gy", None),
        check_vma=False,
    )
```
